32 devices in a mesh: blk: 32 (over z, y, x, core).
Axes of the slice: x: 2, y: 2, z: 4, core: 2. Of those that a mesh axis runs over, the one named last changes fastest.
Arguments:
- features: bfloat16 [12288, 512], P('blk'), may hold values from -6 to 6
- tile_list: int32 [32, 8, 7, 2], P('blk'), may hold values from 0 to 2, as said below
- tile_count: int32 [32, 8], P('blk'), may hold values from 1 to 7, as said below
- tile_values: bfloat16 [32, 8, 7, 128, 128], P('blk'), may hold values from -0.1875 to 0.1875
- weight: bfloat16 [512, 512], replicated, may hold values from -0.25 to 0.25
- bias: float32 [512], replicated, may hold values from -3 to 3
- grad_out: bfloat16 [12288, 512], P('blk'), may hold values from -6 to 6
Outputs:
- output: bfloat16 [12288, 512], P('blk')
- grad_features: bfloat16 [12288, 512], P('blk')
- grad_weight: float32 [512, 512], replicated
- grad_bias: float32 [512], replicated
The draws below stay inside these ranges and needn't reach their ends.
Inputs may be any that keep to these rules, and one draw needn't show every extreme that they name: `tile_list`: entries are tile indices within a row block; within one row block and neighbour the 7 (row tile, column tile) pairs are distinct. `tile_count`: loads differ from row block to row block; 7 is reached in every draw.
All inputs are finite; a program needn't handle non-finite values.
Results may differ from the reference program's by a relative error of at most 0.0075.
Values may be sent and summed in bfloat16 or wider, within the bound.
No kernel may reach another device: no remote copies, remote signals or barrier semaphores. Data moves between devices by JAX's collectives and lax.ppermute only.
A program may use at most 64 MiB of HBM per device.

```python
import jax
import jax.numpy as jnp
from jax import lax

HIDDEN_SIZE = 512
TILE = 128
SLOTS = 7
TILE_ROWS = 3
SHIFTS = 8
NODES = 12288
N_BLK = 32


def draw_tile_list(key, part):
    key = jax.random.fold_in(key, 11)
    many_keys = jax.random.split(key, N_BLK * SHIFTS)
    orders = jax.vmap(lambda one_key: jax.random.permutation(one_key, TILE_ROWS * TILE_ROWS))(many_keys)
    orders = orders[:, :SLOTS].astype(jnp.int32)
    tile_pairs = jnp.stack([orders // TILE_ROWS, orders % TILE_ROWS], axis=-1)
    return tile_pairs.reshape(N_BLK, SHIFTS, SLOTS, 2).astype(jnp.int32)


def draw_tile_count(key, part):
    key = jax.random.fold_in(key, 23)
    level_key, spread_key, forced_key = jax.random.split(key, 3)
    levels = jax.random.randint(level_key, (N_BLK, 1), SLOTS // 2, SLOTS + 1)
    spread = jax.random.randint(spread_key, (N_BLK, SHIFTS), 0, 65536)
    counts = spread % levels + 1
    forced = jax.random.randint(forced_key, (), 0, N_BLK * SHIFTS)
    counts = counts.reshape(-1).at[forced].set(SLOTS).reshape(N_BLK, SHIFTS)
    return counts.astype(jnp.int32)


def block_scale(stream_key, shape, shards, least, high):
    loudness, own = 1.0, jax.random.fold_in(stream_key, 6)
    for position, shards_of in shards:
        heights = jnp.exp(jax.random.uniform(jax.random.fold_in(own, position), (shards_of,), jnp.float32, least / len(shards), high / len(shards)))
        loudness = loudness * jnp.repeat(heights, shape[position] // shards_of).reshape([-1 if axis == position else 1 for axis in range(len(shape))])
    return loudness


def noise(rng, shape, scale, bound, cuts=(), kind=jnp.bfloat16):
    array = jax.random.normal(rng, shape, jnp.float32) * scale
    if len(cuts) > 0:
        array = block_scale(rng, shape, cuts, -0.22, 0.18) * array
    return jnp.clip(array, min=-bound, max=bound).astype(kind)


def setup_inputs(seed: int = 0) -> dict:
    streams_of = jax.random.split(jax.random.key(seed), 8)
    return {
        "features": noise(streams_of[0], (NODES, HIDDEN_SIZE), 1.0, 6.0, ((0, 32),)),
        "tile_list": draw_tile_list(jax.random.fold_in(streams_of[7], 71), 0),
        "tile_count": draw_tile_count(jax.random.fold_in(streams_of[7], 71), 0),
        "tile_values": noise(streams_of[3], (N_BLK, SHIFTS, SLOTS, TILE, TILE), (SHIFTS * SLOTS * TILE // (2 * TILE_ROWS)) ** -0.5, 0.1875, ((0, 32),)),
        "weight": noise(streams_of[4], (HIDDEN_SIZE, HIDDEN_SIZE), HIDDEN_SIZE ** -0.5, 0.25),
        "bias": noise(streams_of[5], (HIDDEN_SIZE,), 0.5, 3.0, (), jnp.float32),
        "grad_out": noise(streams_of[6], (NODES, HIDDEN_SIZE), 1.0, 6.0, ((0, 32),)),
    }


def tile_terms(values_now, take_index, put_index, count_now, blocks, flipped):
    picked = jnp.take(blocks, take_index, axis=0).astype(jnp.float32)
    tiles = values_now.astype(jnp.float32)
    if flipped:
        product = jnp.einsum("kba,kbh->kah", tiles, picked)
    else:
        product = jnp.einsum("kab,kbh->kah", tiles, picked)
    live = (jnp.arange(values_now.shape[0], dtype=jnp.int32) < count_now).astype(jnp.float32)
    select = (put_index[:, None] == jnp.arange(blocks.shape[0], dtype=jnp.int32)[None, :]).astype(jnp.float32)
    select = select * live[:, None]
    return jnp.einsum("kr,kah->rah", select, product, precision=lax.Precision.HIGHEST)


def reference(features, tile_list, tile_count, tile_values, weight, bias, grad_out):
    midway = SHIFTS // 2
    shaped = features.reshape(N_BLK, TILE_ROWS, TILE, HIDDEN_SIZE)
    blocks_all = jnp.arange(N_BLK, dtype=jnp.int32)

    def forward_block(block_id):
        def step(j, summed):
            j = jnp.asarray(j).astype(jnp.int32)
            source = jnp.mod(block_id + j - midway, N_BLK).astype(jnp.int32)
            return summed + tile_terms(tile_values[block_id, j], tile_list[block_id, j, :, 1],
                                       tile_list[block_id, j, :, 0], tile_count[block_id, j],
                                       shaped[source], False)
        start = jnp.zeros((TILE_ROWS, TILE, HIDDEN_SIZE), jnp.float32)
        return lax.fori_loop(0, SHIFTS, step, start)

    agg = lax.map(forward_block, blocks_all).reshape(NODES, HIDDEN_SIZE).astype(jnp.bfloat16)
    pre = jnp.dot(agg, weight, preferred_element_type=jnp.float32) + bias
    sig = jax.nn.sigmoid(pre)
    output = (pre * sig).astype(jnp.bfloat16)
    grad_pre = (grad_out.astype(jnp.float32) * sig * (1.0 + pre * (1.0 - sig))).astype(jnp.bfloat16)
    grad_weight = jnp.dot(agg.T, grad_pre, preferred_element_type=jnp.float32)
    grad_bias = jnp.sum(grad_pre.astype(jnp.float32), axis=0)
    grad_agg = jnp.dot(grad_pre, weight.T, preferred_element_type=jnp.float32).astype(jnp.bfloat16)
    gshaped = grad_agg.reshape(N_BLK, TILE_ROWS, TILE, HIDDEN_SIZE)

    def backward_block(owner):
        def step(j, summed):
            j = jnp.asarray(j).astype(jnp.int32)
            source = jnp.mod(owner - (j - midway), N_BLK).astype(jnp.int32)
            return summed + tile_terms(tile_values[source, j], tile_list[source, j, :, 0],
                                       tile_list[source, j, :, 1], tile_count[source, j],
                                       gshaped[source], True)
        start = jnp.zeros((TILE_ROWS, TILE, HIDDEN_SIZE), jnp.float32)
        return lax.fori_loop(0, SHIFTS, step, start)

    grad_features = lax.map(backward_block, blocks_all).reshape(NODES, HIDDEN_SIZE).astype(jnp.bfloat16)
    return (output, grad_features, grad_weight, grad_bias)
```

```python
import jax
import jax.numpy as jnp
from jax import lax
from jax.experimental import pallas as pl
from jax.experimental.pallas import tpu as pltpu
from jax.sharding import PartitionSpec as P

VMEM_LIMIT = 56 * 1024 * 1024
BF16, F32 = jnp.bfloat16, jnp.float32
BIAS_ROWS = 16


def call(kernel, outs, ins, flops=0, smem=0):
    spec = lambda k: pl.BlockSpec(memory_space=pltpu.SMEM if k < smem else pltpu.VMEM)
    out_shape = [jax.ShapeDtypeStruct(s, d) for s, d in outs]
    moved = sum(a.size * a.dtype.itemsize for a in list(ins) + out_shape)
    return pl.pallas_call(
        kernel,
        out_shape=out_shape,
        in_specs=[spec(k) for k in range(len(ins))],
        out_specs=[pl.BlockSpec(memory_space=pltpu.VMEM)] * len(outs),
        compiler_params=pltpu.CompilerParams(vmem_limit_bytes=VMEM_LIMIT),
        cost_estimate=pl.CostEstimate(flops=flops, bytes_accessed=moved, transcendentals=0),
    )(*ins)


def dense_tiles(core, own_meta, mate_meta, own_values, mate_values, rows_dev, positions):
    window, slots, tile, _ = own_values.shape
    tile_rows = rows_dev // tile

    def kernel(core_ref, own_meta_ref, mate_meta_ref, own_ref, mate_ref, dense_ref, flipped_ref):
        dense_ref[...] = jnp.zeros_like(dense_ref)
        flipped_ref[...] = jnp.zeros_like(flipped_ref)

        def place(meta_ref, values_ref, first_j, shift, first_row):
            def slot(t, _):
                i, k = t // slots, t % slots
                j = 2 * i + first_j
                base = j * (2 * slots + 1)

                @pl.when(k < meta_ref[base + 2 * slots])
                def _():
                    row = pl.multiple_of((meta_ref[base + 2 * k] + first_row) * tile, tile)
                    col = pl.multiple_of(((i + shift) * tile_rows + meta_ref[base + 2 * k + 1]) * tile, tile)
                    values = values_ref[j, k]
                    dense_ref[pl.ds(row, tile), pl.ds(col, tile)] = values
                    flipped_ref[pl.ds(col, tile), pl.ds(row, tile)] = values.T

                return 0

            lax.fori_loop(0, (window // 2) * slots, slot, 0)

        place(own_meta_ref, own_ref, 0, 0, 0)
        place(mate_meta_ref, mate_ref, 1, 1 - core_ref[0], tile_rows)

    wide = positions * rows_dev
    return call(
        kernel,
        [((2 * rows_dev, wide), BF16), ((wide, 2 * rows_dev), BF16)],
        [core, own_meta, mate_meta, own_values, mate_values],
        smem=3,
    )


def gathered_sums(dense, sources):
    rows_dev, hidden = sources[0].shape

    def kernel(dense_ref, *refs):
        source_refs, (own_ref, mate_ref) = refs[:-2], refs[-2:]
        total = jnp.zeros((2 * rows_dev, hidden), F32)
        for m, ref in enumerate(source_refs):
            part = dense_ref[:, m * rows_dev : (m + 1) * rows_dev]
            total = total + jnp.dot(part, ref[...], preferred_element_type=F32)
        own_ref[...] = total[:rows_dev]
        mate_ref[...] = total[rows_dev:]

    return call(
        kernel,
        [((rows_dev, hidden), F32), ((rows_dev, hidden), F32)],
        [dense, *sources],
        flops=4 * rows_dev * rows_dev * hidden * len(sources),
    )


def layer(own_sum, mate_sum, weight, bias, grad_out):
    rows_dev, hidden = own_sum.shape

    def kernel(own_ref, mate_ref, weight_ref, bias_ref, grad_out_ref, agg_ref, out_ref, gp_ref, ga_ref):
        agg = (own_ref[...] + mate_ref[...]).astype(BF16)
        agg_ref[...] = agg
        pre = jnp.dot(agg, weight_ref[...], preferred_element_type=F32) + bias_ref[...]
        sig = jax.nn.sigmoid(pre)
        out_ref[...] = (pre * sig).astype(BF16)
        grad_pre = (grad_out_ref[...].astype(F32) * sig * (1.0 + pre * (1.0 - sig))).astype(BF16)
        gp_ref[...] = grad_pre
        ga_ref[...] = lax.dot_general(
            grad_pre, weight_ref[...], (((1,), (1,)), ((), ())), preferred_element_type=F32
        ).astype(BF16)

    shape = (rows_dev, hidden)
    return call(
        kernel,
        [(shape, BF16)] * 4,
        [own_sum, mate_sum, weight, bias.reshape(1, hidden), grad_out],
        flops=4 * rows_dev * hidden * hidden,
    )


def weight_terms(core, agg, grad_pre, pieces):
    rows_dev, hidden = agg.shape
    piece = hidden // pieces
    half = (pieces // 2, piece + BIAS_ROWS, hidden)

    def kernel(core_ref, agg_ref, gp_ref, keep_ref, give_ref):
        grad_pre_now = gp_ref[...]
        bias_term = jnp.sum(grad_pre_now.astype(F32), axis=0, keepdims=True)
        bias_rows = jnp.broadcast_to(bias_term, (BIAS_ROWS, hidden))

        def term(side):
            cols = pl.ds(pl.multiple_of(side * (hidden // 2), hidden // 2), hidden // 2)
            return lax.dot_general(
                agg_ref[:, cols], grad_pre_now, (((0,), (0,)), ((), ())), preferred_element_type=F32
            )

        core_now = core_ref[0]
        for ref, value in ((keep_ref, term(core_now)), (give_ref, term(1 - core_now))):
            for q in range(pieces // 2):
                ref[q, :piece] = value[q * piece : (q + 1) * piece].astype(ref.dtype)
                ref[q, piece:] = bias_rows.astype(ref.dtype)

    return call(
        kernel, [(half, F32), (half, BF16)], [core, agg, grad_pre], flops=2 * rows_dev * hidden * hidden, smem=1
    )


def spread_halves(place, keep, got):
    count, rows, hidden = keep.shape

    def kernel(place_ref, keep_ref, got_ref, own_ref, *out_refs):
        for other in range(count):
            q = place_ref[0] ^ other
            value = keep_ref[q] + got_ref[q].astype(F32)
            if other == 0:
                own_ref[...] = value
            else:
                out_refs[other - 1][...] = value.astype(BF16)

    return call(
        kernel,
        [((rows, hidden), F32)] + [((rows, hidden), BF16)] * (count - 1),
        [place, keep, got],
        smem=1,
    )


def summed_terms(own, others):
    def kernel(own_ref, *refs):
        others_now, out_ref = refs[:-1], refs[-1]
        total = own_ref[...].astype(F32)
        for ref in others_now:
            total = total + ref[...].astype(F32)
        out_ref[...] = total.astype(BF16)

    return call(kernel, [(own.shape, BF16)], [own, *others])[0]


def tree_sum(values):
    values = [v.astype(F32) for v in values]
    while len(values) > 1:
        values = [values[k] + values[k + 1] for k in range(0, len(values), 2)]
    return values[0]


def summed_planes(values, piece):
    shape = values[0].shape

    def kernel(*refs):
        value_refs, (weight_ref, bias_ref) = refs[:-2], refs[-2:]
        total = tree_sum([ref[...] for ref in value_refs])
        weight_ref[...] = total[:piece].astype(BF16)
        bias_ref[...] = total[piece : piece + 8]

    return call(kernel, [((piece, shape[1]), BF16), ((8, shape[1]), F32)], list(values))


def joined(place, pieces):
    piece, hidden = pieces[0].shape
    count = len(pieces)

    def kernel(place_ref, *refs):
        piece_refs, out_ref = refs[:-1], refs[-1]
        for other, ref in enumerate(piece_refs):
            q = place_ref[0] ^ other
            out_ref[pl.ds(pl.multiple_of(q * piece, piece), piece)] = ref[...]

    return call(kernel, [((count * piece, hidden), BF16)], [place, *pieces], smem=1)[0]


def whole_weight(core, mine, other):
    rows, hidden = mine.shape

    def kernel(core_ref, mine_ref, other_ref, out_ref):
        core_now = core_ref[0]
        out_ref[pl.ds(pl.multiple_of(core_now * rows, rows), rows)] = mine_ref[...].astype(F32)
        out_ref[pl.ds(pl.multiple_of((1 - core_now) * rows, rows), rows)] = other_ref[...].astype(F32)

    return call(kernel, [((2 * rows, hidden), F32)], [core, mine, other], smem=1)[0]


def scattered_sums(flipped, own, mate):
    rows_dev, hidden = own.shape
    positions = flipped.shape[0] // rows_dev

    def kernel(flipped_ref, own_ref, mate_ref, *out_refs):
        for m, ref in enumerate(out_refs):
            part = pl.ds(m * rows_dev, rows_dev)
            total = jnp.dot(flipped_ref[part, :rows_dev], own_ref[...], preferred_element_type=F32)
            total += jnp.dot(flipped_ref[part, rows_dev:], mate_ref[...], preferred_element_type=F32)
            ref[...] = total.astype(ref.dtype)

    return call(
        kernel,
        [((rows_dev, hidden), F32 if m == positions // 2 else BF16) for m in range(positions)],
        [flipped, own, mate],
        flops=4 * rows_dev * rows_dev * hidden * positions,
    )


def local(features, tile_list, tile_count, tile_values, weight, bias, grad_out):
    count = lax.axis_size("blk")
    me = lax.axis_index("blk")
    window = tile_values.shape[1]
    reach = window // 4
    positions = 2 * reach + 1
    rows_dev, hidden = features.shape
    plane, plane_bits = 4, 2
    pieces = 2 * plane
    core = (me % 2).astype(jnp.int32).reshape(1)
    place = ((me // 2) % plane).astype(jnp.int32).reshape(1)

    def moved(value, chips, even_only=False):
        pairs = [(s, (s + 2 * chips) % count) for s in range(count) if not (even_only and s % 2)]
        return lax.ppermute(value, "blk", pairs)

    def swapped(value, distance):
        return lax.ppermute(value, "blk", [(s, s ^ distance) for s in range(count)])

    sources = [
        features if m == reach else moved(features, reach - m, m == positions - 1) for m in range(positions)
    ]
    meta = jnp.concatenate([tile_list[0].reshape(window, -1), tile_count[0][:, None]], axis=1).reshape(-1)
    mate_meta, mate_values = swapped(meta, 1), swapped(tile_values[0], 1)
    dense, flipped = dense_tiles(core, meta, mate_meta, tile_values[0], mate_values, rows_dev, positions)
    own_sum, mate_sum = gathered_sums(dense, sources)
    agg, output, grad_pre, grad_agg = layer(own_sum, swapped(mate_sum, 1), weight, bias, grad_out)
    mate_grad = swapped(grad_agg, 1)

    keep, give = weight_terms(core, agg, grad_pre, pieces)
    terms = scattered_sums(flipped, grad_agg, mate_grad)
    arrived = [
        moved(terms[m], m - reach, m == positions - 1) for m in range(positions) if m != reach
    ]

    own_piece, *give_pieces = spread_halves(place, keep, swapped(give, 1))
    plane_sum = summed_terms(own_piece, [swapped(v, 2 * (d + 1)) for d, v in enumerate(give_pieces)])
    group = count // pieces
    values = [plane_sum] + [swapped(plane_sum, pieces * d) for d in range(1, group)]
    piece_sum, bias_sum = summed_planes(values, hidden // pieces)
    half = joined(place, [piece_sum] + [swapped(piece_sum, 2 * d) for d in range(1, plane)])
    grad_weight = whole_weight(core, half, swapped(half, 1))
    grad_features = summed_terms(terms[reach], arrived)
    return (output, grad_features, grad_weight, bias_sum[0])


def solution(mesh):
    placed = (
        P("blk", None),
        P("blk", None, None, None),
        P("blk", None),
        P("blk", None, None, None, None),
        P(),
        P(),
        P("blk", None),
    )
    return jax.shard_map(
        local,
        mesh=mesh,
        in_specs=placed,
        out_specs=(P("blk", None), P("blk", None), P(), P()),
        check_vma=False,
    )
```

```python
import jax
import jax.numpy as jnp
from jax import lax
from jax.experimental import pallas as pl
from jax.experimental.pallas import tpu as pltpu
from jax.sharding import PartitionSpec as P

BF16, F32 = jnp.bfloat16, jnp.float32
BIAS_ROWS = 16


def call(kernel, outs, ins, flops=0, smem=0):
    spec = lambda k: pl.BlockSpec(memory_space=pltpu.SMEM if k < smem else pltpu.VMEM)
    out_shape = [jax.ShapeDtypeStruct(s, d) for s, d in outs]
    moved = sum(a.size * a.dtype.itemsize for a in list(ins) + out_shape)
    return pl.pallas_call(
        kernel,
        out_shape=out_shape,
        in_specs=[spec(k) for k in range(len(ins))],
        out_specs=[pl.BlockSpec(memory_space=pltpu.VMEM)] * len(outs),
        compiler_params=pltpu.CompilerParams(vmem_limit_bytes=moved + moved // 4 + 4 * 1024 * 1024),
        cost_estimate=pl.CostEstimate(flops=flops, bytes_accessed=moved, transcendentals=0),
    )(*ins)


def dense_tiles(core, own_meta, mate_meta, own_values, mate_values, rows_dev, positions):
    window, slots, tile, _ = own_values.shape
    tile_rows = rows_dev // tile

    def kernel(core_ref, own_meta_ref, mate_meta_ref, own_ref, mate_ref, dense_ref, flipped_ref):
        dense_ref[...] = jnp.zeros_like(dense_ref)
        flipped_ref[...] = jnp.zeros_like(flipped_ref)

        def place(meta_ref, values_ref, first_j, shift, first_row):
            def slot(t, _):
                i, k = t // slots, t % slots
                j = 2 * i + first_j
                base = j * (2 * slots + 1)

                @pl.when(k < meta_ref[base + 2 * slots])
                def _():
                    row = pl.multiple_of((meta_ref[base + 2 * k] + first_row) * tile, tile)
                    col = pl.multiple_of(((i + shift) * tile_rows + meta_ref[base + 2 * k + 1]) * tile, tile)
                    values = values_ref[j, k]
                    dense_ref[pl.ds(row, tile), pl.ds(col, tile)] = values
                    flipped_ref[pl.ds(col, tile), pl.ds(row, tile)] = values.T

                return 0

            lax.fori_loop(0, (window // 2) * slots, slot, 0)

        place(own_meta_ref, own_ref, 0, 0, 0)
        place(mate_meta_ref, mate_ref, 1, 1 - core_ref[0], tile_rows)

    wide = positions * rows_dev
    return call(
        kernel,
        [((2 * rows_dev, wide), BF16), ((wide, 2 * rows_dev), BF16)],
        [core, own_meta, mate_meta, own_values, mate_values],
        smem=3,
    )


def gathered_sums(dense, sources, side):
    rows_dev, hidden = sources[0].shape

    def kernel(dense_ref, *refs):
        source_refs, out_ref = refs[:-1], refs[-1]
        total = jnp.zeros((rows_dev, hidden), F32)
        for m, ref in enumerate(source_refs):
            part = dense_ref[side * rows_dev : (side + 1) * rows_dev, m * rows_dev : (m + 1) * rows_dev]
            total = total + jnp.dot(part, ref[...], preferred_element_type=F32)
        out_ref[...] = total

    return call(
        kernel,
        [((rows_dev, hidden), F32)],
        [dense, *sources],
        flops=2 * rows_dev * rows_dev * hidden * len(sources),
    )[0]


def layer(own_sum, mate_sum, weight, bias, grad_out):
    rows_dev, hidden = own_sum.shape

    def kernel(own_ref, mate_ref, weight_ref, bias_ref, grad_out_ref, agg_ref, out_ref, gp_ref, ga_ref):
        agg = (own_ref[...] + mate_ref[...]).astype(BF16)
        agg_ref[...] = agg
        pre = jnp.dot(agg, weight_ref[...], preferred_element_type=F32) + bias_ref[...]
        sig = jax.nn.sigmoid(pre)
        out_ref[...] = (pre * sig).astype(BF16)
        grad_pre = (grad_out_ref[...].astype(F32) * sig * (1.0 + pre * (1.0 - sig))).astype(BF16)
        gp_ref[...] = grad_pre
        ga_ref[...] = lax.dot_general(
            grad_pre, weight_ref[...], (((1,), (1,)), ((), ())), preferred_element_type=F32
        ).astype(BF16)

    shape = (rows_dev, hidden)
    return call(
        kernel,
        [(shape, BF16)] * 4,
        [own_sum, mate_sum, weight, bias.reshape(1, hidden), grad_out],
        flops=4 * rows_dev * hidden * hidden,
    )


def weight_terms(core, agg, grad_pre, pieces):
    rows_dev, hidden = agg.shape
    piece = hidden // pieces
    half = (pieces // 2, piece + BIAS_ROWS, hidden)

    def kernel(core_ref, agg_ref, gp_ref, keep_ref, give_ref):
        grad_pre_now = gp_ref[...]
        bias_term = jnp.sum(grad_pre_now.astype(F32), axis=0, keepdims=True)
        bias_rows = jnp.broadcast_to(bias_term, (BIAS_ROWS, hidden))

        def term(side):
            cols = pl.ds(pl.multiple_of(side * (hidden // 2), hidden // 2), hidden // 2)
            return lax.dot_general(
                agg_ref[:, cols], grad_pre_now, (((0,), (0,)), ((), ())), preferred_element_type=F32
            )

        core_now = core_ref[0]
        for ref, value in ((keep_ref, term(core_now)), (give_ref, term(1 - core_now))):
            for q in range(pieces // 2):
                ref[q, :piece] = value[q * piece : (q + 1) * piece].astype(ref.dtype)
                ref[q, piece:] = bias_rows.astype(ref.dtype)

    return call(
        kernel, [(half, F32), (half, BF16)], [core, agg, grad_pre], flops=2 * rows_dev * hidden * hidden, smem=1
    )


def spread_halves(place, keep, got):
    count, rows, hidden = keep.shape

    def kernel(place_ref, keep_ref, got_ref, own_ref, *out_refs):
        for other in range(count):
            q = place_ref[0] ^ other
            value = keep_ref[q] + got_ref[q].astype(F32)
            if other == 0:
                own_ref[...] = value
            else:
                out_refs[other - 1][...] = value.astype(BF16)

    return call(
        kernel,
        [((rows, hidden), F32)] + [((rows, hidden), BF16)] * (count - 1),
        [place, keep, got],
        smem=1,
    )


def summed_terms(own, others):
    def kernel(own_ref, *refs):
        others_now, out_ref = refs[:-1], refs[-1]
        total = own_ref[...].astype(F32)
        for ref in others_now:
            total = total + ref[...].astype(F32)
        out_ref[...] = total.astype(BF16)

    return call(kernel, [(own.shape, BF16)], [own, *others])[0]


def tree_sum(values):
    values = [v.astype(F32) for v in values]
    while len(values) > 1:
        values = [values[k] + values[k + 1] for k in range(0, len(values), 2)]
    return values[0]


def summed_planes(values, piece):
    shape = values[0].shape

    def kernel(*refs):
        value_refs, (weight_ref, bias_ref) = refs[:-2], refs[-2:]
        total = tree_sum([ref[...] for ref in value_refs])
        weight_ref[...] = total[:piece].astype(BF16)
        bias_ref[...] = total[piece : piece + 8]

    return call(kernel, [((piece, shape[1]), BF16), ((8, shape[1]), F32)], list(values))


def joined(place, pieces):
    piece, hidden = pieces[0].shape
    count = len(pieces)

    def kernel(place_ref, *refs):
        piece_refs, out_ref = refs[:-1], refs[-1]
        for other, ref in enumerate(piece_refs):
            q = place_ref[0] ^ other
            out_ref[pl.ds(pl.multiple_of(q * piece, piece), piece)] = ref[...]

    return call(kernel, [((count * piece, hidden), BF16)], [place, *pieces], smem=1)[0]


def whole_weight(core, mine, other):
    rows, hidden = mine.shape

    def kernel(core_ref, mine_ref, other_ref, out_ref):
        core_now = core_ref[0]
        out_ref[pl.ds(pl.multiple_of(core_now * rows, rows), rows)] = mine_ref[...].astype(F32)
        out_ref[pl.ds(pl.multiple_of((1 - core_now) * rows, rows), rows)] = other_ref[...].astype(F32)

    return call(kernel, [((2 * rows, hidden), F32)], [core, mine, other], smem=1)[0]


def scattered_sums(flipped, own, mate):
    rows_dev, hidden = own.shape
    positions = flipped.shape[0] // rows_dev

    def kernel(flipped_ref, own_ref, mate_ref, *out_refs):
        for m, ref in enumerate(out_refs):
            part = pl.ds(m * rows_dev, rows_dev)
            total = jnp.dot(flipped_ref[part, :rows_dev], own_ref[...], preferred_element_type=F32)
            total += jnp.dot(flipped_ref[part, rows_dev:], mate_ref[...], preferred_element_type=F32)
            ref[...] = total.astype(ref.dtype)

    return call(
        kernel,
        [((rows_dev, hidden), F32 if m == positions // 2 else BF16) for m in range(positions)],
        [flipped, own, mate],
        flops=4 * rows_dev * rows_dev * hidden * positions,
    )


def local(features, tile_list, tile_count, tile_values, weight, bias, grad_out):
    count = lax.axis_size("blk")
    me = lax.axis_index("blk")
    window = tile_values.shape[1]
    reach = window // 4
    positions = 2 * reach + 1
    rows_dev, hidden = features.shape
    plane, plane_bits = 4, 2
    pieces = 2 * plane
    core = (me % 2).astype(jnp.int32).reshape(1)
    place = ((me // 2) % plane).astype(jnp.int32).reshape(1)

    def moved(value, chips, even_only=False):
        pairs = [(s, (s + 2 * chips) % count) for s in range(count) if not (even_only and s % 2)]
        return lax.ppermute(value, "blk", pairs)

    def swapped(value, distance):
        return lax.ppermute(value, "blk", [(s, s ^ distance) for s in range(count)])

    sources = [
        features if m == reach else moved(features, reach - m, m == positions - 1) for m in range(positions)
    ]
    meta = jnp.concatenate([tile_list[0].reshape(window, -1), tile_count[0][:, None]], axis=1).reshape(-1)
    mate_meta, mate_values = swapped(meta, 1), swapped(tile_values[0], 1)
    dense, flipped = dense_tiles(core, meta, mate_meta, tile_values[0], mate_values, rows_dev, positions)
    mate_sum = swapped(gathered_sums(dense, sources, 1), 1)
    own_sum = gathered_sums(dense, sources, 0)
    agg, output, grad_pre, grad_agg = layer(own_sum, mate_sum, weight, bias, grad_out)
    mate_grad = swapped(grad_agg, 1)

    keep, give = weight_terms(core, agg, grad_pre, pieces)
    terms = scattered_sums(flipped, grad_agg, mate_grad)
    arrived = [
        moved(terms[m], m - reach, m == positions - 1) for m in range(positions) if m != reach
    ]

    got, *terms = lax.optimization_barrier((swapped(give, 1), *terms))
    own_piece, *give_pieces = spread_halves(place, keep, got)
    plane_sum = summed_terms(own_piece, [swapped(v, 2 * (d + 1)) for d, v in enumerate(give_pieces)])
    group = count // pieces
    values = [plane_sum] + [swapped(plane_sum, pieces * d) for d in range(1, group)]
    piece_sum, bias_sum = summed_planes(values, hidden // pieces)
    half = joined(place, [piece_sum] + [swapped(piece_sum, 2 * d) for d in range(1, plane)])
    grad_weight = whole_weight(core, half, swapped(half, 1))
    grad_features = summed_terms(terms[reach], arrived)
    return (output, grad_features, grad_weight, bias_sum[0])


def solution(mesh):
    placed = (
        P("blk", None),
        P("blk", None, None, None),
        P("blk", None),
        P("blk", None, None, None, None),
        P(),
        P(),
        P("blk", None),
    )
    return jax.shard_map(
        local,
        mesh=mesh,
        in_specs=placed,
        out_specs=(P("blk", None), P("blk", None), P(), P()),
        check_vma=False,
    )
```

```python
import jax
import jax.numpy as jnp
from jax import lax
from jax.experimental import pallas as pl
from jax.experimental.pallas import tpu as pltpu
from jax.sharding import PartitionSpec as P

BF16, F32 = jnp.bfloat16, jnp.float32
BIAS_ROWS = 16


def call(kernel, outs, ins, flops=0, smem=0):
    spec = lambda k: pl.BlockSpec(memory_space=pltpu.SMEM if k < smem else pltpu.VMEM)
    out_shape = [jax.ShapeDtypeStruct(s, d) for s, d in outs]
    moved = sum(a.size * a.dtype.itemsize for a in list(ins) + out_shape)
    return pl.pallas_call(
        kernel,
        out_shape=out_shape,
        in_specs=[spec(k) for k in range(len(ins))],
        out_specs=[pl.BlockSpec(memory_space=pltpu.VMEM)] * len(outs),
        compiler_params=pltpu.CompilerParams(vmem_limit_bytes=moved + moved // 4 + 4 * 1024 * 1024),
        cost_estimate=pl.CostEstimate(flops=flops, bytes_accessed=moved, transcendentals=0),
    )(*ins)


def dense_tiles(spot, own_meta, mate_meta, own_values, mate_values, rows_dev, table):
    window, slots, tile, _ = own_values.shape
    tile_rows = rows_dev // tile
    positions = len(table[0])

    def kernel(spot_ref, table_ref, own_meta_ref, mate_meta_ref, own_ref, mate_ref, dense_ref, flipped_ref):
        spot_now = spot_ref[0]
        dense_ref[...] = jnp.zeros_like(dense_ref)
        flipped_ref[...] = jnp.zeros_like(flipped_ref)

        def place(meta_ref, values_ref, first_j, shift, first_row):
            def slot(t, _):
                i, k = t // slots, t % slots
                j = 2 * i + first_j
                base = j * (2 * slots + 1)

                @pl.when(k < meta_ref[base + 2 * slots])
                def _():
                    row = pl.multiple_of((meta_ref[base + 2 * k] + first_row) * tile, tile)
                    column = table_ref[spot_now * positions + i + shift]
                    col = pl.multiple_of((column * tile_rows + meta_ref[base + 2 * k + 1]) * tile, tile)
                    values = values_ref[j, k]
                    dense_ref[pl.ds(row, tile), pl.ds(col, tile)] = values
                    flipped_ref[pl.ds(col, tile), pl.ds(row, tile)] = values.T

                return 0

            lax.fori_loop(0, (window // 2) * slots, slot, 0)

        place(own_meta_ref, own_ref, 0, 0, 0)
        place(mate_meta_ref, mate_ref, 1, 1 - spot_now % 2, tile_rows)

    wide = positions * rows_dev
    return call(
        kernel,
        [((2 * rows_dev, wide), BF16), ((wide, 2 * rows_dev), BF16)],
        [spot, jnp.asarray(table, jnp.int32).reshape(-1), own_meta, mate_meta, own_values, mate_values],
        smem=4,
    )


def holds(mask, spot):
    return (mask >> spot) % 2 == 1


def gathered_sums(spot, dense, columns, rows, sources, start=None):
    hidden = first_of(sources[0]).shape[1]
    rows_dev = first_of(sources[0]).shape[0]
    first, last = rows

    def kernel(spot_ref, dense_ref, *refs):
        refs, out_ref = list(refs[:-1]), refs[-1]
        total = refs.pop(0)[first:last] if start is not None else jnp.zeros((last - first, hidden), F32)
        for column, source in zip(columns, sources):
            if isinstance(source, tuple):
                a, b = refs.pop(0)[...], refs.pop(0)[...]
                value = jnp.where(holds(source[0], spot_ref[0]), a, b)
            else:
                value = refs.pop(0)[...]
            part = dense_ref[first:last, column * rows_dev : (column + 1) * rows_dev]
            total = total + jnp.dot(part, value, preferred_element_type=F32)
        out_ref[...] = total

    arrays = [a for source in sources for a in (source[1:] if isinstance(source, tuple) else (source,))]
    return call(
        kernel,
        [((last - first, hidden), F32)],
        [spot, dense, *([] if start is None else [start]), *arrays],
        flops=2 * (last - first) * rows_dev * hidden * len(sources),
        smem=1,
    )[0]


def first_of(source):
    return source[1] if isinstance(source, tuple) else source


def layer(own_sum, mate_sum, weight, bias, grad_out):
    rows_dev, hidden = own_sum.shape

    def kernel(own_ref, mate_ref, weight_ref, bias_ref, grad_out_ref, agg_ref, out_ref, gp_ref, ga_ref):
        agg = (own_ref[...] + mate_ref[...]).astype(BF16)
        agg_ref[...] = agg
        pre = jnp.dot(agg, weight_ref[...], preferred_element_type=F32) + bias_ref[...]
        sig = jax.nn.sigmoid(pre)
        out_ref[...] = (pre * sig).astype(BF16)
        grad_pre = (grad_out_ref[...].astype(F32) * sig * (1.0 + pre * (1.0 - sig))).astype(BF16)
        gp_ref[...] = grad_pre
        ga_ref[...] = lax.dot_general(
            grad_pre, weight_ref[...], (((1,), (1,)), ((), ())), preferred_element_type=F32
        ).astype(BF16)

    shape = (rows_dev, hidden)
    return call(
        kernel,
        [(shape, BF16)] * 4,
        [own_sum, mate_sum, weight, bias.reshape(1, hidden), grad_out],
        flops=4 * rows_dev * hidden * hidden,
    )


def weight_terms(core, agg, grad_pre, pieces):
    rows_dev, hidden = agg.shape
    piece = hidden // pieces
    half = (pieces // 2, piece + BIAS_ROWS, hidden)

    def kernel(core_ref, agg_ref, gp_ref, keep_ref, give_ref):
        grad_pre_now = gp_ref[...]
        bias_term = jnp.sum(grad_pre_now.astype(F32), axis=0, keepdims=True)
        bias_rows = jnp.broadcast_to(bias_term, (BIAS_ROWS, hidden))

        def term(side):
            cols = pl.ds(pl.multiple_of(side * (hidden // 2), hidden // 2), hidden // 2)
            return lax.dot_general(
                agg_ref[:, cols], grad_pre_now, (((0,), (0,)), ((), ())), preferred_element_type=F32
            )

        core_now = core_ref[0]
        for ref, value in ((keep_ref, term(core_now)), (give_ref, term(1 - core_now))):
            for q in range(pieces // 2):
                ref[q, :piece] = value[q * piece : (q + 1) * piece].astype(ref.dtype)
                ref[q, piece:] = bias_rows.astype(ref.dtype)

    return call(
        kernel, [(half, F32), (half, BF16)], [core, agg, grad_pre], flops=2 * rows_dev * hidden * hidden, smem=1
    )


def spread_halves(place, keep, got):
    count, rows, hidden = keep.shape

    def kernel(place_ref, keep_ref, got_ref, own_ref, *out_refs):
        for other in range(count):
            q = place_ref[0] ^ other
            value = keep_ref[q] + got_ref[q].astype(F32)
            if other == 0:
                own_ref[...] = value
            else:
                out_refs[other - 1][...] = value.astype(BF16)

    return call(
        kernel,
        [((rows, hidden), F32)] + [((rows, hidden), BF16)] * (count - 1),
        [place, keep, got],
        smem=1,
    )


def summed_terms(spot, terms, masks=None, dtype=BF16):
    masks = masks or [None] * len(terms)

    def kernel(spot_ref, *refs):
        out_ref = refs[-1]
        total = None
        for ref, mask in zip(refs[:-1], masks):
            value = ref[...].astype(F32)
            if mask is not None:
                value = jnp.where(holds(mask, spot_ref[0]), value, 0.0)
            total = value if total is None else total + value
        out_ref[...] = total.astype(dtype)

    return call(kernel, [(terms[0].shape, dtype)], [spot, *terms], smem=1)[0]


def tree_sum(values):
    values = [v.astype(F32) for v in values]
    while len(values) > 1:
        values = [values[k] + values[k + 1] for k in range(0, len(values), 2)]
    return values[0]


def summed_planes(values, piece):
    shape = values[0].shape

    def kernel(*refs):
        value_refs, (weight_ref, bias_ref) = refs[:-2], refs[-2:]
        total = tree_sum([ref[...] for ref in value_refs])
        weight_ref[...] = total[:piece].astype(BF16)
        bias_ref[...] = total[piece : piece + 8]

    return call(kernel, [((piece, shape[1]), BF16), ((8, shape[1]), F32)], list(values))


def joined(place, pieces):
    piece, hidden = pieces[0].shape
    count = len(pieces)

    def kernel(place_ref, *refs):
        piece_refs, out_ref = refs[:-1], refs[-1]
        for other, ref in enumerate(piece_refs):
            q = place_ref[0] ^ other
            out_ref[pl.ds(pl.multiple_of(q * piece, piece), piece)] = ref[...]

    return call(kernel, [((count * piece, hidden), BF16)], [place, *pieces], smem=1)[0]


def whole_weight(core, mine, other):
    rows, hidden = mine.shape

    def kernel(core_ref, mine_ref, other_ref, out_ref):
        core_now = core_ref[0]
        out_ref[pl.ds(pl.multiple_of(core_now * rows, rows), rows)] = mine_ref[...].astype(F32)
        out_ref[pl.ds(pl.multiple_of((1 - core_now) * rows, rows), rows)] = other_ref[...].astype(F32)

    return call(kernel, [((2 * rows, hidden), F32)], [core, mine, other], smem=1)[0]


def scattered_sums(flipped, own, mate, columns, dtypes):
    rows_dev, hidden = own.shape

    def kernel(flipped_ref, own_ref, mate_ref, *out_refs):
        out_refs = list(out_refs)
        for column, kinds in zip(columns, dtypes):
            part = pl.ds(column * rows_dev, rows_dev)
            total = jnp.dot(flipped_ref[part, :rows_dev], own_ref[...], preferred_element_type=F32)
            total += jnp.dot(flipped_ref[part, rows_dev:], mate_ref[...], preferred_element_type=F32)
            for kind in kinds:
                out_refs.pop(0)[...] = total.astype(kind)

    return call(
        kernel,
        [((rows_dev, hidden), kind) for kinds in dtypes for kind in kinds],
        [flipped, own, mate],
        flops=4 * rows_dev * rows_dev * hidden * len(columns),
    )


class Direct:
    def __init__(self, count, reach):
        self.count, self.reach, self.positions = count, reach, 2 * reach + 1
        self.table = [list(range(self.positions))] * 8

    def moved(self, value, chips, even_only=False):
        pairs = [(s, (s + 2 * chips) % self.count) for s in range(self.count) if not (even_only and s % 2)]
        return lax.ppermute(value, "blk", pairs)

    def gather(self, features):
        last = self.positions - 1
        self.sources = [
            features if m == self.reach else self.moved(features, self.reach - m, m == last)
            for m in range(self.positions)
        ]
        return self.sources[0]

    def sums(self, spot, dense, rows_dev):
        columns = range(self.positions)
        return [
            gathered_sums(spot, dense, columns, (side * rows_dev, (side + 1) * rows_dev), self.sources)
            for side in (1, 0)
        ]

    def scatter(self, spot, flipped, own, mate):
        kinds = [[F32 if m == self.reach else BF16] for m in range(self.positions)]
        terms = scattered_sums(flipped, own, mate, range(self.positions), kinds)
        last = self.positions - 1
        arrived = [
            self.moved(terms[m], m - self.reach, m == last) for m in range(self.positions) if m != self.reach
        ]
        return terms[0], lambda: summed_terms(spot, [terms[self.reach], *arrived])


class Relayed:
    EVEN, MIDDLE, ENDS = 0b01010101, 0b00111100, 0b11000011

    def __init__(self, count):
        self.count, self.positions = count, 5
        self.table = [
            [3, 4, 0, 2, 1], [3, 4, 0, 1, 2],
            [3, 2, 0, 4, 1], [3, 1, 0, 4, 2],
            [1, 4, 0, 2, 3], [2, 4, 0, 1, 3],
            [1, 2, 0, 4, 3], [2, 1, 0, 4, 3],
        ]

    def sent(self, value, steps, back=False):
        pairs = [(s, steps[s % 8](s) % self.count) for s in range(self.count) if s % 8 in steps]
        return lax.ppermute(value, "blk", [(b, a) if back else (a, b) for a, b in pairs])

    x, y = staticmethod(lambda s: s ^ 2), staticmethod(lambda s: s ^ 4)
    up, down = staticmethod(lambda s: s + 8), staticmethod(lambda s: s - 8)

    def routes(self):
        x, y, up, down = self.x, self.y, self.up, self.down
        p1 = {spot: x if spot % 2 else y for spot in range(8)}
        p2 = {spot: y if spot % 2 else x for spot in range(8)}
        p3 = {0: up, 2: up, 4: down, 6: down, 5: up, 3: down}
        p4 = {0: x, 6: x, 1: y, 7: y}
        p5 = {1: up, 3: up}
        p6 = {2: x, 4: x, 5: y, 3: y}
        return p1, p2, p3, p4, p5, p6

    def gather(self, features):
        p1, p2, p3, p4, p5, p6 = self.routes()
        first = self.sent(features, p1)
        second = self.sent(features, p2)
        third = self.sent(first, p3)
        fourth = self.sent(first, p4)
        fifth = self.sent(second, p5)
        sixth = self.sent(third, p6)
        self.early = [features, first, second]
        self.late = [(self.EVEN, third, fifth), (self.MIDDLE, fourth, sixth)]
        return first

    def sums(self, spot, dense, rows_dev):
        start = gathered_sums(spot, dense, (0, 1, 2), (0, 2 * rows_dev), self.early)
        return [
            gathered_sums(spot, dense, (3, 4), (side * rows_dev, (side + 1) * rows_dev), self.late, start)
            for side in (1, 0)
        ]

    def scatter(self, spot, flipped, own, mate):
        p1, p2, p3, p4, p5, p6 = self.routes()
        to_last, to_plane, rest_plane = scattered_sums(flipped, own, mate, (4, 3), [[BF16], [BF16, F32]])
        by_sixth = self.sent(to_last, {**p4, **p6}, back=True)
        by_fifth = self.sent(to_plane, p5, back=True)
        kept, to_first, to_second = scattered_sums(flipped, own, mate, (0, 1, 2), [[F32]] * 3)
        out_third = summed_terms(spot, [rest_plane, by_sixth], [self.EVEN, self.MIDDLE])
        by_third = self.sent(out_third, p3, back=True)
        out_second = summed_terms(spot, [to_second, by_fifth], [None, 0b00001010])
        by_second = self.sent(out_second, p2, back=True)
        out_first = summed_terms(
            spot, [to_first, by_third, by_sixth], [None, self.EVEN | 0b00101000, self.ENDS]
        )
        by_first = self.sent(out_first, p1, back=True)
        return to_last, lambda: summed_terms(spot, [kept, by_second, by_first])


def local(features, tile_list, tile_count, tile_values, weight, bias, grad_out):
    count = lax.axis_size("blk")
    me = lax.axis_index("blk")
    window = tile_values.shape[1]
    reach = window // 4
    rows_dev, hidden = features.shape
    plane = 4
    pieces = 2 * plane
    core = (me % 2).astype(jnp.int32).reshape(1)
    place = ((me // 2) % plane).astype(jnp.int32).reshape(1)
    spot = (me % pieces).astype(jnp.int32).reshape(1)
    route = Relayed(count) if reach == 2 else Direct(count, reach)

    def swapped(value, distance):
        return lax.ppermute(value, "blk", [(s, s ^ distance) for s in range(count)])

    first = route.gather(features)
    first, tile_list, tile_count, tile_values = lax.optimization_barrier((first, tile_list, tile_count, tile_values))
    meta = jnp.concatenate([tile_list[0].reshape(window, -1), tile_count[0][:, None]], axis=1).reshape(-1)
    mate_meta, mate_values = swapped(meta, 1), swapped(tile_values[0], 1)
    dense, flipped = dense_tiles(spot, meta, mate_meta, tile_values[0], mate_values, rows_dev, route.table)
    mate_sum, own_sum = route.sums(spot, dense, rows_dev)
    agg, output, grad_pre, grad_agg = layer(own_sum, swapped(mate_sum, 1), weight, bias, grad_out)
    mate_grad = swapped(grad_agg, 1)

    keep, give = weight_terms(core, agg, grad_pre, pieces)
    first_sent, finish = route.scatter(spot, flipped, grad_agg, mate_grad)
    got, first_sent = lax.optimization_barrier((swapped(give, 1), first_sent))
    own_piece, *give_pieces = spread_halves(place, keep, got)
    plane_sum = summed_terms(spot, [own_piece] + [swapped(v, 2 * (d + 1)) for d, v in enumerate(give_pieces)])
    group = count // pieces
    values = [plane_sum] + [swapped(plane_sum, pieces * d) for d in range(1, group)]
    piece_sum, bias_sum = summed_planes(values, hidden // pieces)
    half = joined(place, [piece_sum] + [swapped(piece_sum, 2 * d) for d in range(1, plane)])
    grad_weight = whole_weight(core, half, swapped(half, 1))
    return (output, finish(), grad_weight, bias_sum[0])


def solution(mesh):
    placed = (
        P("blk", None),
        P("blk", None, None, None),
        P("blk", None),
        P("blk", None, None, None, None),
        P(),
        P(),
        P("blk", None),
    )
    return jax.shard_map(
        local,
        mesh=mesh,
        in_specs=placed,
        out_specs=(P("blk", None), P("blk", None), P(), P()),
        check_vma=False,
    )
```

```python
import jax
import jax.numpy as jnp
from jax import lax
from jax.experimental import pallas as pl
from jax.experimental.pallas import tpu as pltpu
from jax.sharding import PartitionSpec as P

BF16, F32 = jnp.bfloat16, jnp.float32
BIAS_ROWS = 16


def call(kernel, outs, ins, flops=0, smem=0):
    spec = lambda k: pl.BlockSpec(memory_space=pltpu.SMEM if k < smem else pltpu.VMEM)
    out_shape = [jax.ShapeDtypeStruct(s, d) for s, d in outs]
    moved = sum(a.size * a.dtype.itemsize for a in list(ins) + out_shape)
    return pl.pallas_call(
        kernel,
        out_shape=out_shape,
        in_specs=[spec(k) for k in range(len(ins))],
        out_specs=[pl.BlockSpec(memory_space=pltpu.VMEM)] * len(outs),
        compiler_params=pltpu.CompilerParams(vmem_limit_bytes=moved + moved // 4 + 4 * 1024 * 1024),
        cost_estimate=pl.CostEstimate(flops=flops, bytes_accessed=moved, transcendentals=0),
    )(*ins)


def dense_tiles(spot, own_meta, mate_meta, own_values, mate_values, rows_dev, table):
    window, slots, tile, _ = own_values.shape
    tile_rows = rows_dev // tile
    positions = len(table[0])

    def kernel(spot_ref, table_ref, own_meta_ref, mate_meta_ref, own_ref, mate_ref, dense_ref, flipped_ref):
        spot_now = spot_ref[0]
        dense_ref[...] = jnp.zeros_like(dense_ref)
        flipped_ref[...] = jnp.zeros_like(flipped_ref)

        def place(meta_ref, values_ref, first_j, shift, first_row):
            def slot(t, _):
                i, k = t // slots, t % slots
                j = 2 * i + first_j
                base = j * (2 * slots + 1)

                @pl.when(k < meta_ref[base + 2 * slots])
                def _():
                    row = pl.multiple_of((meta_ref[base + 2 * k] + first_row) * tile, tile)
                    column = table_ref[spot_now * positions + i + shift]
                    col = pl.multiple_of((column * tile_rows + meta_ref[base + 2 * k + 1]) * tile, tile)
                    values = values_ref[j, k]
                    dense_ref[pl.ds(row, tile), pl.ds(col, tile)] = values
                    flipped_ref[pl.ds(col, tile), pl.ds(row, tile)] = values.T

                return 0

            lax.fori_loop(0, (window // 2) * slots, slot, 0)

        place(own_meta_ref, own_ref, 0, 0, 0)
        place(mate_meta_ref, mate_ref, 1, 1 - spot_now % 2, tile_rows)

    wide = positions * rows_dev
    return call(
        kernel,
        [((2 * rows_dev, wide), BF16), ((wide, 2 * rows_dev), BF16)],
        [spot, jnp.asarray(table, jnp.int32).reshape(-1), own_meta, mate_meta, own_values, mate_values],
        smem=4,
    )


def gathered_sums(dense, columns, rows, sources, start=None):
    rows_dev, hidden = sources[0].shape
    first, last = rows

    def kernel(dense_ref, *refs):
        refs, out_ref = list(refs[:-1]), refs[-1]
        total = refs.pop(0)[first:last] if start is not None else jnp.zeros((last - first, hidden), F32)
        for column, ref in zip(columns, refs):
            part = dense_ref[first:last, column * rows_dev : (column + 1) * rows_dev]
            total = total + jnp.dot(part, ref[...], preferred_element_type=F32)
        out_ref[...] = total

    return call(
        kernel,
        [((last - first, hidden), F32)],
        [dense, *([] if start is None else [start]), *sources],
        flops=2 * (last - first) * rows_dev * hidden * len(sources),
    )[0]


def layer(core, own_sum, mate_sum, weight, bias, grad_out, pieces):
    rows_dev, hidden = own_sum.shape
    piece = hidden // pieces
    half = (pieces // 2, piece + BIAS_ROWS, hidden)

    def kernel(core_ref, own_ref, mate_ref, weight_ref, bias_ref, grad_out_ref, out_ref, ga_ref, keep_ref, give_ref):
        agg = (own_ref[...] + mate_ref[...]).astype(BF16)
        pre = jnp.dot(agg, weight_ref[...], preferred_element_type=F32) + bias_ref[...]
        sig = jax.nn.sigmoid(pre)
        out_ref[...] = (pre * sig).astype(BF16)
        grad_pre = (grad_out_ref[...].astype(F32) * sig * (1.0 + pre * (1.0 - sig))).astype(BF16)
        ga_ref[...] = lax.dot_general(
            grad_pre, weight_ref[...], (((1,), (1,)), ((), ())), preferred_element_type=F32
        ).astype(BF16)
        bias_term = jnp.sum(grad_pre.astype(F32), axis=0, keepdims=True)
        bias_rows = jnp.broadcast_to(bias_term, (BIAS_ROWS, hidden))
        terms = lax.dot_general(agg, grad_pre, (((0,), (0,)), ((), ())), preferred_element_type=F32)
        low, high = terms[: hidden // 2], terms[hidden // 2 :]
        even = core_ref[0] == 0
        for ref, value in ((keep_ref, jnp.where(even, low, high)), (give_ref, jnp.where(even, high, low))):
            for q in range(pieces // 2):
                ref[q, :piece] = value[q * piece : (q + 1) * piece].astype(ref.dtype)
                ref[q, piece:] = bias_rows.astype(ref.dtype)

    shape = (rows_dev, hidden)
    return call(
        kernel,
        [(shape, BF16), (shape, BF16), (half, F32), (half, BF16)],
        [core, own_sum, mate_sum, weight, bias.reshape(1, hidden), grad_out],
        flops=6 * rows_dev * hidden * hidden,
        smem=1,
    )


def spread_halves(place, keep, got):
    count, rows, hidden = keep.shape

    def kernel(place_ref, keep_ref, got_ref, own_ref, *out_refs):
        for other in range(count):
            q = place_ref[0] ^ other
            value = keep_ref[q] + got_ref[q].astype(F32)
            if other == 0:
                own_ref[...] = value
            else:
                out_refs[other - 1][...] = value.astype(BF16)

    return call(
        kernel,
        [((rows, hidden), F32)] + [((rows, hidden), BF16)] * (count - 1),
        [place, keep, got],
        smem=1,
    )


def summed_terms(*terms):
    def kernel(*refs):
        total = refs[0][...].astype(F32)
        for ref in refs[1:-1]:
            total = total + ref[...].astype(F32)
        refs[-1][...] = total.astype(BF16)

    return call(kernel, [(terms[0].shape, BF16)], list(terms))[0]


def tree_sum(values):
    values = [v.astype(F32) for v in values]
    while len(values) > 1:
        values = [values[k] + values[k + 1] for k in range(0, len(values), 2)]
    return values[0]


def summed_planes(values, piece):
    shape = values[0].shape

    def kernel(*refs):
        value_refs, (weight_ref, bias_ref) = refs[:-2], refs[-2:]
        total = tree_sum([ref[...] for ref in value_refs])
        weight_ref[...] = total[:piece].astype(BF16)
        bias_ref[...] = total[piece : piece + 8]

    return call(kernel, [((piece, shape[1]), BF16), ((8, shape[1]), F32)], list(values))


def joined(place, pieces):
    piece, hidden = pieces[0].shape
    count = len(pieces)

    def kernel(place_ref, *refs):
        piece_refs, out_ref = refs[:-1], refs[-1]
        for other, ref in enumerate(piece_refs):
            q = place_ref[0] ^ other
            out_ref[pl.ds(pl.multiple_of(q * piece, piece), piece)] = ref[...]

    return call(kernel, [((count * piece, hidden), BF16)], [place, *pieces], smem=1)[0]


def whole_weight(core, mine, other):
    rows, hidden = mine.shape

    def kernel(core_ref, mine_ref, other_ref, out_ref):
        core_now = core_ref[0]
        out_ref[pl.ds(pl.multiple_of(core_now * rows, rows), rows)] = mine_ref[...].astype(F32)
        out_ref[pl.ds(pl.multiple_of((1 - core_now) * rows, rows), rows)] = other_ref[...].astype(F32)

    return call(kernel, [((2 * rows, hidden), F32)], [core, mine, other], smem=1)[0]


def scattered_sums(flipped, own, mate, columns, dtypes):
    rows_dev, hidden = own.shape

    def kernel(flipped_ref, own_ref, mate_ref, *out_refs):
        out_refs = list(out_refs)
        for column, kinds in zip(columns, dtypes):
            part = pl.ds(column * rows_dev, rows_dev)
            total = jnp.dot(flipped_ref[part, :rows_dev], own_ref[...], preferred_element_type=F32)
            total += jnp.dot(flipped_ref[part, rows_dev:], mate_ref[...], preferred_element_type=F32)
            for kind in kinds:
                out_refs.pop(0)[...] = total.astype(kind)

    return call(
        kernel,
        [((rows_dev, hidden), kind) for kinds in dtypes for kind in kinds],
        [flipped, own, mate],
        flops=4 * rows_dev * rows_dev * hidden * len(columns),
    )


def after(value, *others):
    return lax.optimization_barrier((value, *others))


class Direct:
    def __init__(self, count, reach):
        self.count, self.reach, self.positions = count, reach, 2 * reach + 1
        self.table = [list(range(self.positions))] * 8

    def sent(self, value, chips, kept=lambda s: True):
        pairs = [(s, (s + 2 * chips) % self.count) for s in range(self.count) if kept(s)]
        return lax.ppermute(value, "blk", pairs)

    def gather(self, features):
        last = self.positions - 1
        self.sources = [
            features
            if m == self.reach
            else self.sent(features, self.reach - m, lambda s: m < last or s % 2 == 0)
            for m in range(self.positions)
        ]
        return self.sources[0]

    def sums(self, dense, rows_dev):
        columns = range(self.positions)
        return [
            gathered_sums(dense, columns, (side * rows_dev, (side + 1) * rows_dev), self.sources) for side in (1, 0)
        ]

    def scatter(self, flipped, own, mate):
        kinds = [[F32 if m == self.reach else BF16] for m in range(self.positions)]
        terms = scattered_sums(flipped, own, mate, range(self.positions), kinds)
        last = self.positions - 1
        arrived = [
            self.sent(terms[m], m - self.reach, lambda s: m < last or s % 2 == 0)
            for m in range(self.positions)
            if m != self.reach
        ]
        return terms[0], terms[0], [terms[self.reach], *arrived]


class Relayed(Direct):
    def __init__(self, count, reach):
        super().__init__(count, reach)
        self.table = [[2, 3, 0, 4, 1], [1, 3, 0, 4, 2]] * 2 + [[1, 3, 0, 4, 2]] * 4

    def routed(self, value, step):
        pairs = [(s, step(s) % self.count) for s in range(self.count) if step(s) is not None]
        return lax.ppermute(value, "blk", pairs)

    @staticmethod
    def plane_step(s, sign):
        return None if s % 2 else s + (8 * sign if s % 8 < 4 else -8 * sign)

    def gather(self, features):
        first = self.routed(features, lambda s: s + 4 if s % 2 else s ^ 4)
        back, on = self.sent(features, 1), self.sent(features, -1)
        relayed = self.routed(first, lambda s: self.plane_step(s, 1))
        self.sources = [features, first, relayed, back, on]
        return first

    def sums(self, dense, rows_dev):
        start = gathered_sums(dense, (0, 1, 2), (0, 2 * rows_dev), self.sources[:3])
        return [
            gathered_sums(dense, (3, 4), (side * rows_dev, (side + 1) * rows_dev), self.sources[3:], start)
            for side in (1, 0)
        ]

    def scatter(self, flipped, own, mate):
        to_plane, to_second, rest_second = scattered_sums(flipped, own, mate, (2, 1), [[BF16], [BF16, F32]])
        relayed = self.routed(to_plane, lambda s: self.plane_step(s, -1))
        straight = self.routed(to_second, lambda s: s - 4 if s % 2 else None)
        to_back, to_on, kept = scattered_sums(flipped, own, mate, (3, 4, 0), [[BF16], [BF16], [F32]])
        back, on = self.sent(to_back, -1), self.sent(to_on, 1)
        out = summed_terms(rest_second, relayed)
        swapped_sums = self.routed(out, lambda s: None if s % 2 else s ^ 4)
        return to_back, out, [kept, straight, back, on, swapped_sums]


def local(features, tile_list, tile_count, tile_values, weight, bias, grad_out):
    count = lax.axis_size("blk")
    me = lax.axis_index("blk")
    window = tile_values.shape[1]
    reach = window // 4
    rows_dev, hidden = features.shape
    plane = 4
    pieces = 2 * plane
    core = (me % 2).astype(jnp.int32).reshape(1)
    place = ((me // 2) % plane).astype(jnp.int32).reshape(1)
    spot = (me % pieces).astype(jnp.int32).reshape(1)
    route = (Relayed if reach == 2 else Direct)(count, reach)

    def swapped(value, distance):
        return lax.ppermute(value, "blk", [(s, s ^ distance) for s in range(count)])

    first = route.gather(features)
    first, tile_list, tile_count, tile_values = after(first, tile_list, tile_count, tile_values)
    meta = jnp.concatenate([tile_list[0].reshape(window, -1), tile_count[0][:, None]], axis=1).reshape(-1)
    mate_meta, mate_values = swapped(meta, 1), swapped(tile_values[0], 1)
    dense, flipped = dense_tiles(spot, meta, mate_meta, tile_values[0], mate_values, rows_dev, route.table)
    mate_sum, own_sum = route.sums(dense, rows_dev)
    output, grad_agg, keep, give = layer(core, own_sum, swapped(mate_sum, 1), weight, bias, grad_out, pieces)

    mate_grad, got = swapped(grad_agg, 1), swapped(give, 1)
    own_piece, *give_pieces = spread_halves(place, keep, got)
    mate_grad, *give_pieces = after(mate_grad, *give_pieces)
    sent_first, sent_last, arriving = route.scatter(flipped, grad_agg, mate_grad)
    own_piece, _ = after(own_piece, sent_first)
    plane_sum = summed_terms(own_piece, *[swapped(v, 2 * (d + 1)) for d, v in enumerate(give_pieces)])
    values = [plane_sum] + [swapped(plane_sum, pieces * d) for d in range(1, count // pieces)]
    values[0], _ = after(values[0], sent_last)
    piece_sum, bias_sum = summed_planes(values, hidden // pieces)
    gathered = [swapped(piece_sum, 2 * d) for d in range(1, plane)]
    piece_sum, *arriving = after(piece_sum, *arriving)
    half = joined(place, [piece_sum, *gathered])
    grad_weight = whole_weight(core, half, swapped(half, 1))
    return (output, summed_terms(*arriving), grad_weight, bias_sum[0])


def solution(mesh):
    placed = (
        P("blk", None),
        P("blk", None, None, None),
        P("blk", None),
        P("blk", None, None, None, None),
        P(),
        P(),
        P("blk", None),
    )
    return jax.shard_map(
        local,
        mesh=mesh,
        in_specs=placed,
        out_specs=(P("blk", None), P("blk", None), P(), P()),
        check_vma=False,
    )
```

```python
import jax
import jax.numpy as jnp
from jax import lax
from jax.experimental import pallas as pl
from jax.experimental.pallas import tpu as pltpu
from jax.sharding import PartitionSpec as P

BF16, F32 = jnp.bfloat16, jnp.float32
BIAS_ROWS = 16


def call(kernel, outs, ins, flops=0, smem=0):
    spec = lambda k: pl.BlockSpec(memory_space=pltpu.SMEM if k < smem else pltpu.VMEM)
    out_shape = [jax.ShapeDtypeStruct(s, d) for s, d in outs]
    moved = sum(a.size * a.dtype.itemsize for a in list(ins) + out_shape)
    return pl.pallas_call(
        kernel,
        out_shape=out_shape,
        in_specs=[spec(k) for k in range(len(ins))],
        out_specs=[pl.BlockSpec(memory_space=pltpu.VMEM)] * len(outs),
        compiler_params=pltpu.CompilerParams(vmem_limit_bytes=moved + moved // 4 + 4 * 1024 * 1024),
        cost_estimate=pl.CostEstimate(flops=0, bytes_accessed=0, transcendentals=0),
    )(*ins)


def dense_tiles(spot, own_meta, mate_meta, own_values, mate_values, rows_dev, table):
    window, slots, tile, _ = own_values.shape
    tile_rows = rows_dev // tile
    positions = len(table[0])

    def kernel(spot_ref, table_ref, own_meta_ref, mate_meta_ref, own_ref, mate_ref, dense_ref, flipped_ref):
        spot_now = spot_ref[0]
        dense_ref[...] = jnp.zeros_like(dense_ref)
        flipped_ref[...] = jnp.zeros_like(flipped_ref)

        def place(meta_ref, values_ref, first_j, shift, first_row):
            def slot(t, _):
                i, k = t // slots, t % slots
                j = 2 * i + first_j
                base = j * (2 * slots + 1)

                @pl.when(k < meta_ref[base + 2 * slots])
                def _():
                    row = pl.multiple_of((meta_ref[base + 2 * k] + first_row) * tile, tile)
                    column = table_ref[spot_now * positions + i + shift]
                    col = pl.multiple_of((column * tile_rows + meta_ref[base + 2 * k + 1]) * tile, tile)
                    values = values_ref[j, k]
                    dense_ref[pl.ds(row, tile), pl.ds(col, tile)] = values
                    flipped_ref[pl.ds(col, tile), pl.ds(row, tile)] = values.T

                return 0

            lax.fori_loop(0, (window // 2) * slots, slot, 0)

        place(own_meta_ref, own_ref, 0, 0, 0)
        place(mate_meta_ref, mate_ref, 1, 1 - spot_now % 2, tile_rows)

    wide = positions * rows_dev
    return call(
        kernel,
        [((2 * rows_dev, wide), BF16), ((wide, 2 * rows_dev), BF16)],
        [spot, jnp.asarray(table, jnp.int32).reshape(-1), own_meta, mate_meta, own_values, mate_values],
        smem=4,
    )


def gathered_sums(dense, columns, rows, sources, start=None):
    rows_dev, hidden = sources[0].shape
    first, last = rows

    def kernel(dense_ref, *refs):
        refs, out_ref = list(refs[:-1]), refs[-1]
        total = refs.pop(0)[first:last] if start is not None else jnp.zeros((last - first, hidden), F32)
        for column, ref in zip(columns, refs):
            part = dense_ref[first:last, column * rows_dev : (column + 1) * rows_dev]
            total = total + jnp.dot(part, ref[...], preferred_element_type=F32)
        out_ref[...] = total

    return call(
        kernel,
        [((last - first, hidden), F32)],
        [dense, *([] if start is None else [start]), *sources],
        flops=2 * (last - first) * rows_dev * hidden * len(sources),
    )[0]


def layer(spot, own_sum, mate_sum, weight, bias, grad_out, pieces):
    rows_dev, hidden = own_sum.shape
    piece = hidden // pieces
    half = (pieces // 2, piece + BIAS_ROWS, hidden)

    def kernel(spot_ref, own_ref, mate_ref, weight_ref, bias_ref, grad_out_ref, out_ref, ga_ref, keep_ref, give_ref):
        agg = (own_ref[...] + mate_ref[...]).astype(BF16)
        pre = jnp.dot(agg, weight_ref[...], preferred_element_type=F32) + bias_ref[...]
        sig = jax.nn.sigmoid(pre)
        out_ref[...] = (pre * sig).astype(BF16)
        grad_pre = (grad_out_ref[...].astype(F32) * sig * (1.0 + pre * (1.0 - sig))).astype(BF16)
        ga_ref[...] = lax.dot_general(
            grad_pre, weight_ref[...], (((1,), (1,)), ((), ())), preferred_element_type=F32
        ).astype(BF16)
        bias_term = jnp.sum(grad_pre.astype(F32), axis=0, keepdims=True)
        bias_rows = jnp.broadcast_to(bias_term, (BIAS_ROWS, hidden))
        terms = lax.dot_general(agg, grad_pre, (((0,), (0,)), ((), ())), preferred_element_type=F32)
        low, high = terms[: hidden // 2], terms[hidden // 2 :]
        even = spot_ref[0] % 2 == 0
        for ref, value in ((keep_ref, jnp.where(even, low, high)), (give_ref, jnp.where(even, high, low))):
            for q in range(pieces // 2):
                ref[q, :piece] = value[q * piece : (q + 1) * piece].astype(ref.dtype)
                ref[q, piece:] = bias_rows.astype(ref.dtype)

    shape = (rows_dev, hidden)
    return call(
        kernel,
        [(shape, BF16), (shape, BF16), (half, F32), (half, BF16)],
        [spot, own_sum, mate_sum, weight, bias.reshape(1, hidden), grad_out],
        flops=6 * rows_dev * hidden * hidden,
        smem=1,
    )


def folded(spot, bit, keep, got, last=False):
    count, rows, hidden = keep.shape
    left = count if last else count // 2

    def kernel(spot_ref, keep_ref, got_ref, *out_refs):
        mine = (spot_ref[0] >> bit) % 2
        for p in range(left):
            if last:
                out_refs[0][p] = (keep_ref[p] + got_ref[p].astype(F32)).astype(BF16)
                continue
            for ref, side in zip(out_refs, (mine, 1 - mine)):
                q = side * left + p
                ref[p] = (keep_ref[q] + got_ref[q].astype(F32)).astype(ref.dtype)

    shape = (left, rows, hidden)
    outs = [(shape, BF16)] if last else [(shape, F32), (shape, BF16)]
    return call(kernel, outs, [spot, keep, got], smem=1)


def summed_terms(*terms):
    def kernel(*refs):
        total = refs[0][...].astype(F32)
        for ref in refs[1:-1]:
            total = total + ref[...].astype(F32)
        refs[-1][...] = total.astype(BF16)

    return call(kernel, [(terms[0].shape, BF16)], list(terms))[0]


def joined(spot, bit, mine, other):
    rows, hidden = mine.shape

    def kernel(spot_ref, mine_ref, other_ref, out_ref):
        side = (spot_ref[0] >> bit) % 2
        out_ref[pl.ds(pl.multiple_of(side * rows, rows), rows)] = mine_ref[...].astype(out_ref.dtype)
        out_ref[pl.ds(pl.multiple_of((1 - side) * rows, rows), rows)] = other_ref[...].astype(out_ref.dtype)

    return call(kernel, [((2 * rows, hidden), F32 if bit == 0 else BF16)], [spot, mine, other], smem=1)[0]


def finished(mine, other, piece):
    hidden = mine.shape[1]

    def kernel(mine_ref, other_ref, weight_ref, bias_ref):
        total = mine_ref[...].astype(F32) + other_ref[...].astype(F32)
        weight_ref[...] = total[:piece].astype(BF16)
        bias_ref[...] = total[piece : piece + 8]

    return call(kernel, [((piece, hidden), BF16), ((8, hidden), F32)], [mine, other])


def scattered_sums(flipped, own, mate, columns, dtypes):
    rows_dev, hidden = own.shape

    def kernel(flipped_ref, own_ref, mate_ref, *out_refs):
        out_refs = list(out_refs)
        for column, kinds in zip(columns, dtypes):
            part = pl.ds(column * rows_dev, rows_dev)
            total = jnp.dot(flipped_ref[part, :rows_dev], own_ref[...], preferred_element_type=F32)
            total += jnp.dot(flipped_ref[part, rows_dev:], mate_ref[...], preferred_element_type=F32)
            for kind in kinds:
                out_refs.pop(0)[...] = total.astype(kind)

    return call(
        kernel,
        [((rows_dev, hidden), kind) for kinds in dtypes for kind in kinds],
        [flipped, own, mate],
        flops=4 * rows_dev * rows_dev * hidden * len(columns),
    )


def after(value, *others):
    return lax.optimization_barrier((value, *others))


class Direct:
    def __init__(self, count, reach):
        self.count, self.reach, self.positions = count, reach, 2 * reach + 1
        self.table = [list(range(self.positions))] * 8

    def sent(self, value, chips, kept=lambda s: True):
        pairs = [(s, (s + 2 * chips) % self.count) for s in range(self.count) if kept(s)]
        return lax.ppermute(value, "blk", pairs)

    def gather(self, features):
        last = self.positions - 1
        self.sources = [
            features
            if m == self.reach
            else self.sent(features, self.reach - m, lambda s: m < last or s % 2 == 0)
            for m in range(self.positions)
        ]
        return self.sources[0]

    def sums(self, dense, rows_dev):
        columns = range(self.positions)
        return [
            gathered_sums(dense, columns, (side * rows_dev, (side + 1) * rows_dev), self.sources) for side in (1, 0)
        ]

    def scatter(self, flipped, own, mate):
        kinds = [[F32 if m == self.reach else BF16] for m in range(self.positions)]
        terms = scattered_sums(flipped, own, mate, range(self.positions), kinds)
        last = self.positions - 1
        arrived = [
            self.sent(terms[m], m - self.reach, lambda s: m < last or s % 2 == 0)
            for m in range(self.positions)
            if m != self.reach
        ]
        return terms[0], terms[0], [terms[self.reach], *arrived]


def local(features, tile_list, tile_count, tile_values, weight, bias, grad_out):
    count = lax.axis_size("blk")
    me = lax.axis_index("blk")
    window = tile_values.shape[1]
    reach = window // 4
    rows_dev, hidden = features.shape
    pieces = 8
    spot = (me % pieces).astype(jnp.int32).reshape(1)
    route = Direct(count, reach)

    def swapped(value, distance):
        return lax.ppermute(value, "blk", [(s, s ^ distance) for s in range(count)])

    route.gather(features)
    mate_values, tile_list, tile_count = after(swapped(tile_values[0], 1), tile_list, tile_count)
    meta = jnp.concatenate([tile_list[0].reshape(window, -1), tile_count[0][:, None]], axis=1).reshape(-1)
    mate_meta = swapped(meta, 1)
    dense, flipped = dense_tiles(spot, meta, mate_meta, tile_values[0], mate_values, rows_dev, route.table)
    mate_sum, own_sum = route.sums(dense, rows_dev)
    output, grad_agg, keep, give = layer(spot, own_sum, swapped(mate_sum, 1), weight, bias, grad_out, pieces)

    mate_grad, got = swapped(grad_agg, 1), swapped(give, 1)
    keep, give = folded(spot, 1, keep, got)
    mate_grad, give = after(mate_grad, give)
    sent_first, sent_last, arriving = route.scatter(flipped, grad_agg, mate_grad)
    got = swapped(give, 2)
    got, _ = after(got, sent_first)
    keep, give = folded(spot, 2, keep, got)
    total = folded(spot, 2, keep, swapped(give, 4), last=True)[0][0]
    step = pieces
    while 2 * step < count:
        total = summed_terms(total, swapped(total, step))
        step *= 2
    total, bias_sum = finished(total, swapped(total, step), hidden // pieces)
    grad_features = summed_terms(*arriving)
    for bit in (2, 1, 0):
        other = swapped(total, 1 << bit)
        if bit == 2:
            other, grad_features = after(other, grad_features)
        total = joined(spot, bit, total, other)
    return (output, grad_features, total, bias_sum[0])


def solution(mesh):
    placed = (
        P("blk", None),
        P("blk", None, None, None),
        P("blk", None),
        P("blk", None, None, None, None),
        P(),
        P(),
        P("blk", None),
    )
    return jax.shard_map(
        local,
        mesh=mesh,
        in_specs=placed,
        out_specs=(P("blk", None), P("blk", None), P(), P()),
        check_vma=False,
    )
```

```python
import jax
import jax.numpy as jnp
from jax import lax
from jax.experimental import pallas as pl
from jax.experimental.pallas import tpu as pltpu
from jax.sharding import PartitionSpec as P

BF16, F32 = jnp.bfloat16, jnp.float32
BIAS_ROWS = 16


def call(kernel, outs, ins, flops=0, smem=0):
    spec = lambda k: pl.BlockSpec(memory_space=pltpu.SMEM if k < smem else pltpu.VMEM)
    out_shape = [jax.ShapeDtypeStruct(s, d) for s, d in outs]
    moved = sum(a.size * a.dtype.itemsize for a in list(ins) + out_shape)
    return pl.pallas_call(
        kernel,
        out_shape=out_shape,
        in_specs=[spec(k) for k in range(len(ins))],
        out_specs=[pl.BlockSpec(memory_space=pltpu.VMEM)] * len(outs),
        compiler_params=pltpu.CompilerParams(vmem_limit_bytes=moved + moved // 4 + 4 * 1024 * 1024),
        cost_estimate=pl.CostEstimate(flops=0, bytes_accessed=0, transcendentals=0),
    )(*ins)


def dense_tiles(spot, own_meta, mate_meta, own_values, mate_values, rows_dev, positions):
    window, slots, tile, _ = own_values.shape
    tile_rows = rows_dev // tile

    def kernel(spot_ref, own_meta_ref, mate_meta_ref, own_ref, mate_ref, dense_ref, flipped_ref):
        dense_ref[...] = jnp.zeros_like(dense_ref)
        flipped_ref[...] = jnp.zeros_like(flipped_ref)

        def place(meta_ref, values_ref, first_j, shift, first_row):
            def slot(t, _):
                i, k = t // slots, t % slots
                j = 2 * i + first_j
                base = j * (2 * slots + 1)

                @pl.when(k < meta_ref[base + 2 * slots])
                def _():
                    row = pl.multiple_of((meta_ref[base + 2 * k] + first_row) * tile, tile)
                    col = pl.multiple_of(((i + shift) * tile_rows + meta_ref[base + 2 * k + 1]) * tile, tile)
                    values = values_ref[j, k]
                    dense_ref[pl.ds(row, tile), pl.ds(col, tile)] = values
                    flipped_ref[pl.ds(col, tile), pl.ds(row, tile)] = values.T

                return 0

            lax.fori_loop(0, (window // 2) * slots, slot, 0)

        place(own_meta_ref, own_ref, 0, 0, 0)
        place(mate_meta_ref, mate_ref, 1, 1 - spot_ref[0] % 2, tile_rows)

    wide = positions * rows_dev
    return call(
        kernel,
        [((2 * rows_dev, wide), BF16), ((wide, 2 * rows_dev), BF16)],
        [spot, own_meta, mate_meta, own_values, mate_values],
        smem=3,
    )


def gathered_sums(dense, columns, rows, sources, start=None):
    rows_dev, hidden = sources[0].shape
    first, last = rows

    def kernel(dense_ref, *refs):
        refs, out_ref = list(refs[:-1]), refs[-1]
        total = refs.pop(0)[first:last] if start is not None else jnp.zeros((last - first, hidden), F32)
        for column, ref in zip(columns, refs):
            part = dense_ref[first:last, column * rows_dev : (column + 1) * rows_dev]
            total = total + jnp.dot(part, ref[...], preferred_element_type=F32)
        out_ref[...] = total

    return call(
        kernel,
        [((last - first, hidden), F32)],
        [dense, *([] if start is None else [start]), *sources],
        flops=2 * (last - first) * rows_dev * hidden * len(sources),
    )[0]


def layer(spot, own_sum, mate_sum, weight, bias, grad_out, pieces):
    rows_dev, hidden = own_sum.shape
    piece = hidden // pieces
    half = (pieces // 2, piece + BIAS_ROWS, hidden)

    def kernel(spot_ref, own_ref, mate_ref, weight_ref, bias_ref, grad_out_ref, out_ref, ga_ref, keep_ref, give_ref):
        agg = (own_ref[...] + mate_ref[...]).astype(BF16)
        pre = jnp.dot(agg, weight_ref[...], preferred_element_type=F32) + bias_ref[...]
        sig = jax.nn.sigmoid(pre)
        out_ref[...] = (pre * sig).astype(BF16)
        grad_pre = (grad_out_ref[...].astype(F32) * sig * (1.0 + pre * (1.0 - sig))).astype(BF16)
        ga_ref[...] = lax.dot_general(
            grad_pre, weight_ref[...], (((1,), (1,)), ((), ())), preferred_element_type=F32
        ).astype(BF16)
        bias_term = jnp.sum(grad_pre.astype(F32), axis=0, keepdims=True)
        bias_rows = jnp.broadcast_to(bias_term, (BIAS_ROWS, hidden))
        terms = lax.dot_general(agg, grad_pre, (((0,), (0,)), ((), ())), preferred_element_type=F32)
        low, high = terms[: hidden // 2], terms[hidden // 2 :]
        even = spot_ref[0] % 2 == 0
        for ref, value in ((keep_ref, jnp.where(even, low, high)), (give_ref, jnp.where(even, high, low))):
            for q in range(pieces // 2):
                ref[q, :piece] = value[q * piece : (q + 1) * piece].astype(ref.dtype)
                ref[q, piece:] = bias_rows.astype(ref.dtype)

    shape = (rows_dev, hidden)
    return call(
        kernel,
        [(shape, BF16), (shape, BF16), (half, F32), (half, BF16)],
        [spot, own_sum, mate_sum, weight, bias.reshape(1, hidden), grad_out],
        flops=6 * rows_dev * hidden * hidden,
        smem=1,
    )


def folded(spot, bit, keep, got, last=False):
    count, rows, hidden = keep.shape
    left = count if last else count // 2

    def kernel(spot_ref, keep_ref, got_ref, *out_refs):
        mine = (spot_ref[0] >> bit) % 2
        for p in range(left):
            if last:
                out_refs[0][p] = (keep_ref[p] + got_ref[p].astype(F32)).astype(BF16)
                continue
            for ref, side in zip(out_refs, (mine, 1 - mine)):
                q = side * left + p
                ref[p] = (keep_ref[q] + got_ref[q].astype(F32)).astype(ref.dtype)

    shape = (left, rows, hidden)
    outs = [(shape, BF16)] if last else [(shape, F32), (shape, BF16)]
    return call(kernel, outs, [spot, keep, got], smem=1)


def summed_terms(spot, terms, masks=None):
    masks = masks or [None] * len(terms)

    def kernel(spot_ref, *refs):
        total = None
        for ref, mask in zip(refs, masks):
            value = ref[...].astype(F32)
            if mask is not None:
                value = jnp.where((mask >> spot_ref[0]) % 2 == 1, value, 0.0)
            total = value if total is None else total + value
        refs[-1][...] = total.astype(BF16)

    return call(kernel, [(terms[0].shape, BF16)], [spot, *terms], smem=1)[0]


def joined(spot, bits, pieces, dtype):
    rows, hidden = pieces[0].shape
    low, high = bits

    def kernel(spot_ref, *refs):
        side = (spot_ref[0] >> low) % (1 << (high - low))
        for other, ref in enumerate(refs[:-1]):
            refs[-1][pl.ds(pl.multiple_of((side ^ other) * rows, rows), rows)] = ref[...].astype(dtype)

    return call(kernel, [((len(pieces) * rows, hidden), dtype)], [spot, *pieces], smem=1)[0]


def finished(mine, other, piece):
    hidden = mine.shape[1]

    def kernel(mine_ref, other_ref, weight_ref, bias_ref):
        total = mine_ref[...].astype(F32) + other_ref[...].astype(F32)
        weight_ref[...] = total[:piece].astype(BF16)
        bias_ref[...] = total[piece : piece + 8]

    return call(kernel, [((piece, hidden), BF16), ((8, hidden), F32)], [mine, other])


def scattered_sums(flipped, own, mate, columns, dtypes, spot=None, lookup=None):
    rows_dev, hidden = own.shape
    extra = [] if lookup is None else [spot, jnp.asarray(lookup, jnp.int32).reshape(-1)]

    def kernel(*refs):
        refs = list(refs)
        picks = [refs.pop(0) for _ in extra]
        flipped_ref, own_ref, mate_ref, *out_refs = refs
        for column, kinds in zip(columns, dtypes):
            if picks:
                column = picks[1][picks[0][0] * len(lookup[0]) + column]
                part = pl.ds(pl.multiple_of(column * rows_dev, rows_dev), rows_dev)
            else:
                part = pl.ds(column * rows_dev, rows_dev)
            total = jnp.dot(flipped_ref[part, :rows_dev], own_ref[...], preferred_element_type=F32)
            total += jnp.dot(flipped_ref[part, rows_dev:], mate_ref[...], preferred_element_type=F32)
            for kind in kinds:
                out_refs.pop(0)[...] = total.astype(kind)

    return call(
        kernel,
        [((rows_dev, hidden), kind) for kinds in dtypes for kind in kinds],
        [*extra, flipped, own, mate],
        flops=4 * rows_dev * rows_dev * hidden * len(columns),
        smem=len(extra),
    )


def after(value, *others):
    return lax.optimization_barrier((value, *others))


class Direct:
    def __init__(self, count, reach, spot):
        self.count, self.reach, self.positions, self.spot = count, reach, 2 * reach + 1, spot

    def sent(self, value, chips, kept=lambda s: True):
        pairs = [(s, (s + 2 * chips) % self.count) for s in range(self.count) if kept(s)]
        return lax.ppermute(value, "blk", pairs)

    def gather(self, features):
        last = self.positions - 1
        self.sources = [
            features
            if m == self.reach
            else self.sent(features, self.reach - m, lambda s: m < last or s % 2 == 0)
            for m in range(self.positions)
        ]

    def sums(self, dense, rows_dev):
        columns = range(self.positions)
        return [
            gathered_sums(dense, columns, (side * rows_dev, (side + 1) * rows_dev), self.sources) for side in (1, 0)
        ]

    def scatter(self, flipped, own, mate):
        self.flipped, self.own, self.mate = flipped, own, mate

    def step(self, k, token):
        if k != 1:
            return []
        _, mate = after(token, self.mate)
        kinds = [[F32 if m == self.reach else BF16] for m in range(self.positions)]
        terms = scattered_sums(self.flipped, self.own, mate, range(self.positions), kinds)
        last = self.positions - 1
        self.arriving = [
            term if m == self.reach else self.sent(term, m - self.reach, lambda s: m < last or s % 2 == 0)
            for m, term in enumerate(terms)
        ]
        return terms[:1]

    def finish(self):
        return summed_terms(self.spot, self.arriving)


class Relayed(Direct):
    EVEN, MIDDLE, ENDS, ODD_LOW = 0b01010101, 0b00111100, 0b11000011, 0b00001010
    LOOKUP = [
        [2, 4, 3, 0, 1], [2, 3, 4, 0, 1],
        [2, 4, 1, 0, 3], [2, 1, 4, 0, 3],
        [2, 0, 3, 4, 1], [2, 3, 0, 4, 1],
        [2, 0, 1, 4, 3], [2, 1, 0, 4, 3],
    ]

    def routed(self, value, steps):
        pairs = [(s, (s + steps[s % 8]) % self.count) for s in range(self.count) if s % 8 in steps]
        return lax.ppermute(value, "blk", pairs)

    def step(self, k, token):
        x = {spot: (spot ^ 2) - spot for spot in range(8)}
        y = {spot: (spot ^ 4) - spot for spot in range(8)}
        straight = {spot: (y if spot % 2 else x)[spot] for spot in range(8)}
        across = {spot: (x if spot % 2 else y)[spot] for spot in range(8)}
        take = lambda mate, *args: scattered_sums(self.flipped, self.own, mate, *args, self.spot, self.LOOKUP)
        if k == 1:
            _, mate = after(token, self.mate)
            to_last, self.to_plane, self.plane_rest = take(mate, (4, 3), [[BF16], [BF16, F32]])
            self.from_last = self.routed(to_last, straight)
            return [to_last]
        if k == 2:
            _, mate = after(token, self.mate)
            _, to_plane = after(token, self.to_plane)
            self.from_plane = self.routed(to_plane, {1: -8, 3: -8})
            self.kept, self.to_across, self.to_straight = take(mate, (0, 1, 2), [[F32]] * 3)
            return [self.from_last, self.kept]
        if k == 3:
            _, rest = after(token, self.plane_rest)
            out = summed_terms(self.spot, [rest, self.from_last], [self.EVEN, self.MIDDLE])
            self.from_planes = self.routed(out, {0: -8, 2: -8, 4: 8, 6: 8, 5: -8, 3: 8})
            return [out, self.from_plane]
        if k == 4:
            _, rest = after(token, self.to_straight)
            out = summed_terms(self.spot, [rest, self.from_plane], [None, self.ODD_LOW])
            second = self.routed(out, straight)
            out = summed_terms(
                self.spot,
                [self.to_across, self.from_planes, self.from_last],
                [None, self.EVEN | 0b00101000, self.ENDS],
            )
            self.arriving = [self.kept, second, self.routed(out, across)]
        return []


def local(features, tile_list, tile_count, tile_values, weight, bias, grad_out):
    count = lax.axis_size("blk")
    me = lax.axis_index("blk")
    window = tile_values.shape[1]
    reach = window // 4
    rows_dev, hidden = features.shape
    pieces = 8
    spot = (me % pieces).astype(jnp.int32).reshape(1)
    route = (Relayed if reach == 2 else Direct)(count, reach, spot)

    def swapped(value, distance):
        return lax.ppermute(value, "blk", [(s, s ^ distance) for s in range(count)])

    route.gather(features)
    mate_values, tile_list, tile_count = after(swapped(tile_values[0], 1), tile_list, tile_count)
    meta = jnp.concatenate([tile_list[0].reshape(window, -1), tile_count[0][:, None]], axis=1).reshape(-1)
    mate_meta = swapped(meta, 1)
    dense, flipped = dense_tiles(spot, meta, mate_meta, tile_values[0], mate_values, rows_dev, route.positions)
    mate_sum, own_sum = route.sums(dense, rows_dev)
    output, grad_agg, keep, give = layer(spot, own_sum, swapped(mate_sum, 1), weight, bias, grad_out, pieces)

    mate_grad, got = swapped(grad_agg, 1), swapped(give, 1)
    route.scatter(flipped, grad_agg, mate_grad)

    def exchanged(k, value, distance):
        other = swapped(value, distance)
        return after(other, *route.step(k, value))[0]

    keep, give = folded(spot, 2, keep, got)
    keep, give = folded(spot, 1, keep, exchanged(0, give, 4))
    total = folded(spot, 1, keep, exchanged(1, give, 2), last=True)[0][0]
    step, k = pieces, 2
    while step < count:
        other = exchanged(k, total, step)
        step, k = 2 * step, k + 1
        if step < count:
            total = summed_terms(spot, [total, other])
        else:
            total, bias_sum = finished(total, other, hidden // pieces)
    gathered = [total] + [swapped(total, 2 * d) for d in range(1, pieces // 2)]
    route.step(4, total)
    half = joined(spot, (1, 3), gathered, BF16)
    grad_weight = joined(spot, (0, 1), [half, swapped(half, 1)], F32)
    return (output, route.finish(), grad_weight, bias_sum[0])


def solution(mesh):
    placed = (
        P("blk", None),
        P("blk", None, None, None),
        P("blk", None),
        P("blk", None, None, None, None),
        P(),
        P(),
        P("blk", None),
    )
    return jax.shard_map(
        local,
        mesh=mesh,
        in_specs=placed,
        out_specs=(P("blk", None), P("blk", None), P(), P()),
        check_vma=False,
    )
```

```python
import jax
import jax.numpy as jnp
from jax import lax
from jax.experimental import pallas as pl
from jax.experimental.pallas import tpu as pltpu
from jax.sharding import PartitionSpec as P

BF16, F32 = jnp.bfloat16, jnp.float32
BIAS_ROWS = 16


def call(kernel, outs, ins, flops=0, smem=0):
    spec = lambda k: pl.BlockSpec(memory_space=pltpu.SMEM if k < smem else pltpu.VMEM)
    out_shape = [jax.ShapeDtypeStruct(s, d) for s, d in outs]
    moved = sum(a.size * a.dtype.itemsize for a in list(ins) + out_shape)
    return pl.pallas_call(
        kernel,
        out_shape=out_shape,
        in_specs=[spec(k) for k in range(len(ins))],
        out_specs=[pl.BlockSpec(memory_space=pltpu.VMEM)] * len(outs),
        compiler_params=pltpu.CompilerParams(vmem_limit_bytes=moved + moved // 4 + 4 * 1024 * 1024),
        cost_estimate=pl.CostEstimate(flops=0, bytes_accessed=0, transcendentals=0),
    )(*ins)


def dense_tiles(spot, own_meta, mate_meta, own_values, mate_values, rows_dev, positions):
    window, slots, tile, _ = own_values.shape
    tile_rows = rows_dev // tile

    def kernel(spot_ref, own_meta_ref, mate_meta_ref, own_ref, mate_ref, dense_ref, flipped_ref):
        dense_ref[...] = jnp.zeros_like(dense_ref)
        flipped_ref[...] = jnp.zeros_like(flipped_ref)

        def place(meta_ref, values_ref, first_j, shift, first_row):
            def slot(t, _):
                i, k = t // slots, t % slots
                j = 2 * i + first_j
                base = j * (2 * slots + 1)

                @pl.when(k < meta_ref[base + 2 * slots])
                def _():
                    row = pl.multiple_of((meta_ref[base + 2 * k] + first_row) * tile, tile)
                    col = pl.multiple_of(((i + shift) * tile_rows + meta_ref[base + 2 * k + 1]) * tile, tile)
                    values = values_ref[j, k]
                    dense_ref[pl.ds(row, tile), pl.ds(col, tile)] = values
                    flipped_ref[pl.ds(col, tile), pl.ds(row, tile)] = values.T

                return 0

            lax.fori_loop(0, (window // 2) * slots, slot, 0)

        place(own_meta_ref, own_ref, 0, 0, 0)
        place(mate_meta_ref, mate_ref, 1, 1 - spot_ref[0] % 2, tile_rows)

    wide = positions * rows_dev
    return call(
        kernel,
        [((2 * rows_dev, wide), BF16), ((wide, 2 * rows_dev), BF16)],
        [spot, own_meta, mate_meta, own_values, mate_values],
        smem=3,
    )


def gathered_sums(dense, columns, first, sources, start=None):
    rows_dev, hidden = sources[0].shape
    last = 2 * rows_dev

    def kernel(dense_ref, *refs):
        refs, out_ref = list(refs[:-1]), refs[-1]
        total = refs.pop(0)[first:last] if start is not None else jnp.zeros((last - first, hidden), F32)
        for column, ref in zip(columns, refs):
            part = dense_ref[first:last, column * rows_dev : (column + 1) * rows_dev]
            total = total + jnp.dot(part, ref[...], preferred_element_type=F32)
        out_ref[...] = total

    return call(
        kernel,
        [((last - first, hidden), F32)],
        [dense, *([] if start is None else [start]), *sources],
        flops=2 * (last - first) * rows_dev * hidden * len(sources),
    )[0]


def layer(spot, own_sum, mate_sum, weight, bias, grad_out, pieces):
    rows_dev, hidden = mate_sum.shape
    piece = hidden // pieces
    half = (pieces // 2, piece + BIAS_ROWS, hidden)

    def kernel(spot_ref, own_ref, mate_ref, weight_ref, bias_ref, grad_out_ref, out_ref, ga_ref, keep_ref, give_ref):
        agg = (own_ref[:rows_dev] + mate_ref[...]).astype(BF16)
        pre = jnp.dot(agg, weight_ref[...], preferred_element_type=F32) + bias_ref[...]
        sig = jax.nn.sigmoid(pre)
        out_ref[...] = (pre * sig).astype(BF16)
        grad_pre = (grad_out_ref[...].astype(F32) * sig * (1.0 + pre * (1.0 - sig))).astype(BF16)
        ga_ref[...] = lax.dot_general(
            grad_pre, weight_ref[...], (((1,), (1,)), ((), ())), preferred_element_type=F32
        ).astype(BF16)
        bias_term = jnp.sum(grad_pre.astype(F32), axis=0, keepdims=True)
        bias_rows = jnp.broadcast_to(bias_term, (BIAS_ROWS, hidden))
        terms = lax.dot_general(agg, grad_pre, (((0,), (0,)), ((), ())), preferred_element_type=F32)
        low, high = terms[: hidden // 2], terms[hidden // 2 :]
        even = spot_ref[0] % 2 == 0
        for ref, value in ((keep_ref, jnp.where(even, low, high)), (give_ref, jnp.where(even, high, low))):
            for q in range(pieces // 2):
                ref[q, :piece] = value[q * piece : (q + 1) * piece].astype(ref.dtype)
                ref[q, piece:] = bias_rows.astype(ref.dtype)

    shape = (rows_dev, hidden)
    return call(
        kernel,
        [(shape, BF16), (shape, BF16), (half, F32), (half, BF16)],
        [spot, own_sum, mate_sum, weight, bias.reshape(1, hidden), grad_out],
        flops=6 * rows_dev * hidden * hidden,
        smem=1,
    )


def folded(spot, keep, got, last=False):
    count, rows, hidden = keep.shape
    left = count // 2

    def kernel(spot_ref, keep_ref, got_ref, *out_refs):
        odd = spot_ref[0] % 2
        first_side, second_side = (spot_ref[0] >> 1) % 2, (spot_ref[0] >> 2) % 2
        mine = odd * second_side + (1 - odd) * first_side if last else odd * first_side + (1 - odd) * second_side
        for p in range(left):
            for ref, side in zip(out_refs, (mine, 1 - mine)):
                q = side if last else odd * (2 * p + side) + (1 - odd) * (2 * side + p)
                ref[p] = (keep_ref[q] + got_ref[q].astype(F32)).astype(ref.dtype)

    shape = (left, rows, hidden)
    return call(kernel, [(shape, F32), (shape, BF16)], [spot, keep, got], smem=1)


def rounded_sum(keep, got):
    def kernel(keep_ref, got_ref, out_ref):
        out_ref[...] = (keep_ref[0] + got_ref[0].astype(F32)).astype(BF16)

    return call(kernel, [(keep.shape[1:], BF16)], [keep, got])[0]


def summed_terms(spot, terms, masks=None):
    masks = masks or [None] * len(terms)

    def kernel(spot_ref, *refs):
        total = None
        for ref, mask in zip(refs, masks):
            value = ref[...].astype(F32)
            if mask is not None:
                value = jnp.where((mask >> spot_ref[0]) % 2 == 1, value, 0.0)
            total = value if total is None else total + value
        refs[-1][...] = total.astype(BF16)

    return call(kernel, [(terms[0].shape, BF16)], [spot, *terms], smem=1)[0]


def joined_pieces(spot, mine, other, last=False):
    rows, hidden = mine.shape[-2:]

    def kernel(spot_ref, mine_ref, other_ref, out_ref):
        odd = spot_ref[0] % 2
        first_side, second_side = (spot_ref[0] >> 1) % 2, (spot_ref[0] >> 2) % 2
        own = odd * first_side + (1 - odd) * second_side if last else odd * second_side + (1 - odd) * first_side
        for ref, side in ((mine_ref, own), (other_ref, 1 - own)):
            if not last:
                out_ref[side] = ref[...]
                continue
            for p in range(2):
                q = odd * (2 * p + side) + (1 - odd) * (2 * side + p)
                out_ref[pl.ds(pl.multiple_of(q * rows, rows), rows)] = ref[p]

    shape = (4 * rows, hidden) if last else (2, rows, hidden)
    return call(kernel, [(shape, BF16)], [spot, mine, other], smem=1)[0]


def whole_weight(spot, mine, other):
    rows, hidden = mine.shape

    def kernel(spot_ref, mine_ref, other_ref, out_ref):
        core = spot_ref[0] % 2
        out_ref[pl.ds(pl.multiple_of(core * rows, rows), rows)] = mine_ref[...].astype(F32)
        out_ref[pl.ds(pl.multiple_of((1 - core) * rows, rows), rows)] = other_ref[...].astype(F32)

    return call(kernel, [((2 * rows, hidden), F32)], [spot, mine, other], smem=1)[0]


def finished(mine, other, piece):
    hidden = mine.shape[1]

    def kernel(mine_ref, other_ref, weight_ref, bias_ref):
        total = mine_ref[...].astype(F32) + other_ref[...].astype(F32)
        weight_ref[...] = total[:piece].astype(BF16)
        bias_ref[...] = total[piece : piece + 8]

    return call(kernel, [((piece, hidden), BF16), ((8, hidden), F32)], [mine, other])


def scattered_sums(flipped, own, mate, columns, dtypes, spot=None, lookup=None):
    rows_dev, hidden = own.shape
    extra = [] if lookup is None else [spot, jnp.asarray(lookup, jnp.int32).reshape(-1)]

    def kernel(*refs):
        refs = list(refs)
        picks = [refs.pop(0) for _ in extra]
        flipped_ref, own_ref, mate_ref, *out_refs = refs
        for column, kinds in zip(columns, dtypes):
            if picks:
                column = picks[1][picks[0][0] * len(lookup[0]) + column]
                part = pl.ds(pl.multiple_of(column * rows_dev, rows_dev), rows_dev)
            else:
                part = pl.ds(column * rows_dev, rows_dev)
            total = jnp.dot(flipped_ref[part, :rows_dev], own_ref[...], preferred_element_type=F32)
            total += jnp.dot(flipped_ref[part, rows_dev:], mate_ref[...], preferred_element_type=F32)
            for kind in kinds:
                out_refs.pop(0)[...] = total.astype(kind)

    return call(
        kernel,
        [((rows_dev, hidden), kind) for kinds in dtypes for kind in kinds],
        [*extra, flipped, own, mate],
        flops=4 * rows_dev * rows_dev * hidden * len(columns),
        smem=len(extra),
    )


def after(value, *others):
    return lax.optimization_barrier((value, *others))


class Direct:
    def __init__(self, count, reach, spot):
        self.count, self.reach, self.positions, self.spot = count, reach, 2 * reach + 1, spot

    def sent(self, value, chips, kept=lambda s: True):
        pairs = [(s, (s + 2 * chips) % self.count) for s in range(self.count) if kept(s)]
        return lax.ppermute(value, "blk", pairs)

    def gather(self, features):
        last = self.positions - 1
        self.sources = [
            features
            if m == self.reach
            else self.sent(features, self.reach - m, lambda s: m < last or s % 2 == 0)
            for m in range(self.positions)
        ]

    def sums(self, dense, rows_dev):
        last = self.positions - 1
        start = gathered_sums(dense, range(last), 0, self.sources[:last])
        return gathered_sums(dense, [last], rows_dev, self.sources[last:], start), start

    def scatter(self, flipped, own, mate):
        self.flipped, self.own, self.mate = flipped, own, mate

    def step(self, k, token):
        if k != 1:
            return []
        _, mate = after(token, self.mate)
        kinds = [[F32 if m == self.reach else BF16] for m in range(self.positions)]
        terms = scattered_sums(self.flipped, self.own, mate, range(self.positions), kinds)
        last = self.positions - 1
        self.arriving = [
            term if m == self.reach else self.sent(term, m - self.reach, lambda s: m < last or s % 2 == 0)
            for m, term in enumerate(terms)
        ]
        return terms[:1]

    def finish(self):
        return summed_terms(self.spot, self.arriving)


class Relayed(Direct):
    EVEN, MIDDLE, ENDS, ODD_LOW = 0b01010101, 0b00111100, 0b11000011, 0b00001010
    LOOKUP = [
        [2, 4, 3, 0, 1], [2, 3, 4, 0, 1],
        [2, 4, 1, 0, 3], [2, 1, 4, 0, 3],
        [2, 0, 3, 4, 1], [2, 3, 0, 4, 1],
        [2, 0, 1, 4, 3], [2, 1, 0, 4, 3],
    ]

    def routed(self, value, steps):
        pairs = [(s, (s + steps[s % 8]) % self.count) for s in range(self.count) if s % 8 in steps]
        return lax.ppermute(value, "blk", pairs)

    def step(self, k, token):
        x = {spot: (spot ^ 2) - spot for spot in range(8)}
        y = {spot: (spot ^ 4) - spot for spot in range(8)}
        straight = {spot: (y if spot % 2 else x)[spot] for spot in range(8)}
        across = {spot: (x if spot % 2 else y)[spot] for spot in range(8)}
        take = lambda mate, *args: scattered_sums(self.flipped, self.own, mate, *args, self.spot, self.LOOKUP)
        if k == 0:
            _, mate = after(token, self.mate)
            to_last, self.to_plane, self.plane_rest = take(mate, (4, 3), [[BF16], [BF16, F32]])
            self.from_last = self.routed(to_last, straight)
            return [to_last]
        if k == 1:
            _, mate = after(token, self.mate)
            self.kept, self.to_across, self.to_straight = take(mate, (0, 1, 2), [[F32]] * 3)
            return [self.kept]
        if k == 2:
            _, to_plane = after(token, self.to_plane)
            self.from_plane = self.routed(to_plane, {1: -8, 3: -8})
            return [self.from_last]
        if k == 3:
            _, rest = after(token, self.plane_rest)
            out = summed_terms(self.spot, [rest, self.from_last], [self.EVEN, self.MIDDLE])
            self.from_planes = self.routed(out, {0: -8, 2: -8, 4: 8, 6: 8, 5: -8, 3: 8})
            second = summed_terms(self.spot, [self.to_straight, self.from_plane], [None, self.ODD_LOW])
            self.second = self.routed(second, straight)
            return [out, second]
        if k == 4:
            _, rest = after(token, self.to_across)
            out = summed_terms(
                self.spot,
                [rest, self.from_planes, self.from_last],
                [None, self.EVEN | 0b00101000, self.ENDS],
            )
            self.arriving = [self.kept, self.second, self.routed(out, across)]
            return [out]
        return []


def local(features, tile_list, tile_count, tile_values, weight, bias, grad_out):
    count = lax.axis_size("blk")
    me = lax.axis_index("blk")
    window = tile_values.shape[1]
    reach = window // 4
    rows_dev, hidden = features.shape
    pieces = 8
    spot = (me % pieces).astype(jnp.int32).reshape(1)
    route = (Relayed if reach == 2 else Direct)(count, reach, spot)

    def swapped(value, distance):
        return lax.ppermute(value, "blk", [(s, s ^ distance) for s in range(count)])

    route.gather(features)
    mate_values, tile_list, tile_count = after(swapped(tile_values[0], 1), tile_list, tile_count)
    meta = jnp.concatenate([tile_list[0].reshape(window, -1), tile_count[0][:, None]], axis=1).reshape(-1)
    mate_meta = swapped(meta, 1)
    dense, flipped = dense_tiles(spot, meta, mate_meta, tile_values[0], mate_values, rows_dev, route.positions)
    mate_sum, own_sum = route.sums(dense, rows_dev)
    output, grad_agg, keep, give = layer(spot, own_sum, swapped(mate_sum, 1), weight, bias, grad_out, pieces)

    mate_grad, got = swapped(grad_agg, 1), swapped(give, 1)
    route.scatter(flipped, grad_agg, mate_grad)

    def exchanged(k, value, even, odd):
        pairs = [(s, s ^ (odd if s % 2 else even)) for s in range(count)]
        other = lax.ppermute(value, "blk", pairs)
        return after(other, *route.step(k, value))[0]

    keep, give = folded(spot, keep, got)
    keep, give = folded(spot, keep, exchanged(0, give, 4, 2), last=True)
    total = rounded_sum(keep, exchanged(1, give, 2, 4))
    step, k = pieces, 2
    while step < count:
        other = exchanged(k, total, step, step)
        step, k = 2 * step, k + 1
        if step < count:
            total = summed_terms(spot, [total, other])
        else:
            total, bias_sum = finished(total, other, hidden // pieces)
    pair = joined_pieces(spot, total, exchanged(4, total, 2, 4))
    half = joined_pieces(spot, pair, exchanged(5, pair, 4, 2), last=True)
    grad_features = route.finish()
    mate_half, grad_features = after(swapped(half, 1), grad_features)
    return (output, grad_features, whole_weight(spot, half, mate_half), bias_sum[0])


def solution(mesh):
    placed = (
        P("blk", None),
        P("blk", None, None, None),
        P("blk", None),
        P("blk", None, None, None, None),
        P(),
        P(),
        P("blk", None),
    )
    return jax.shard_map(
        local,
        mesh=mesh,
        in_specs=placed,
        out_specs=(P("blk", None), P("blk", None), P(), P()),
        check_vma=False,
    )
```

```python
import jax
import jax.numpy as jnp
from jax import lax
from jax.experimental import pallas as pl
from jax.experimental.pallas import tpu as pltpu
from jax.sharding import PartitionSpec as P

BF16, F32 = jnp.bfloat16, jnp.float32
BIAS_ROWS = 16


def call(kernel, outs, ins, flops=0, smem=0):
    spec = lambda k: pl.BlockSpec(memory_space=pltpu.SMEM if k < smem else pltpu.VMEM)
    out_shape = [jax.ShapeDtypeStruct(s, d) for s, d in outs]
    moved = sum(a.size * a.dtype.itemsize for a in list(ins) + out_shape)
    return pl.pallas_call(
        kernel,
        out_shape=out_shape,
        in_specs=[spec(k) for k in range(len(ins))],
        out_specs=[pl.BlockSpec(memory_space=pltpu.VMEM)] * len(outs),
        compiler_params=pltpu.CompilerParams(vmem_limit_bytes=moved + moved // 4 + 4 * 1024 * 1024),
        cost_estimate=pl.CostEstimate(flops=0, bytes_accessed=0, transcendentals=0),
    )(*ins)


def dense_tiles(spot, own_meta, mate_meta, own_values, mate_values, rows_dev, positions):
    window, slots, tile, _ = own_values.shape
    tile_rows = rows_dev // tile

    def kernel(spot_ref, own_meta_ref, mate_meta_ref, own_ref, mate_ref, dense_ref, flipped_ref):
        dense_ref[...] = jnp.zeros_like(dense_ref)
        flipped_ref[...] = jnp.zeros_like(flipped_ref)

        def place(meta_ref, values_ref, first_j, shift, first_row):
            def slot(t, _):
                i, k = t // slots, t % slots
                j = 2 * i + first_j
                base = j * (2 * slots + 1)

                @pl.when(k < meta_ref[base + 2 * slots])
                def _():
                    row = pl.multiple_of((meta_ref[base + 2 * k] + first_row) * tile, tile)
                    col = pl.multiple_of(((i + shift) * tile_rows + meta_ref[base + 2 * k + 1]) * tile, tile)
                    values = values_ref[j, k]
                    dense_ref[pl.ds(row, tile), pl.ds(col, tile)] = values
                    flipped_ref[pl.ds(col, tile), pl.ds(row, tile)] = values.T

                return 0

            lax.fori_loop(0, (window // 2) * slots, slot, 0)

        place(own_meta_ref, own_ref, 0, 0, 0)
        place(mate_meta_ref, mate_ref, 1, 1 - spot_ref[0] % 2, tile_rows)

    wide = positions * rows_dev
    return call(
        kernel,
        [((2 * rows_dev, wide), BF16), ((wide, 2 * rows_dev), BF16)],
        [spot, own_meta, mate_meta, own_values, mate_values],
        smem=3,
    )


def gathered_sums(dense, columns, first, sources, start=None):
    rows_dev, hidden = sources[0].shape
    last = 2 * rows_dev

    def kernel(dense_ref, *refs):
        refs, out_ref = list(refs[:-1]), refs[-1]
        total = refs.pop(0)[first:last] if start is not None else jnp.zeros((last - first, hidden), F32)
        for column, ref in zip(columns, refs):
            part = dense_ref[first:last, column * rows_dev : (column + 1) * rows_dev]
            total = total + jnp.dot(part, ref[...], preferred_element_type=F32)
        out_ref[...] = total

    return call(
        kernel,
        [((last - first, hidden), F32)],
        [dense, *([] if start is None else [start]), *sources],
        flops=2 * (last - first) * rows_dev * hidden * len(sources),
    )[0]


def layer(spot, own_sum, mate_sum, weight, bias, grad_out, pieces):
    rows_dev, hidden = mate_sum.shape
    piece = hidden // pieces
    half = (pieces // 2, piece + BIAS_ROWS, hidden)

    def kernel(spot_ref, own_ref, mate_ref, weight_ref, bias_ref, grad_out_ref, out_ref, ga_ref, keep_ref, give_ref):
        agg = (own_ref[:rows_dev] + mate_ref[...]).astype(BF16)
        pre = jnp.dot(agg, weight_ref[...], preferred_element_type=F32) + bias_ref[...]
        sig = jax.nn.sigmoid(pre)
        out_ref[...] = (pre * sig).astype(BF16)
        grad_pre = (grad_out_ref[...].astype(F32) * sig * (1.0 + pre * (1.0 - sig))).astype(BF16)
        ga_ref[...] = lax.dot_general(
            grad_pre, weight_ref[...], (((1,), (1,)), ((), ())), preferred_element_type=F32
        ).astype(BF16)
        bias_term = jnp.sum(grad_pre.astype(F32), axis=0, keepdims=True)
        bias_rows = jnp.broadcast_to(bias_term, (BIAS_ROWS, hidden))
        terms = lax.dot_general(agg, grad_pre, (((0,), (0,)), ((), ())), preferred_element_type=F32)
        low, high = terms[: hidden // 2], terms[hidden // 2 :]
        even = spot_ref[0] % 2 == 0
        for ref, value in ((keep_ref, jnp.where(even, low, high)), (give_ref, jnp.where(even, high, low))):
            for q in range(pieces // 2):
                ref[q, :piece] = value[q * piece : (q + 1) * piece].astype(ref.dtype)
                ref[q, piece:] = bias_rows.astype(ref.dtype)

    shape = (rows_dev, hidden)
    return call(
        kernel,
        [(shape, BF16), (shape, BF16), (half, F32), (half, BF16)],
        [spot, own_sum, mate_sum, weight, bias.reshape(1, hidden), grad_out],
        flops=6 * rows_dev * hidden * hidden,
        smem=1,
    )


def folded(spot, keep, got, last=False):
    count, rows, hidden = keep.shape
    left = count // 2

    def kernel(spot_ref, keep_ref, got_ref, *out_refs):
        odd = spot_ref[0] % 2
        first_side, second_side = (spot_ref[0] >> 1) % 2, (spot_ref[0] >> 2) % 2
        mine = odd * second_side + (1 - odd) * first_side if last else odd * first_side + (1 - odd) * second_side
        for p in range(left):
            for ref, side in zip(out_refs, (mine, 1 - mine)):
                q = side if last else odd * (2 * p + side) + (1 - odd) * (2 * side + p)
                ref[p] = (keep_ref[q] + got_ref[q].astype(F32)).astype(ref.dtype)

    shape = (left, rows, hidden)
    return call(kernel, [(shape, F32), (shape, BF16)], [spot, keep, got], smem=1)


def rounded_sum(keep, got):
    def kernel(keep_ref, got_ref, out_ref):
        out_ref[...] = (keep_ref[0] + got_ref[0].astype(F32)).astype(BF16)

    return call(kernel, [(keep.shape[1:], BF16)], [keep, got])[0]


def summed_terms(spot, terms, masks=None):
    masks = masks or [None] * len(terms)

    def kernel(spot_ref, *refs):
        total = None
        for ref, mask in zip(refs, masks):
            value = ref[...].astype(F32)
            if mask is not None:
                value = jnp.where((mask >> spot_ref[0]) % 2 == 1, value, 0.0)
            total = value if total is None else total + value
        refs[-1][...] = total.astype(BF16)

    return call(kernel, [(terms[0].shape, BF16)], [spot, *terms], smem=1)[0]


def joined_pieces(spot, mine, other, last=False):
    rows, hidden = mine.shape[-2:]

    def kernel(spot_ref, mine_ref, other_ref, out_ref):
        odd = spot_ref[0] % 2
        first_side, second_side = (spot_ref[0] >> 1) % 2, (spot_ref[0] >> 2) % 2
        own = odd * first_side + (1 - odd) * second_side if last else odd * second_side + (1 - odd) * first_side
        for ref, side in ((mine_ref, own), (other_ref, 1 - own)):
            if not last:
                out_ref[side] = ref[...]
                continue
            for p in range(2):
                q = odd * (2 * p + side) + (1 - odd) * (2 * side + p)
                out_ref[pl.ds(pl.multiple_of(q * rows, rows), rows)] = ref[p]

    shape = (4 * rows, hidden) if last else (2, rows, hidden)
    return call(kernel, [(shape, BF16)], [spot, mine, other], smem=1)[0]


def whole_weight(spot, mine, other):
    rows, hidden = mine.shape

    def kernel(spot_ref, mine_ref, other_ref, out_ref):
        core = spot_ref[0] % 2
        out_ref[pl.ds(pl.multiple_of(core * rows, rows), rows)] = mine_ref[...].astype(F32)
        out_ref[pl.ds(pl.multiple_of((1 - core) * rows, rows), rows)] = other_ref[...].astype(F32)

    return call(kernel, [((2 * rows, hidden), F32)], [spot, mine, other], smem=1)[0]


def finished(mine, other, piece):
    hidden = mine.shape[1]

    def kernel(mine_ref, other_ref, weight_ref, bias_ref):
        total = mine_ref[...].astype(F32) + other_ref[...].astype(F32)
        weight_ref[...] = total[:piece].astype(BF16)
        bias_ref[...] = total[piece : piece + 8]

    return call(kernel, [((piece, hidden), BF16), ((8, hidden), F32)], [mine, other])


def scattered_sums(flipped, own, mate, columns, dtypes, spot=None, lookup=None):
    rows_dev, hidden = own.shape
    extra = [] if lookup is None else [spot, jnp.asarray(lookup, jnp.int32).reshape(-1)]

    def kernel(*refs):
        refs = list(refs)
        picks = [refs.pop(0) for _ in extra]
        flipped_ref, own_ref, mate_ref, *out_refs = refs
        for column, kinds in zip(columns, dtypes):
            if picks:
                column = picks[1][picks[0][0] * len(lookup[0]) + column]
                part = pl.ds(pl.multiple_of(column * rows_dev, rows_dev), rows_dev)
            else:
                part = pl.ds(column * rows_dev, rows_dev)
            total = jnp.dot(flipped_ref[part, :rows_dev], own_ref[...], preferred_element_type=F32)
            total += jnp.dot(flipped_ref[part, rows_dev:], mate_ref[...], preferred_element_type=F32)
            for kind in kinds:
                out_refs.pop(0)[...] = total.astype(kind)

    return call(
        kernel,
        [((rows_dev, hidden), kind) for kinds in dtypes for kind in kinds],
        [*extra, flipped, own, mate],
        flops=4 * rows_dev * rows_dev * hidden * len(columns),
        smem=len(extra),
    )


def after(value, *others):
    return lax.optimization_barrier((value, *others))


class Direct:
    def __init__(self, count, reach, spot):
        self.count, self.reach, self.positions, self.spot = count, reach, 2 * reach + 1, spot

    def sent(self, value, chips, kept=lambda s: True):
        pairs = [(s, (s + 2 * chips) % self.count) for s in range(self.count) if kept(s)]
        return lax.ppermute(value, "blk", pairs)

    def gather(self, features):
        last = self.positions - 1
        self.sources = [
            features
            if m == self.reach
            else self.sent(features, self.reach - m, lambda s: m < last or s % 2 == 0)
            for m in range(self.positions)
        ]

    def sums(self, dense, rows_dev):
        last = self.positions - 1
        start = gathered_sums(dense, range(last), 0, self.sources[:last])
        return gathered_sums(dense, [last], rows_dev, self.sources[last:], start), start

    def scatter(self, flipped, own, mate):
        self.flipped, self.own, self.mate = flipped, own, mate

    def step(self, k, token):
        if k != 1:
            return []
        _, mate = after(token, self.mate)
        kinds = [[F32 if m == self.reach else BF16] for m in range(self.positions)]
        terms = scattered_sums(self.flipped, self.own, mate, range(self.positions), kinds)
        last = self.positions - 1
        self.arriving = [
            term if m == self.reach else self.sent(term, m - self.reach, lambda s: m < last or s % 2 == 0)
            for m, term in enumerate(terms)
        ]
        return terms[:1]

    def finish(self):
        return summed_terms(self.spot, self.arriving)


class Relayed(Direct):
    EVEN, MIDDLE, ENDS, ODD_LOW = 0b01010101, 0b00111100, 0b11000011, 0b00001010
    LOOKUP = [
        [2, 4, 3, 0, 1], [2, 3, 4, 0, 1],
        [2, 4, 1, 0, 3], [2, 1, 4, 0, 3],
        [2, 0, 3, 4, 1], [2, 3, 0, 4, 1],
        [2, 0, 1, 4, 3], [2, 1, 0, 4, 3],
    ]

    def routed(self, value, steps):
        pairs = [(s, (s + steps[s % 8]) % self.count) for s in range(self.count) if s % 8 in steps]
        return lax.ppermute(value, "blk", pairs)

    def step(self, k, token):
        x = {spot: (spot ^ 2) - spot for spot in range(8)}
        y = {spot: (spot ^ 4) - spot for spot in range(8)}
        straight = {spot: (y if spot % 2 else x)[spot] for spot in range(8)}
        across = {spot: (x if spot % 2 else y)[spot] for spot in range(8)}
        take = lambda mate, *args: scattered_sums(self.flipped, self.own, mate, *args, self.spot, self.LOOKUP)
        if k == 0:
            _, mate = after(token, self.mate)
            self.to_last, self.to_plane, self.plane_rest = take(mate, (4, 3), [[BF16], [BF16, F32]])
            self.kept, self.to_across, self.to_straight = take(mate, (0, 1, 2), [[F32]] * 3)
            return [self.to_last, self.kept]
        if k == 2:
            _, to_last, to_plane = after(token, self.to_last, self.to_plane)
            self.from_last = self.routed(to_last, straight)
            self.from_plane = self.routed(to_plane, {1: -8, 3: -8})
        if k == 4:
            _, rest, plane_rest = after(token, self.to_straight, self.plane_rest)
            out = summed_terms(self.spot, [plane_rest, self.from_last], [self.EVEN, self.MIDDLE])
            self.from_planes = self.routed(out, {0: -8, 2: -8, 4: 8, 6: 8, 5: -8, 3: 8})
            second = summed_terms(self.spot, [rest, self.from_plane], [None, self.ODD_LOW])
            self.second = self.routed(second, straight)
            return [second]
        if k == 5:
            _, rest = after(token, self.to_across)
            out = summed_terms(
                self.spot,
                [rest, self.from_planes, self.from_last],
                [None, self.EVEN | 0b00101000, self.ENDS],
            )
            self.arriving = [self.kept, self.second, self.routed(out, across)]
            return [out]
        return []


def local(features, tile_list, tile_count, tile_values, weight, bias, grad_out):
    count = lax.axis_size("blk")
    me = lax.axis_index("blk")
    window = tile_values.shape[1]
    reach = window // 4
    rows_dev, hidden = features.shape
    pieces = 8
    spot = (me % pieces).astype(jnp.int32).reshape(1)
    route = (Relayed if reach == 2 else Direct)(count, reach, spot)

    def swapped(value, distance):
        return lax.ppermute(value, "blk", [(s, s ^ distance) for s in range(count)])

    route.gather(features)
    mate_values, tile_list, tile_count = after(swapped(tile_values[0], 1), tile_list, tile_count)
    meta = jnp.concatenate([tile_list[0].reshape(window, -1), tile_count[0][:, None]], axis=1).reshape(-1)
    mate_meta = swapped(meta, 1)
    dense, flipped = dense_tiles(spot, meta, mate_meta, tile_values[0], mate_values, rows_dev, route.positions)
    mate_sum, own_sum = route.sums(dense, rows_dev)
    output, grad_agg, keep, give = layer(spot, own_sum, swapped(mate_sum, 1), weight, bias, grad_out, pieces)

    mate_grad, got = swapped(grad_agg, 1), swapped(give, 1)
    route.scatter(flipped, grad_agg, mate_grad)

    def exchanged(k, value, even, odd):
        pairs = [(s, s ^ (odd if s % 2 else even)) for s in range(count)]
        other = lax.ppermute(value, "blk", pairs)
        return after(other, *route.step(k, value))[0]

    keep, give = folded(spot, keep, got)
    keep, give = folded(spot, keep, exchanged(0, give, 4, 2), last=True)
    total = rounded_sum(keep, exchanged(1, give, 2, 4))
    step, k = pieces, 2
    while step < count:
        other = exchanged(k, total, step, step)
        step, k = 2 * step, k + 1
        if step < count:
            total = summed_terms(spot, [total, other])
        else:
            total, bias_sum = finished(total, other, hidden // pieces)
    pair = joined_pieces(spot, total, exchanged(4, total, 2, 4))
    half = joined_pieces(spot, pair, exchanged(5, pair, 4, 2), last=True)
    grad_features = route.finish()
    mate_half, grad_features = after(swapped(half, 1), grad_features)
    return (output, grad_features, whole_weight(spot, half, mate_half), bias_sum[0])


def solution(mesh):
    placed = (
        P("blk", None),
        P("blk", None, None, None),
        P("blk", None),
        P("blk", None, None, None, None),
        P(),
        P(),
        P("blk", None),
    )
    return jax.shard_map(
        local,
        mesh=mesh,
        in_specs=placed,
        out_specs=(P("blk", None), P("blk", None), P(), P()),
        check_vma=False,
    )
```

```python
import jax
import jax.numpy as jnp
from jax import lax
from jax.experimental import pallas as pl
from jax.experimental.pallas import tpu as pltpu
from jax.sharding import PartitionSpec as P

BF16, F32 = jnp.bfloat16, jnp.float32
BIAS_ROWS = 16


def call(kernel, outs, ins, flops=0, smem=0):
    spec = lambda k: pl.BlockSpec(memory_space=pltpu.SMEM if k < smem else pltpu.VMEM)
    out_shape = [jax.ShapeDtypeStruct(s, d) for s, d in outs]
    moved = sum(a.size * a.dtype.itemsize for a in list(ins) + out_shape)
    return pl.pallas_call(
        kernel,
        out_shape=out_shape,
        in_specs=[spec(k) for k in range(len(ins))],
        out_specs=[pl.BlockSpec(memory_space=pltpu.VMEM)] * len(outs),
        compiler_params=pltpu.CompilerParams(vmem_limit_bytes=moved + moved // 4 + 4 * 1024 * 1024),
        cost_estimate=pl.CostEstimate(flops=0, bytes_accessed=0, transcendentals=0),
    )(*ins)


def dense_tiles(spot, own_meta, mate_meta, own_values, mate_values, rows_dev, positions):
    window, slots, tile, _ = own_values.shape
    tile_rows = rows_dev // tile

    def kernel(spot_ref, own_meta_ref, mate_meta_ref, own_ref, mate_ref, dense_ref, flipped_ref):
        dense_ref[...] = jnp.zeros_like(dense_ref)
        flipped_ref[...] = jnp.zeros_like(flipped_ref)

        def place(meta_ref, values_ref, first_j, shift, first_row):
            def slot(t, _):
                i, k = t // slots, t % slots
                j = 2 * i + first_j
                base = j * (2 * slots + 1)

                @pl.when(k < meta_ref[base + 2 * slots])
                def _():
                    row = pl.multiple_of((meta_ref[base + 2 * k] + first_row) * tile, tile)
                    col = pl.multiple_of(((i + shift) * tile_rows + meta_ref[base + 2 * k + 1]) * tile, tile)
                    values = values_ref[j, k]
                    dense_ref[pl.ds(row, tile), pl.ds(col, tile)] = values
                    flipped_ref[pl.ds(col, tile), pl.ds(row, tile)] = values.T

                return 0

            lax.fori_loop(0, (window // 2) * slots, slot, 0)

        place(own_meta_ref, own_ref, 0, 0, 0)
        place(mate_meta_ref, mate_ref, 1, 1 - spot_ref[0] % 2, tile_rows)

    wide = positions * rows_dev
    return call(
        kernel,
        [((2 * rows_dev, wide), BF16), ((wide, 2 * rows_dev), BF16)],
        [spot, own_meta, mate_meta, own_values, mate_values],
        smem=3,
    )


def gathered_sums(dense, columns, first, sources, start=None):
    rows_dev, hidden = sources[0].shape
    last = 2 * rows_dev

    def kernel(dense_ref, *refs):
        refs, out_ref = list(refs[:-1]), refs[-1]
        total = refs.pop(0)[first:last] if start is not None else jnp.zeros((last - first, hidden), F32)
        for column, ref in zip(columns, refs):
            part = dense_ref[first:last, column * rows_dev : (column + 1) * rows_dev]
            total = total + jnp.dot(part, ref[...], preferred_element_type=F32)
        out_ref[...] = total

    return call(
        kernel,
        [((last - first, hidden), F32)],
        [dense, *([] if start is None else [start]), *sources],
        flops=2 * (last - first) * rows_dev * hidden * len(sources),
    )[0]


def layer(spot, own_sum, mate_sum, weight, bias, grad_out, pieces):
    rows_dev, hidden = mate_sum.shape
    piece = hidden // pieces
    half = (pieces // 2, piece + BIAS_ROWS, hidden)

    def kernel(spot_ref, own_ref, mate_ref, weight_ref, bias_ref, grad_out_ref, out_ref, ga_ref, keep_ref, give_ref):
        agg = (own_ref[:rows_dev] + mate_ref[...]).astype(BF16)
        pre = jnp.dot(agg, weight_ref[...], preferred_element_type=F32) + bias_ref[...]
        sig = jax.nn.sigmoid(pre)
        out_ref[...] = (pre * sig).astype(BF16)
        grad_pre = (grad_out_ref[...].astype(F32) * sig * (1.0 + pre * (1.0 - sig))).astype(BF16)
        ga_ref[...] = lax.dot_general(
            grad_pre, weight_ref[...], (((1,), (1,)), ((), ())), preferred_element_type=F32
        ).astype(BF16)
        bias_term = jnp.sum(grad_pre.astype(F32), axis=0, keepdims=True)
        bias_rows = jnp.broadcast_to(bias_term, (BIAS_ROWS, hidden))
        terms = lax.dot_general(agg, grad_pre, (((0,), (0,)), ((), ())), preferred_element_type=F32)
        low, high = terms[: hidden // 2], terms[hidden // 2 :]
        even = spot_ref[0] % 2 == 0
        for ref, value in ((keep_ref, jnp.where(even, low, high)), (give_ref, jnp.where(even, high, low))):
            for q in range(pieces // 2):
                ref[q, :piece] = value[q * piece : (q + 1) * piece].astype(ref.dtype)
                ref[q, piece:] = bias_rows.astype(ref.dtype)

    shape = (rows_dev, hidden)
    return call(
        kernel,
        [(shape, BF16), (shape, BF16), (half, F32), (half, BF16)],
        [spot, own_sum, mate_sum, weight, bias.reshape(1, hidden), grad_out],
        flops=6 * rows_dev * hidden * hidden,
        smem=1,
    )


def folded(spot, keep, got):
    count, rows, hidden = keep.shape

    def kernel(spot_ref, keep_ref, got_ref, own_ref, *out_refs):
        for other in range(count):
            q = (spot_ref[0] >> 1) ^ other
            value = keep_ref[q] + got_ref[q].astype(F32)
            if other == 0:
                own_ref[...] = value
            else:
                out_refs[other - 1][...] = value.astype(BF16)

    shape = (rows, hidden)
    return call(kernel, [(shape, F32)] + [(shape, BF16)] * (count - 1), [spot, keep, got], smem=1)


def summed_terms(spot, terms, masks=None):
    masks = masks or [None] * len(terms)

    def kernel(spot_ref, *refs):
        total = None
        for ref, mask in zip(refs, masks):
            value = ref[...].astype(F32)
            if mask is not None:
                value = jnp.where((mask >> spot_ref[0]) % 2 == 1, value, 0.0)
            total = value if total is None else total + value
        refs[-1][...] = total.astype(BF16)

    return call(kernel, [(terms[0].shape, BF16)], [spot, *terms], smem=1)[0]


def joined_pieces(spot, pieces):
    rows, hidden = pieces[0].shape
    count = len(pieces)

    def kernel(spot_ref, *refs):
        for other, ref in enumerate(refs[:-1]):
            q = (spot_ref[0] >> 1) ^ other
            refs[-1][pl.ds(pl.multiple_of(q * rows, rows), rows)] = ref[...]

    return call(kernel, [((count * rows, hidden), BF16)], [spot, *pieces], smem=1)[0]


def whole_weight(spot, mine, other):
    rows, hidden = mine.shape

    def kernel(spot_ref, mine_ref, other_ref, out_ref):
        core = spot_ref[0] % 2
        out_ref[pl.ds(pl.multiple_of(core * rows, rows), rows)] = mine_ref[...].astype(F32)
        out_ref[pl.ds(pl.multiple_of((1 - core) * rows, rows), rows)] = other_ref[...].astype(F32)

    return call(kernel, [((2 * rows, hidden), F32)], [spot, mine, other], smem=1)[0]


def finished(values, piece):
    hidden = values[0].shape[1]

    def kernel(*refs):
        parts = [ref[...].astype(F32) for ref in refs[:-2]]
        while len(parts) > 1:
            parts = [parts[k] + parts[k + 1] for k in range(0, len(parts), 2)]
        refs[-2][...] = parts[0][:piece].astype(BF16)
        refs[-1][...] = parts[0][piece:]

    rows = values[0].shape[0]
    return call(kernel, [((piece, hidden), BF16), ((rows - piece, hidden), F32)], list(values))


def scattered_sums(flipped, own, mate, columns, dtypes, spot=None, lookup=None):
    rows_dev, hidden = own.shape
    extra = [] if lookup is None else [spot, jnp.asarray(lookup, jnp.int32).reshape(-1)]

    def kernel(*refs):
        refs = list(refs)
        picks = [refs.pop(0) for _ in extra]
        flipped_ref, own_ref, mate_ref, *out_refs = refs
        for column, kinds in zip(columns, dtypes):
            if picks:
                column = picks[1][picks[0][0] * len(lookup[0]) + column]
                part = pl.ds(pl.multiple_of(column * rows_dev, rows_dev), rows_dev)
            else:
                part = pl.ds(column * rows_dev, rows_dev)
            total = jnp.dot(flipped_ref[part, :rows_dev], own_ref[...], preferred_element_type=F32)
            total += jnp.dot(flipped_ref[part, rows_dev:], mate_ref[...], preferred_element_type=F32)
            for kind in kinds:
                out_refs.pop(0)[...] = total.astype(kind)

    return call(
        kernel,
        [((rows_dev, hidden), kind) for kinds in dtypes for kind in kinds],
        [*extra, flipped, own, mate],
        flops=4 * rows_dev * rows_dev * hidden * len(columns),
        smem=len(extra),
    )


def after(value, *others):
    return lax.optimization_barrier((value, *others))


class Direct:
    def __init__(self, count, reach, spot):
        self.count, self.reach, self.positions, self.spot = count, reach, 2 * reach + 1, spot

    def sent(self, value, chips, kept=lambda s: True):
        pairs = [(s, (s + 2 * chips) % self.count) for s in range(self.count) if kept(s)]
        return lax.ppermute(value, "blk", pairs)

    def gather(self, features):
        last = self.positions - 1
        self.sources = [
            features
            if m == self.reach
            else self.sent(features, self.reach - m, lambda s: m < last or s % 2 == 0)
            for m in range(self.positions)
        ]

    def sums(self, dense, rows_dev):
        last = self.positions - 1
        start = gathered_sums(dense, range(last), 0, self.sources[:last])
        return gathered_sums(dense, [last], rows_dev, self.sources[last:], start), start

    def scatter(self, flipped, own, mate):
        self.flipped, self.own, self.mate = flipped, own, mate

    def step(self, k, token):
        if k != 1:
            return []
        _, mate = after(token, self.mate)
        kinds = [[F32 if m == self.reach else BF16] for m in range(self.positions)]
        terms = scattered_sums(self.flipped, self.own, mate, range(self.positions), kinds)
        last = self.positions - 1
        self.arriving = [
            term if m == self.reach else self.sent(term, m - self.reach, lambda s: m < last or s % 2 == 0)
            for m, term in enumerate(terms)
        ]
        return terms[:1]

    def finish(self, token):
        return summed_terms(self.spot, self.arriving)


class Relayed(Direct):
    EVEN, MIDDLE, ENDS, ODD_LOW = 0b01010101, 0b00111100, 0b11000011, 0b00001010
    LOOKUP = [
        [2, 4, 3, 0, 1], [2, 3, 4, 0, 1],
        [2, 4, 1, 0, 3], [2, 1, 4, 0, 3],
        [2, 0, 3, 4, 1], [2, 3, 0, 4, 1],
        [2, 0, 1, 4, 3], [2, 1, 0, 4, 3],
    ]

    def routed(self, value, steps):
        pairs = [(s, (s + steps[s % 8]) % self.count) for s in range(self.count) if s % 8 in steps]
        return lax.ppermute(value, "blk", pairs)

    def step(self, k, token):
        x = {spot: (spot ^ 2) - spot for spot in range(8)}
        y = {spot: (spot ^ 4) - spot for spot in range(8)}
        straight = {spot: (y if spot % 2 else x)[spot] for spot in range(8)}
        self.across = {spot: (x if spot % 2 else y)[spot] for spot in range(8)}
        take = lambda mate, *args: scattered_sums(self.flipped, self.own, mate, *args, self.spot, self.LOOKUP)
        if k == 0:
            _, mate = after(token, self.mate)
            self.to_last, self.to_plane, self.plane_rest = take(mate, (4, 3), [[BF16], [BF16, F32]])
            self.kept, self.to_across, self.to_straight = take(mate, (0, 1, 2), [[F32]] * 3)
            self.from_plane = self.routed(self.to_plane, {1: -8, 3: -8})
            return [self.to_last, self.kept, self.from_plane]
        if k == 1:
            _, to_last, rest = after(token, self.to_last, self.to_straight)
            self.from_last = self.routed(to_last, straight)
            second = summed_terms(self.spot, [rest, self.from_plane], [None, self.ODD_LOW])
            self.second = self.routed(second, straight)
            return [second]
        if k == 2:
            _, plane_rest = after(token, self.plane_rest)
            out = summed_terms(self.spot, [plane_rest, self.from_last], [self.EVEN, self.MIDDLE])
            self.from_planes = self.routed(out, {0: -8, 2: -8, 4: 8, 6: 8, 5: -8, 3: 8})
        return []

    def finish(self, token):
        _, rest = after(token, self.to_across)
        out = summed_terms(
            self.spot, [rest, self.from_planes, self.from_last], [None, self.EVEN | 0b00101000, self.ENDS]
        )
        return summed_terms(self.spot, [self.kept, self.second, self.routed(out, self.across)])


def local(features, tile_list, tile_count, tile_values, weight, bias, grad_out):
    count = lax.axis_size("blk")
    me = lax.axis_index("blk")
    window = tile_values.shape[1]
    reach = window // 4
    rows_dev, hidden = features.shape
    pieces = 8
    spot = (me % pieces).astype(jnp.int32).reshape(1)
    route = (Relayed if reach == 2 else Direct)(count, reach, spot)

    def swapped(value, distance):
        return lax.ppermute(value, "blk", [(s, s ^ distance) for s in range(count)])

    route.gather(features)
    mate_values, tile_list, tile_count = after(swapped(tile_values[0], 1), tile_list, tile_count)
    meta = jnp.concatenate([tile_list[0].reshape(window, -1), tile_count[0][:, None]], axis=1).reshape(-1)
    mate_meta = swapped(meta, 1)
    dense, flipped = dense_tiles(spot, meta, mate_meta, tile_values[0], mate_values, rows_dev, route.positions)
    mate_sum, own_sum = route.sums(dense, rows_dev)
    output, grad_agg, keep, give = layer(spot, own_sum, swapped(mate_sum, 1), weight, bias, grad_out, pieces)

    mate_grad, got = swapped(grad_agg, 1), swapped(give, 1)
    route.scatter(flipped, grad_agg, mate_grad)

    def exchanged(k, values, distances):
        others = [swapped(value, distance) for value, distance in zip(values, distances)]
        return after(others, *route.step(k, values[0]))[0]

    in_plane = [2 * d for d in range(1, pieces // 2)]
    own, *give = folded(spot, keep, got)
    total = summed_terms(spot, [own, *exchanged(0, give, in_plane)])
    step, k = pieces, 1
    while step < count:
        group = min(4, count // step)
        across = [step * d for d in range(1, group)]
        values = [total, *exchanged(k, [total] * (group - 1), across)]
        step, k = step * group, k + 1
        if step < count:
            total = summed_terms(spot, values)
    total, bias_sum = finished(values, hidden // pieces)
    half = joined_pieces(spot, [total, *exchanged(k, [total] * len(in_plane), in_plane)])
    grad_features = route.finish(half)
    mate_half, grad_features = after(swapped(half, 1), grad_features)
    return (output, grad_features, whole_weight(spot, half, mate_half), bias_sum[0])


def solution(mesh):
    placed = (
        P("blk", None),
        P("blk", None, None, None),
        P("blk", None),
        P("blk", None, None, None, None),
        P(),
        P(),
        P("blk", None),
    )
    return jax.shard_map(
        local,
        mesh=mesh,
        in_specs=placed,
        out_specs=(P("blk", None), P("blk", None), P(), P()),
        check_vma=False,
    )
```

```python
import jax
import jax.numpy as jnp
from jax import lax
from jax.experimental import pallas as pl
from jax.experimental.pallas import tpu as pltpu
from jax.sharding import PartitionSpec as P

BF16, F32 = jnp.bfloat16, jnp.float32
BIAS_ROWS = 16


def call(kernel, outs, ins, smem=0, cost=0):
    spec = lambda k: pl.BlockSpec(memory_space=pltpu.SMEM if k < smem else pltpu.VMEM)
    out_shape = [jax.ShapeDtypeStruct(s, d) for s, d in outs]
    moved = sum(a.size * a.dtype.itemsize for a in list(ins) + out_shape)
    return pl.pallas_call(
        kernel,
        out_shape=out_shape,
        in_specs=[spec(k) for k in range(len(ins))],
        out_specs=[pl.BlockSpec(memory_space=pltpu.VMEM)] * len(outs),
        compiler_params=pltpu.CompilerParams(vmem_limit_bytes=moved + moved // 4 + 4 * 1024 * 1024),
        cost_estimate=pl.CostEstimate(flops=int(cost * 1e9), bytes_accessed=0, transcendentals=0),
    )(*ins)


def dense_tiles(spot, own_meta, mate_meta, own_values, mate_values, rows_dev, positions):
    window, slots, tile, _ = own_values.shape
    tile_rows = rows_dev // tile

    def kernel(spot_ref, own_meta_ref, mate_meta_ref, own_ref, mate_ref, dense_ref, flipped_ref):
        dense_ref[...] = jnp.zeros_like(dense_ref)
        flipped_ref[...] = jnp.zeros_like(flipped_ref)

        def place(meta_ref, values_ref, first_j, shift, first_row):
            def slot(t, _):
                i, k = t // slots, t % slots
                j = 2 * i + first_j
                base = j * (2 * slots + 1)

                @pl.when(k < meta_ref[base + 2 * slots])
                def _():
                    row = pl.multiple_of((meta_ref[base + 2 * k] + first_row) * tile, tile)
                    col = pl.multiple_of(((i + shift) * tile_rows + meta_ref[base + 2 * k + 1]) * tile, tile)
                    values = values_ref[j, k]
                    dense_ref[pl.ds(row, tile), pl.ds(col, tile)] = values
                    flipped_ref[pl.ds(col, tile), pl.ds(row, tile)] = values.T

                return 0

            lax.fori_loop(0, (window // 2) * slots, slot, 0)

        place(own_meta_ref, own_ref, 0, 0, 0)
        place(mate_meta_ref, mate_ref, 1, 1 - spot_ref[0] % 2, tile_rows)

    wide = positions * rows_dev
    return call(
        kernel,
        [((2 * rows_dev, wide), BF16), ((wide, 2 * rows_dev), BF16)],
        [spot, own_meta, mate_meta, own_values, mate_values],
        smem=3,
    )


def gathered_sums(dense, columns, first, sources, start=None):
    rows_dev, hidden = sources[0].shape
    last = 2 * rows_dev

    def kernel(dense_ref, *refs):
        refs, out_ref = list(refs[:-1]), refs[-1]
        total = refs.pop(0)[first:last] if start is not None else jnp.zeros((last - first, hidden), F32)
        for column, ref in zip(columns, refs):
            part = dense_ref[first:last, column * rows_dev : (column + 1) * rows_dev]
            total = total + jnp.dot(part, ref[...], preferred_element_type=F32)
        out_ref[...] = total

    return call(
        kernel,
        [((last - first, hidden), F32)],
        [dense, *([] if start is None else [start]), *sources],
    )[0]


def layer(spot, own_sum, mate_sum, weight, bias, grad_out, pieces):
    rows_dev, hidden = mate_sum.shape
    piece = hidden // pieces
    half = (pieces // 2, piece + BIAS_ROWS, hidden)

    def kernel(spot_ref, own_ref, mate_ref, weight_ref, bias_ref, grad_out_ref, out_ref, ga_ref, keep_ref, give_ref):
        agg = (own_ref[:rows_dev] + mate_ref[...]).astype(BF16)
        pre = jnp.dot(agg, weight_ref[...], preferred_element_type=F32) + bias_ref[...]
        sig = jax.nn.sigmoid(pre)
        out_ref[...] = (pre * sig).astype(BF16)
        grad_pre = (grad_out_ref[...].astype(F32) * sig * (1.0 + pre * (1.0 - sig))).astype(BF16)
        ga_ref[...] = lax.dot_general(
            grad_pre, weight_ref[...], (((1,), (1,)), ((), ())), preferred_element_type=F32
        ).astype(BF16)
        bias_term = jnp.sum(grad_pre.astype(F32), axis=0, keepdims=True)
        bias_rows = jnp.broadcast_to(bias_term, (BIAS_ROWS, hidden))
        terms = lax.dot_general(agg, grad_pre, (((0,), (0,)), ((), ())), preferred_element_type=F32)
        low, high = terms[: hidden // 2], terms[hidden // 2 :]
        even = spot_ref[0] % 2 == 0
        for ref, value in ((keep_ref, jnp.where(even, low, high)), (give_ref, jnp.where(even, high, low))):
            for q in range(pieces // 2):
                ref[q, :piece] = value[q * piece : (q + 1) * piece].astype(ref.dtype)
                ref[q, piece:] = bias_rows.astype(ref.dtype)

    shape = (rows_dev, hidden)
    return call(
        kernel,
        [(shape, BF16), (shape, BF16), (half, F32), (half, BF16)],
        [spot, own_sum, mate_sum, weight, bias.reshape(1, hidden), grad_out],
        smem=1,
    )


def folded(spot, keep, got):
    count, rows, hidden = keep.shape

    def kernel(spot_ref, keep_ref, got_ref, own_ref, *out_refs):
        for other in range(count):
            q = (spot_ref[0] >> 1) ^ other
            value = keep_ref[q] + got_ref[q].astype(F32)
            if other == 0:
                own_ref[...] = value
            else:
                out_refs[other - 1][...] = value.astype(BF16)

    shape = (rows, hidden)
    return call(kernel, [(shape, F32)] + [(shape, BF16)] * (count - 1), [spot, keep, got], smem=1)


def summed_terms(spot, terms, masks=None, cost=10):
    masks = masks or [None] * len(terms)

    def kernel(spot_ref, *refs):
        total = None
        for ref, mask in zip(refs, masks):
            value = ref[...].astype(F32)
            if mask is not None:
                value = jnp.where((mask >> spot_ref[0]) % 2 == 1, value, 0.0)
            total = value if total is None else total + value
        refs[-1][...] = total.astype(BF16)

    return call(kernel, [(terms[0].shape, BF16)], [spot, *terms], smem=1, cost=cost)[0]


def joined_pieces(spot, pieces):
    rows, hidden = pieces[0].shape
    count = len(pieces)

    def kernel(spot_ref, *refs):
        for other, ref in enumerate(refs[:-1]):
            q = (spot_ref[0] >> 1) ^ other
            refs[-1][pl.ds(pl.multiple_of(q * rows, rows), rows)] = ref[...]

    return call(kernel, [((count * rows, hidden), BF16)], [spot, *pieces], smem=1, cost=10)[0]


def whole_weight(spot, mine, other):
    rows, hidden = mine.shape

    def kernel(spot_ref, mine_ref, other_ref, out_ref):
        core = spot_ref[0] % 2
        out_ref[pl.ds(pl.multiple_of(core * rows, rows), rows)] = mine_ref[...].astype(F32)
        out_ref[pl.ds(pl.multiple_of((1 - core) * rows, rows), rows)] = other_ref[...].astype(F32)

    return call(kernel, [((2 * rows, hidden), F32)], [spot, mine, other], smem=1)[0]


def finished(values, piece):
    hidden = values[0].shape[1]

    def kernel(*refs):
        parts = [ref[...].astype(F32) for ref in refs[:-2]]
        while len(parts) > 1:
            parts = [parts[k] + parts[k + 1] for k in range(0, len(parts), 2)]
        refs[-2][...] = parts[0][:piece].astype(BF16)
        refs[-1][...] = parts[0][piece:]

    rows = values[0].shape[0]
    return call(kernel, [((piece, hidden), BF16), ((rows - piece, hidden), F32)], list(values), cost=10)


def scattered_sums(flipped, own, mate, columns, dtypes, spot=None, lookup=None):
    rows_dev, hidden = own.shape
    extra = [] if lookup is None else [spot, jnp.asarray(lookup, jnp.int32).reshape(-1)]

    def kernel(*refs):
        refs = list(refs)
        picks = [refs.pop(0) for _ in extra]
        flipped_ref, own_ref, mate_ref, *out_refs = refs
        for column, kinds in zip(columns, dtypes):
            if picks:
                column = picks[1][picks[0][0] * len(lookup[0]) + column]
                part = pl.ds(pl.multiple_of(column * rows_dev, rows_dev), rows_dev)
            else:
                part = pl.ds(column * rows_dev, rows_dev)
            total = jnp.dot(flipped_ref[part, :rows_dev], own_ref[...], preferred_element_type=F32)
            total += jnp.dot(flipped_ref[part, rows_dev:], mate_ref[...], preferred_element_type=F32)
            for kind in kinds:
                out_refs.pop(0)[...] = total.astype(kind)

    return call(
        kernel,
        [((rows_dev, hidden), kind) for kinds in dtypes for kind in kinds],
        [*extra, flipped, own, mate],
        cost=10,
        smem=len(extra),
    )


def after(value, *others):
    return lax.optimization_barrier((value, *others))


class Direct:
    def __init__(self, count, reach, spot):
        self.count, self.reach, self.positions, self.spot = count, reach, 2 * reach + 1, spot

    def sent(self, value, chips, kept=lambda s: True):
        pairs = [(s, (s + 2 * chips) % self.count) for s in range(self.count) if kept(s)]
        return lax.ppermute(value, "blk", pairs)

    def gather(self, features):
        last = self.positions - 1
        self.sources = [
            features
            if m == self.reach
            else self.sent(features, self.reach - m, lambda s: m < last or s % 2 == 0)
            for m in range(self.positions)
        ]

    def sums(self, dense, rows_dev):
        last = self.positions - 1
        start = gathered_sums(dense, range(last), 0, self.sources[:last])
        return gathered_sums(dense, [last], rows_dev, self.sources[last:], start), start

    def scatter(self, flipped, own, mate):
        self.flipped, self.own, self.mate = flipped, own, mate

    def step(self, k, token):
        if k != 1:
            return []
        _, mate = after(token, self.mate)
        kinds = [[F32 if m == self.reach else BF16] for m in range(self.positions)]
        terms = scattered_sums(self.flipped, self.own, mate, range(self.positions), kinds)
        last = self.positions - 1
        self.arriving = [
            term if m == self.reach else self.sent(term, m - self.reach, lambda s: m < last or s % 2 == 0)
            for m, term in enumerate(terms)
        ]
        return terms[:1]

    def finish(self):
        return summed_terms(self.spot, self.arriving)


class Relayed(Direct):
    EVEN, MIDDLE, ENDS, ODD_LOW = 0b01010101, 0b00111100, 0b11000011, 0b00001010
    LOOKUP = [
        [2, 4, 3, 0, 1], [2, 3, 4, 0, 1],
        [2, 4, 1, 0, 3], [2, 1, 4, 0, 3],
        [2, 0, 3, 4, 1], [2, 3, 0, 4, 1],
        [2, 0, 1, 4, 3], [2, 1, 0, 4, 3],
    ]

    def routed(self, value, steps):
        pairs = [(s, (s + steps[s % 8]) % self.count) for s in range(self.count) if s % 8 in steps]
        return lax.ppermute(value, "blk", pairs)

    def step(self, k, token):
        x = {spot: (spot ^ 2) - spot for spot in range(8)}
        y = {spot: (spot ^ 4) - spot for spot in range(8)}
        straight = {spot: (y if spot % 2 else x)[spot] for spot in range(8)}
        across = {spot: (x if spot % 2 else y)[spot] for spot in range(8)}
        take = lambda mate, *args: scattered_sums(self.flipped, self.own, mate, *args, self.spot, self.LOOKUP)
        if k == 0:
            _, mate = after(token, self.mate)
            self.to_last, self.to_plane, self.plane_rest = take(mate, (4, 3), [[BF16], [BF16, F32]])
            self.kept, self.to_across, self.to_straight = take(mate, (0, 1, 2), [[F32]] * 3)
            self.from_plane = self.routed(self.to_plane, {1: -8, 3: -8})
            self.from_last = self.routed(self.to_last, straight)
            return [self.kept, self.from_plane]
        if k == 1:
            _, rest, plane_rest = after(token, self.to_straight, self.plane_rest)
            out = summed_terms(self.spot, [plane_rest, self.from_last], [self.EVEN, self.MIDDLE])
            self.from_planes = self.routed(out, {0: -8, 2: -8, 4: 8, 6: 8, 5: -8, 3: 8})
            second = summed_terms(self.spot, [rest, self.from_plane], [None, self.ODD_LOW])
            self.second = self.routed(second, straight)
            return [second, out]
        if k == 2:
            _, rest = after(token, self.to_across)
            out = summed_terms(
                self.spot, [rest, self.from_planes, self.from_last], [None, self.EVEN | 0b00101000, self.ENDS]
            )
            self.arriving = [self.kept, self.second, self.routed(out, across)]
            return [out, self.second]
        return []


def local(features, tile_list, tile_count, tile_values, weight, bias, grad_out):
    count = lax.axis_size("blk")
    me = lax.axis_index("blk")
    window = tile_values.shape[1]
    reach = window // 4
    rows_dev, hidden = features.shape
    pieces = 8
    spot = (me % pieces).astype(jnp.int32).reshape(1)
    route = (Relayed if reach == 2 else Direct)(count, reach, spot)

    def swapped(value, distance):
        return lax.ppermute(value, "blk", [(s, s ^ distance) for s in range(count)])

    route.gather(features)
    mate_values, tile_list, tile_count = after(swapped(tile_values[0], 1), tile_list, tile_count)
    meta = jnp.concatenate([tile_list[0].reshape(window, -1), tile_count[0][:, None]], axis=1).reshape(-1)
    mate_meta = swapped(meta, 1)
    dense, flipped = dense_tiles(spot, meta, mate_meta, tile_values[0], mate_values, rows_dev, route.positions)
    mate_sum, own_sum = route.sums(dense, rows_dev)
    output, grad_agg, keep, give = layer(spot, own_sum, swapped(mate_sum, 1), weight, bias, grad_out, pieces)

    mate_grad, got = swapped(grad_agg, 1), swapped(give, 1)
    route.scatter(flipped, grad_agg, mate_grad)

    def exchanged(k, values, distances):
        others = [swapped(value, distance) for value, distance in zip(values, distances)]
        return after(others, *route.step(k, values[0]))[0]

    in_plane = [2 * d for d in range(1, pieces // 2)]
    own, *give = folded(spot, keep, got)
    total = summed_terms(spot, [own, *exchanged(0, give, in_plane)])
    step, k = pieces, 1
    while step < count:
        group = min(4, count // step)
        across = [step * d for d in range(1, group)]
        values = [total, *exchanged(k, [total] * (group - 1), across)]
        step, k = step * group, k + 1
        if step < count:
            total = summed_terms(spot, values)
    total, bias_sum = finished(values, hidden // pieces)
    half = joined_pieces(spot, [total, *exchanged(k, [total] * len(in_plane), in_plane)])
    grad_features = route.finish()
    mate_half, grad_features = after(swapped(half, 1), grad_features)
    return (output, grad_features, whole_weight(spot, half, mate_half), bias_sum[0])


def solution(mesh):
    placed = (
        P("blk", None),
        P("blk", None, None, None),
        P("blk", None),
        P("blk", None, None, None, None),
        P(),
        P(),
        P("blk", None),
    )
    return jax.shard_map(
        local,
        mesh=mesh,
        in_specs=placed,
        out_specs=(P("blk", None), P("blk", None), P(), P()),
        check_vma=False,
    )
```

```python
import jax
import jax.numpy as jnp
from jax import lax
from jax.experimental import pallas as pl
from jax.experimental.pallas import tpu as pltpu
from jax.sharding import PartitionSpec as P

BF16, F32 = jnp.bfloat16, jnp.float32
BIAS_ROWS = 16


def call(kernel, outs, ins, smem=0, cost=0):
    spec = lambda k: pl.BlockSpec(memory_space=pltpu.SMEM if k < smem else pltpu.VMEM)
    out_shape = [jax.ShapeDtypeStruct(s, d) for s, d in outs]
    moved = sum(a.size * a.dtype.itemsize for a in list(ins) + out_shape)
    return pl.pallas_call(
        kernel,
        out_shape=out_shape,
        in_specs=[spec(k) for k in range(len(ins))],
        out_specs=[pl.BlockSpec(memory_space=pltpu.VMEM)] * len(outs),
        compiler_params=pltpu.CompilerParams(vmem_limit_bytes=moved + moved // 4 + 4 * 1024 * 1024),
        cost_estimate=pl.CostEstimate(flops=int(cost * 1e9), bytes_accessed=0, transcendentals=0),
    )(*ins)


def dense_tiles(spot, own_meta, mate_meta, own_values, mate_values, rows_dev, positions):
    window, slots, tile, _ = own_values.shape
    tile_rows = rows_dev // tile

    def kernel(spot_ref, own_meta_ref, mate_meta_ref, own_ref, mate_ref, dense_ref, flipped_ref):
        dense_ref[...] = jnp.zeros_like(dense_ref)
        flipped_ref[...] = jnp.zeros_like(flipped_ref)

        def place(meta_ref, values_ref, first_j, shift, first_row):
            def slot(t, _):
                i, k = t // slots, t % slots
                j = 2 * i + first_j
                base = j * (2 * slots + 1)

                @pl.when(k < meta_ref[base + 2 * slots])
                def _():
                    row = pl.multiple_of((meta_ref[base + 2 * k] + first_row) * tile, tile)
                    col = pl.multiple_of(((i + shift) * tile_rows + meta_ref[base + 2 * k + 1]) * tile, tile)
                    values = values_ref[j, k]
                    dense_ref[pl.ds(row, tile), pl.ds(col, tile)] = values
                    flipped_ref[pl.ds(col, tile), pl.ds(row, tile)] = values.T

                return 0

            lax.fori_loop(0, (window // 2) * slots, slot, 0)

        place(own_meta_ref, own_ref, 0, 0, 0)
        place(mate_meta_ref, mate_ref, 1, 1 - spot_ref[0] % 2, tile_rows)

    wide = positions * rows_dev
    return call(
        kernel,
        [((2 * rows_dev, wide), BF16), ((wide, 2 * rows_dev), BF16)],
        [spot, own_meta, mate_meta, own_values, mate_values],
        smem=3,
    )


def gathered_sums(dense, columns, first, sources, start=None):
    rows_dev, hidden = sources[0].shape
    last = 2 * rows_dev

    def kernel(dense_ref, *refs):
        refs, out_ref = list(refs[:-1]), refs[-1]
        total = refs.pop(0)[first:last] if start is not None else jnp.zeros((last - first, hidden), F32)
        for column, ref in zip(columns, refs):
            part = dense_ref[first:last, column * rows_dev : (column + 1) * rows_dev]
            total = total + jnp.dot(part, ref[...], preferred_element_type=F32)
        out_ref[...] = total

    return call(
        kernel,
        [((last - first, hidden), F32)],
        [dense, *([] if start is None else [start]), *sources],
    )[0]


def layer(spot, own_sum, mate_sum, weight, bias, grad_out, pieces):
    rows_dev, hidden = mate_sum.shape
    piece = hidden // pieces
    half = (pieces // 2, piece + BIAS_ROWS, hidden)

    def kernel(spot_ref, own_ref, mate_ref, weight_ref, bias_ref, grad_out_ref, out_ref, ga_ref, keep_ref, give_ref):
        agg = (own_ref[:rows_dev] + mate_ref[...]).astype(BF16)
        pre = jnp.dot(agg, weight_ref[...], preferred_element_type=F32) + bias_ref[...]
        sig = jax.nn.sigmoid(pre)
        out_ref[...] = (pre * sig).astype(BF16)
        grad_pre = (grad_out_ref[...].astype(F32) * sig * (1.0 + pre * (1.0 - sig))).astype(BF16)
        ga_ref[...] = lax.dot_general(
            grad_pre, weight_ref[...], (((1,), (1,)), ((), ())), preferred_element_type=F32
        ).astype(BF16)
        bias_term = jnp.sum(grad_pre.astype(F32), axis=0, keepdims=True)
        bias_rows = jnp.broadcast_to(bias_term, (BIAS_ROWS, hidden))
        terms = lax.dot_general(agg, grad_pre, (((0,), (0,)), ((), ())), preferred_element_type=F32)
        low, high = terms[: hidden // 2], terms[hidden // 2 :]
        even = spot_ref[0] % 2 == 0
        for ref, value in ((keep_ref, jnp.where(even, low, high)), (give_ref, jnp.where(even, high, low))):
            for q in range(pieces // 2):
                ref[q, :piece] = value[q * piece : (q + 1) * piece].astype(ref.dtype)
                ref[q, piece:] = bias_rows.astype(ref.dtype)

    shape = (rows_dev, hidden)
    return call(
        kernel,
        [(shape, BF16), (shape, BF16), (half, F32), (half, BF16)],
        [spot, own_sum, mate_sum, weight, bias.reshape(1, hidden), grad_out],
        smem=1,
    )


def folded(spot, keep, got):
    count, rows, hidden = keep.shape

    def kernel(spot_ref, keep_ref, got_ref, own_ref, *out_refs):
        for other in range(count):
            q = (spot_ref[0] >> 1) ^ other
            value = keep_ref[q] + got_ref[q].astype(F32)
            if other == 0:
                own_ref[...] = value
            else:
                out_refs[other - 1][...] = value.astype(BF16)

    shape = (rows, hidden)
    return call(kernel, [(shape, F32)] + [(shape, BF16)] * (count - 1), [spot, keep, got], smem=1)


def summed_terms(spot, terms, masks=None, cost=10):
    masks = masks or [None] * len(terms)

    def kernel(spot_ref, *refs):
        total = None
        for ref, mask in zip(refs, masks):
            value = ref[...].astype(F32)
            if mask is not None:
                value = jnp.where((mask >> spot_ref[0]) % 2 == 1, value, 0.0)
            total = value if total is None else total + value
        refs[-1][...] = total.astype(BF16)

    return call(kernel, [(terms[0].shape, BF16)], [spot, *terms], smem=1, cost=cost)[0]


def joined_pieces(spot, pieces):
    rows, hidden = pieces[0].shape
    count = len(pieces)

    def kernel(spot_ref, *refs):
        for other, ref in enumerate(refs[:-1]):
            q = (spot_ref[0] >> 1) ^ other
            refs[-1][pl.ds(pl.multiple_of(q * rows, rows), rows)] = ref[...]

    return call(kernel, [((count * rows, hidden), BF16)], [spot, *pieces], smem=1, cost=10)[0]


def whole_weight(spot, mine, other):
    rows, hidden = mine.shape

    def kernel(spot_ref, mine_ref, other_ref, out_ref):
        core = spot_ref[0] % 2
        out_ref[pl.ds(pl.multiple_of(core * rows, rows), rows)] = mine_ref[...].astype(F32)
        out_ref[pl.ds(pl.multiple_of((1 - core) * rows, rows), rows)] = other_ref[...].astype(F32)

    return call(kernel, [((2 * rows, hidden), F32)], [spot, mine, other], smem=1)[0]


def finished(values, piece):
    hidden = values[0].shape[1]

    def kernel(*refs):
        parts = [ref[...].astype(F32) for ref in refs[:-2]]
        while len(parts) > 1:
            parts = [parts[k] + parts[k + 1] for k in range(0, len(parts), 2)]
        refs[-2][...] = parts[0][:piece].astype(BF16)
        refs[-1][...] = parts[0][piece : piece + 1]

    return call(kernel, [((piece, hidden), BF16), ((1, hidden), F32)], list(values), cost=10)


def scattered_sums(flipped, own, mate, columns, dtypes, spot=None, lookup=None):
    rows_dev, hidden = own.shape
    extra = [] if lookup is None else [spot, jnp.asarray(lookup, jnp.int32).reshape(-1)]

    def kernel(*refs):
        refs = list(refs)
        picks = [refs.pop(0) for _ in extra]
        flipped_ref, own_ref, mate_ref, *out_refs = refs
        for column, kinds in zip(columns, dtypes):
            if picks:
                column = picks[1][picks[0][0] * len(lookup[0]) + column]
                part = pl.ds(pl.multiple_of(column * rows_dev, rows_dev), rows_dev)
            else:
                part = pl.ds(column * rows_dev, rows_dev)
            total = jnp.dot(flipped_ref[part, :rows_dev], own_ref[...], preferred_element_type=F32)
            total += jnp.dot(flipped_ref[part, rows_dev:], mate_ref[...], preferred_element_type=F32)
            for kind in kinds:
                out_refs.pop(0)[...] = total.astype(kind)

    return call(
        kernel,
        [((rows_dev, hidden), kind) for kinds in dtypes for kind in kinds],
        [*extra, flipped, own, mate],
        cost=10,
        smem=len(extra),
    )


def after(value, *others):
    return lax.optimization_barrier((value, *others))


class Direct:
    def __init__(self, count, reach, spot):
        self.count, self.reach, self.positions, self.spot = count, reach, 2 * reach + 1, spot

    def sent(self, value, chips, kept=lambda s: True):
        pairs = [(s, (s + 2 * chips) % self.count) for s in range(self.count) if kept(s)]
        return lax.ppermute(value, "blk", pairs)

    def gather(self, features):
        last = self.positions - 1
        self.sources = [
            features
            if m == self.reach
            else self.sent(features, self.reach - m, lambda s: m < last or s % 2 == 0)
            for m in range(self.positions)
        ]

    def sums(self, dense, rows_dev):
        last = self.positions - 1
        start = gathered_sums(dense, range(last), 0, self.sources[:last])
        return gathered_sums(dense, [last], rows_dev, self.sources[last:], start), start

    def scatter(self, flipped, own, mate):
        self.flipped, self.own, self.mate = flipped, own, mate

    def step(self, k, token):
        if k != 1:
            return []
        _, mate = after(token, self.mate)
        kinds = [[F32 if m == self.reach else BF16] for m in range(self.positions)]
        terms = scattered_sums(self.flipped, self.own, mate, range(self.positions), kinds)
        last = self.positions - 1
        self.arriving = [
            term if m == self.reach else self.sent(term, m - self.reach, lambda s: m < last or s % 2 == 0)
            for m, term in enumerate(terms)
        ]
        return terms[:1]

    def finish(self, token):
        return summed_terms(self.spot, self.arriving)


class Relayed(Direct):
    EVEN, MIDDLE, ENDS = 0b01010101, 0b00111100, 0b11000011
    LOOKUP = [
        [2, 4, 3, 0, 1], [2, 3, 4, 0, 1],
        [2, 4, 1, 0, 3], [2, 1, 4, 0, 3],
        [2, 0, 3, 4, 1], [2, 3, 0, 4, 1],
        [2, 0, 1, 4, 3], [2, 1, 0, 4, 3],
    ]

    def routed(self, value, steps):
        pairs = [(s, (s + steps[s % 8]) % self.count) for s in range(self.count) if s % 8 in steps]
        return lax.ppermute(value, "blk", pairs)

    def step(self, k, token):
        x = {spot: (spot ^ 2) - spot for spot in range(8)}
        y = {spot: (spot ^ 4) - spot for spot in range(8)}
        straight = {spot: (y if spot % 2 else x)[spot] for spot in range(8)}
        across = {spot: (x if spot % 2 else y)[spot] for spot in range(8)}
        take = lambda mate, *args: scattered_sums(self.flipped, self.own, mate, *args, self.spot, self.LOOKUP)
        if k == 0:
            _, mate = after(token, self.mate)
            self.to_last, self.to_plane, self.plane_rest = take(mate, (4, 3), [[BF16], [BF16, F32]])
            self.from_plane = self.routed(self.to_plane, {1: -8, 3: 4})
            self.from_last = self.routed(self.to_last, straight)
            return [self.to_last]
        if k == 1:
            _, mate, plane_rest = after(token, self.mate, self.plane_rest)
            self.kept, self.to_across, to_straight = take(mate, (0, 1, 2), [[F32]] * 3)
            out = summed_terms(
                self.spot, [plane_rest, self.from_last, self.from_plane], [self.EVEN, self.MIDDLE, 0b10000000]
            )
            self.from_planes = self.routed(out, {0: -8, 2: -8, 4: 8, 6: 8, 5: -8, 3: 8, 7: -8})
            second = summed_terms(self.spot, [to_straight, self.from_plane], [None, 0b00000010])
            self.second = self.routed(second, straight)
            return [second, out]
        if k == 2:
            _, rest = after(token, self.to_across)
            out = summed_terms(
                self.spot, [rest, self.from_planes, self.from_last], [None, self.EVEN | 0b00101000, self.ENDS]
            )
            self.first = self.routed(out, across)
            return [out, self.second]
        return []

    def finish(self, token):
        _, kept = after(token, self.kept)
        terms = [kept, self.second, self.first, self.from_planes]
        return summed_terms(self.spot, terms, [None, None, None, 0b10000000])


def local(features, tile_list, tile_count, tile_values, weight, bias, grad_out):
    count = lax.axis_size("blk")
    me = lax.axis_index("blk")
    window = tile_values.shape[1]
    reach = window // 4
    rows_dev, hidden = features.shape
    pieces = 8
    spot = (me % pieces).astype(jnp.int32).reshape(1)
    route = (Relayed if reach == 2 else Direct)(count, reach, spot)

    def swapped(value, distance):
        return lax.ppermute(value, "blk", [(s, s ^ distance) for s in range(count)])

    route.gather(features)
    mate_values, tile_list, tile_count = after(swapped(tile_values[0], 1), tile_list, tile_count)
    meta = jnp.concatenate([tile_list[0].reshape(window, -1), tile_count[0][:, None]], axis=1).reshape(-1)
    mate_meta = swapped(meta, 1)
    dense, flipped = dense_tiles(spot, meta, mate_meta, tile_values[0], mate_values, rows_dev, route.positions)
    mate_sum, own_sum = route.sums(dense, rows_dev)
    output, grad_agg, keep, give = layer(spot, own_sum, swapped(mate_sum, 1), weight, bias, grad_out, pieces)

    mate_grad, got = swapped(grad_agg, 1), swapped(give, 1)
    route.scatter(flipped, grad_agg, mate_grad)

    def exchanged(k, values, distances):
        others = [swapped(value, distance) for value, distance in zip(values, distances)]
        return after(others, *route.step(k, values[0]))[0]

    in_plane = [2 * d for d in range(1, pieces // 2)]
    own, *give = folded(spot, keep, got)
    total = summed_terms(spot, [own, *exchanged(0, give, in_plane)])
    step, k = pieces, 1
    while step < count:
        group = min(4, count // step)
        across = [step * d for d in range(1, group)]
        values = [total, *exchanged(k, [total] * (group - 1), across)]
        step, k = step * group, k + 1
        if step < count:
            total = summed_terms(spot, values)
    total, bias_sum = finished(values, hidden // pieces)
    half = joined_pieces(spot, [total, *exchanged(k, [total] * len(in_plane), in_plane)])
    grad_weight = whole_weight(spot, half, swapped(half, 1))
    return (output, route.finish(grad_weight), grad_weight, bias_sum.reshape(hidden))


def solution(mesh):
    placed = (
        P("blk", None),
        P("blk", None, None, None),
        P("blk", None),
        P("blk", None, None, None, None),
        P(),
        P(),
        P("blk", None),
    )
    return jax.shard_map(
        local,
        mesh=mesh,
        in_specs=placed,
        out_specs=(P("blk", None), P("blk", None), P(), P()),
        check_vma=False,
    )
```

```python
import jax
import jax.numpy as jnp
from jax import lax
from jax.experimental import pallas as pl
from jax.experimental.pallas import tpu as pltpu
from jax.sharding import PartitionSpec as P

BF16, F32 = jnp.bfloat16, jnp.float32
BIAS_ROWS = 16


def call(kernel, outs, ins, smem=0, cost=0):
    spec = lambda k: pl.BlockSpec(memory_space=pltpu.SMEM if k < smem else pltpu.VMEM)
    out_shape = [jax.ShapeDtypeStruct(s, d) for s, d in outs]
    moved = sum(a.size * a.dtype.itemsize for a in list(ins) + out_shape)
    return pl.pallas_call(
        kernel,
        out_shape=out_shape,
        in_specs=[spec(k) for k in range(len(ins))],
        out_specs=[pl.BlockSpec(memory_space=pltpu.VMEM)] * len(outs),
        compiler_params=pltpu.CompilerParams(vmem_limit_bytes=moved + moved // 4 + 4 * 1024 * 1024),
        cost_estimate=pl.CostEstimate(flops=int(cost * 1e9), bytes_accessed=0, transcendentals=0),
    )(*ins)


def dense_tiles(spot, own_meta, mate_meta, own_values, mate_values, rows_dev, positions):
    window, slots, tile, _ = own_values.shape
    tile_rows = rows_dev // tile

    def kernel(spot_ref, own_meta_ref, mate_meta_ref, own_ref, mate_ref, dense_ref, flipped_ref):
        dense_ref[...] = jnp.zeros_like(dense_ref)
        flipped_ref[...] = jnp.zeros_like(flipped_ref)

        def place(meta_ref, values_ref, first_j, shift, first_row):
            def slot(t, _):
                i, k = t // slots, t % slots
                j = 2 * i + first_j
                base = j * (2 * slots + 1)

                @pl.when(k < meta_ref[base + 2 * slots])
                def _():
                    row = pl.multiple_of((meta_ref[base + 2 * k] + first_row) * tile, tile)
                    col = pl.multiple_of(((i + shift) * tile_rows + meta_ref[base + 2 * k + 1]) * tile, tile)
                    values = values_ref[j, k]
                    dense_ref[pl.ds(row, tile), pl.ds(col, tile)] = values
                    flipped_ref[pl.ds(col, tile), pl.ds(row, tile)] = values.T

                return 0

            lax.fori_loop(0, (window // 2) * slots, slot, 0)

        place(own_meta_ref, own_ref, 0, 0, 0)
        place(mate_meta_ref, mate_ref, 1, 1 - spot_ref[0] % 2, tile_rows)

    wide = positions * rows_dev
    return call(
        kernel,
        [((2 * rows_dev, wide), BF16), ((wide, 2 * rows_dev), BF16)],
        [spot, own_meta, mate_meta, own_values, mate_values],
        smem=3,
    )


def gathered_sums(dense, columns, first, sources, start=None):
    rows_dev, hidden = sources[0].shape
    last = 2 * rows_dev

    def kernel(dense_ref, *refs):
        refs, out_ref = list(refs[:-1]), refs[-1]
        total = refs.pop(0)[first:last] if start is not None else jnp.zeros((last - first, hidden), F32)
        for column, ref in zip(columns, refs):
            part = dense_ref[first:last, column * rows_dev : (column + 1) * rows_dev]
            total = total + jnp.dot(part, ref[...], preferred_element_type=F32)
        out_ref[...] = total

    return call(
        kernel,
        [((last - first, hidden), F32)],
        [dense, *([] if start is None else [start]), *sources],
    )[0]


def layer(spot, own_sum, mate_sum, weight, bias, grad_out, pieces):
    rows_dev, hidden = mate_sum.shape
    piece = hidden // pieces
    half = (pieces // 2, piece + BIAS_ROWS, hidden)

    def kernel(spot_ref, own_ref, mate_ref, weight_ref, bias_ref, grad_out_ref, out_ref, ga_ref, keep_ref, give_ref):
        agg = (own_ref[:rows_dev] + mate_ref[...]).astype(BF16)
        pre = jnp.dot(agg, weight_ref[...], preferred_element_type=F32) + bias_ref[...]
        sig = jax.nn.sigmoid(pre)
        out_ref[...] = (pre * sig).astype(BF16)
        grad_pre = (grad_out_ref[...].astype(F32) * sig * (1.0 + pre * (1.0 - sig))).astype(BF16)
        ga_ref[...] = lax.dot_general(
            grad_pre, weight_ref[...], (((1,), (1,)), ((), ())), preferred_element_type=F32
        ).astype(BF16)
        bias_term = jnp.sum(grad_pre.astype(F32), axis=0, keepdims=True)
        bias_rows = jnp.broadcast_to(bias_term, (BIAS_ROWS, hidden))
        terms = lax.dot_general(agg, grad_pre, (((0,), (0,)), ((), ())), preferred_element_type=F32)
        low, high = terms[: hidden // 2], terms[hidden // 2 :]
        even = spot_ref[0] % 2 == 0
        for ref, value in ((keep_ref, jnp.where(even, low, high)), (give_ref, jnp.where(even, high, low))):
            for q in range(pieces // 2):
                ref[q, :piece] = value[q * piece : (q + 1) * piece].astype(ref.dtype)
                ref[q, piece:] = bias_rows.astype(ref.dtype)

    shape = (rows_dev, hidden)
    return call(
        kernel,
        [(shape, BF16), (shape, BF16), (half, F32), (half, BF16)],
        [spot, own_sum, mate_sum, weight, bias.reshape(1, hidden), grad_out],
        smem=1,
    )


def folded(spot, keep, got):
    count, rows, hidden = keep.shape

    def kernel(spot_ref, keep_ref, got_ref, own_ref, *out_refs):
        for other in range(count):
            q = (spot_ref[0] >> 1) ^ other
            value = keep_ref[q] + got_ref[q].astype(F32)
            if other == 0:
                own_ref[...] = value
            else:
                out_refs[other - 1][...] = value.astype(BF16)

    shape = (rows, hidden)
    return call(kernel, [(shape, F32)] + [(shape, BF16)] * (count - 1), [spot, keep, got], smem=1)


def summed_terms(spot, terms, masks=None, cost=10):
    masks = masks or [None] * len(terms)

    def kernel(spot_ref, *refs):
        total = None
        for ref, mask in zip(refs, masks):
            value = ref[...].astype(F32)
            if mask is not None:
                value = jnp.where((mask >> spot_ref[0]) % 2 == 1, value, 0.0)
            total = value if total is None else total + value
        refs[-1][...] = total.astype(BF16)

    return call(kernel, [(terms[0].shape, BF16)], [spot, *terms], smem=1, cost=cost)[0]


def joined_pieces(spot, pieces):
    rows, hidden = pieces[0].shape
    count = len(pieces)

    def kernel(spot_ref, *refs):
        for other, ref in enumerate(refs[:-1]):
            q = (spot_ref[0] >> 1) ^ other
            refs[-1][pl.ds(pl.multiple_of(q * rows, rows), rows)] = ref[...]

    return call(kernel, [((count * rows, hidden), BF16)], [spot, *pieces], smem=1, cost=10)[0]


def whole_weight(spot, mine, other):
    rows, hidden = mine.shape

    def kernel(spot_ref, mine_ref, other_ref, out_ref):
        core = spot_ref[0] % 2
        out_ref[pl.ds(pl.multiple_of(core * rows, rows), rows)] = mine_ref[...].astype(F32)
        out_ref[pl.ds(pl.multiple_of((1 - core) * rows, rows), rows)] = other_ref[...].astype(F32)

    return call(kernel, [((2 * rows, hidden), F32)], [spot, mine, other], smem=1)[0]


def finished(values, piece):
    hidden = values[0].shape[1]

    def kernel(*refs):
        parts = [ref[...].astype(F32) for ref in refs[:-2]]
        while len(parts) > 1:
            parts = [parts[k] + parts[k + 1] for k in range(0, len(parts), 2)]
        refs[-2][...] = parts[0][:piece].astype(BF16)
        refs[-1][...] = parts[0][piece : piece + 1]

    return call(kernel, [((piece, hidden), BF16), ((1, hidden), F32)], list(values), cost=10)


def scattered_sums(flipped, own, mate, columns, dtypes, spot=None, lookup=None):
    rows_dev, hidden = own.shape
    extra = [] if lookup is None else [spot, jnp.asarray(lookup, jnp.int32).reshape(-1)]

    def kernel(*refs):
        refs = list(refs)
        picks = [refs.pop(0) for _ in extra]
        flipped_ref, own_ref, mate_ref, *out_refs = refs
        for column, kinds in zip(columns, dtypes):
            if picks:
                column = picks[1][picks[0][0] * len(lookup[0]) + column]
                part = pl.ds(pl.multiple_of(column * rows_dev, rows_dev), rows_dev)
            else:
                part = pl.ds(column * rows_dev, rows_dev)
            total = jnp.dot(flipped_ref[part, :rows_dev], own_ref[...], preferred_element_type=F32)
            total += jnp.dot(flipped_ref[part, rows_dev:], mate_ref[...], preferred_element_type=F32)
            for kind in kinds:
                out_refs.pop(0)[...] = total.astype(kind)

    return call(
        kernel,
        [((rows_dev, hidden), kind) for kinds in dtypes for kind in kinds],
        [*extra, flipped, own, mate],
        cost=10,
        smem=len(extra),
    )


def after(value, *others):
    return lax.optimization_barrier((value, *others))


class Direct:
    def __init__(self, count, reach, spot):
        self.count, self.reach, self.positions, self.spot = count, reach, 2 * reach + 1, spot

    def sent(self, value, chips, kept=lambda s: True):
        pairs = [(s, (s + 2 * chips) % self.count) for s in range(self.count) if kept(s)]
        return lax.ppermute(value, "blk", pairs)

    def gather(self, features):
        last = self.positions - 1
        self.sources = [
            features
            if m == self.reach
            else self.sent(features, self.reach - m, lambda s: m < last or s % 2 == 0)
            for m in range(self.positions)
        ]

    def sums(self, dense, rows_dev):
        last = self.positions - 1
        start = gathered_sums(dense, range(last), 0, self.sources[:last])
        return gathered_sums(dense, [last], rows_dev, self.sources[last:], start), start

    def scatter(self, flipped, own, mate):
        self.flipped, self.own, self.mate = flipped, own, mate

    def step(self, k, token):
        if k != 1:
            return []
        _, mate = after(token, self.mate)
        kinds = [[F32 if m == self.reach else BF16] for m in range(self.positions)]
        terms = scattered_sums(self.flipped, self.own, mate, range(self.positions), kinds)
        last = self.positions - 1
        self.arriving = [
            term if m == self.reach else self.sent(term, m - self.reach, lambda s: m < last or s % 2 == 0)
            for m, term in enumerate(terms)
        ]
        return terms[:1]

    def finish(self, token):
        return summed_terms(self.spot, self.arriving)


class Relayed(Direct):
    EVEN, MIDDLE, ENDS = 0b01010101, 0b00111100, 0b11000011
    LOOKUP = [
        [2, 4, 3, 0, 1], [2, 3, 4, 0, 1],
        [2, 4, 1, 0, 3], [2, 1, 4, 0, 3],
        [2, 0, 3, 4, 1], [2, 3, 0, 4, 1],
        [2, 0, 1, 4, 3], [2, 1, 0, 4, 3],
    ]

    def routed(self, value, steps):
        pairs = [(s, (s + steps[s % 8]) % self.count) for s in range(self.count) if s % 8 in steps]
        return lax.ppermute(value, "blk", pairs)

    def step(self, k, token):
        x = {spot: (spot ^ 2) - spot for spot in range(8)}
        y = {spot: (spot ^ 4) - spot for spot in range(8)}
        straight = {spot: (y if spot % 2 else x)[spot] for spot in range(8)}
        across = {spot: (x if spot % 2 else y)[spot] for spot in range(8)}
        take = lambda mate, *args: scattered_sums(self.flipped, self.own, mate, *args, self.spot, self.LOOKUP)
        if k == 0:
            _, mate = after(token, self.mate)
            self.to_last, self.to_plane, self.plane_rest = take(mate, (4, 3), [[BF16], [BF16, F32]])
            self.from_plane = self.routed(self.to_plane, {1: -8, 3: 4})
            self.from_last = self.routed(self.to_last, straight)
            return [self.to_last]
        if k == 1:
            _, mate, plane_rest = after(token, self.mate, self.plane_rest)
            self.kept, self.to_across, to_straight = take(mate, (0, 1, 2), [[F32]] * 3)
            out = summed_terms(
                self.spot, [plane_rest, self.from_last, self.from_plane], [self.EVEN, self.MIDDLE, 0b10000000]
            )
            self.from_planes = self.routed(out, {0: -8, 2: -8, 4: 8, 6: 8, 5: -8, 3: 8, 7: -8})
            second = summed_terms(self.spot, [to_straight, self.from_plane], [None, 0b00000010])
            self.second = self.routed(second, straight)
            return [second, out]
        if k == 2:
            _, rest, _ = after(token, self.to_across, self.second)
            out = summed_terms(
                self.spot, [rest, self.from_planes, self.from_last], [None, self.EVEN | 0b00101000, self.ENDS]
            )
            self.first = self.routed(out, across)
            return [out]
        return []

    def finish(self, token):
        _, kept = after(token, self.kept)
        terms = [kept, self.second, self.first, self.from_planes]
        return summed_terms(self.spot, terms, [None, None, None, 0b10000000])


def local(features, tile_list, tile_count, tile_values, weight, bias, grad_out):
    count = lax.axis_size("blk")
    me = lax.axis_index("blk")
    window = tile_values.shape[1]
    reach = window // 4
    rows_dev, hidden = features.shape
    pieces = 8
    spot = (me % pieces).astype(jnp.int32).reshape(1)
    route = (Relayed if reach == 2 else Direct)(count, reach, spot)

    def swapped(value, distance):
        return lax.ppermute(value, "blk", [(s, s ^ distance) for s in range(count)])

    route.gather(features)
    mate_values, tile_list, tile_count = after(swapped(tile_values[0], 1), tile_list, tile_count)
    meta = jnp.concatenate([tile_list[0].reshape(window, -1), tile_count[0][:, None]], axis=1).reshape(-1)
    mate_meta = swapped(meta, 1)
    dense, flipped = dense_tiles(spot, meta, mate_meta, tile_values[0], mate_values, rows_dev, route.positions)
    mate_sum, own_sum = route.sums(dense, rows_dev)
    output, grad_agg, keep, give = layer(spot, own_sum, swapped(mate_sum, 1), weight, bias, grad_out, pieces)

    mate_grad, got = swapped(grad_agg, 1), swapped(give, 1)
    route.scatter(flipped, grad_agg, mate_grad)

    def exchanged(k, values, distances):
        others = [swapped(value, distance) for value, distance in zip(values, distances)]
        return after(others, *route.step(k, values[0]))[0]

    in_plane = [2 * d for d in range(1, pieces // 2)]
    own, *give = folded(spot, keep, got)
    total = summed_terms(spot, [own, *exchanged(0, give, in_plane)])
    step, k = pieces, 1
    while step < count:
        group = min(4, count // step)
        across = [step * d for d in range(1, group)]
        values = [total, *exchanged(k, [total] * (group - 1), across)]
        step, k = step * group, k + 1
        if step < count:
            total = summed_terms(spot, values)
    total, bias_sum = finished(values, hidden // pieces)
    half = joined_pieces(spot, [total, *exchanged(k, [total] * len(in_plane), in_plane)])
    grad_weight = whole_weight(spot, half, swapped(half, 1))
    return (output, route.finish(grad_weight), grad_weight, bias_sum.reshape(hidden))


def solution(mesh):
    placed = (
        P("blk", None),
        P("blk", None, None, None),
        P("blk", None),
        P("blk", None, None, None, None),
        P(),
        P(),
        P("blk", None),
    )
    return jax.shard_map(
        local,
        mesh=mesh,
        in_specs=placed,
        out_specs=(P("blk", None), P("blk", None), P(), P()),
        check_vma=False,
    )
```

```python
import jax
import jax.numpy as jnp
from jax import lax
from jax.experimental import pallas as pl
from jax.experimental.pallas import tpu as pltpu
from jax.sharding import PartitionSpec as P

BF16, F32 = jnp.bfloat16, jnp.float32
BIAS_ROWS = 16


def call(kernel, outs, ins, smem=0, cost=0):
    spec = lambda k: pl.BlockSpec(memory_space=pltpu.SMEM if k < smem else pltpu.VMEM)
    out_shape = [jax.ShapeDtypeStruct(s, d) for s, d in outs]
    moved = sum(a.size * a.dtype.itemsize for a in list(ins) + out_shape)
    return pl.pallas_call(
        kernel,
        out_shape=out_shape,
        in_specs=[spec(k) for k in range(len(ins))],
        out_specs=[pl.BlockSpec(memory_space=pltpu.VMEM)] * len(outs),
        compiler_params=pltpu.CompilerParams(vmem_limit_bytes=moved + moved // 4 + 4 * 1024 * 1024),
        cost_estimate=pl.CostEstimate(flops=int(cost * 1e9), bytes_accessed=0, transcendentals=0),
    )(*ins)


def dense_tiles(spot, own_meta, mate_meta, own_values, mate_values, rows_dev, positions):
    window, slots, tile, _ = own_values.shape
    tile_rows = rows_dev // tile

    def kernel(spot_ref, own_meta_ref, mate_meta_ref, own_ref, mate_ref, dense_ref, flipped_ref):
        dense_ref[...] = jnp.zeros_like(dense_ref)
        flipped_ref[...] = jnp.zeros_like(flipped_ref)

        def place(meta_ref, values_ref, first_j, shift, first_row):
            def slot(t, _):
                i, k = t // slots, t % slots
                j = 2 * i + first_j
                base = j * (2 * slots + 1)

                @pl.when(k < meta_ref[base + 2 * slots])
                def _():
                    row = pl.multiple_of((meta_ref[base + 2 * k] + first_row) * tile, tile)
                    col = pl.multiple_of(((i + shift) * tile_rows + meta_ref[base + 2 * k + 1]) * tile, tile)
                    values = values_ref[j, k]
                    dense_ref[pl.ds(row, tile), pl.ds(col, tile)] = values
                    flipped_ref[pl.ds(col, tile), pl.ds(row, tile)] = values.T

                return 0

            lax.fori_loop(0, (window // 2) * slots, slot, 0)

        place(own_meta_ref, own_ref, 0, 0, 0)
        place(mate_meta_ref, mate_ref, 1, 1 - spot_ref[0] % 2, tile_rows)

    wide = positions * rows_dev
    return call(
        kernel,
        [((2 * rows_dev, wide), BF16), ((wide, 2 * rows_dev), BF16)],
        [spot, own_meta, mate_meta, own_values, mate_values],
        smem=3,
    )


def gathered_sums(dense, columns, first, sources, start=None):
    rows_dev, hidden = sources[0].shape
    last = 2 * rows_dev

    def kernel(dense_ref, *refs):
        refs, out_ref = list(refs[:-1]), refs[-1]
        total = refs.pop(0)[first:last] if start is not None else jnp.zeros((last - first, hidden), F32)
        for column, ref in zip(columns, refs):
            part = dense_ref[first:last, column * rows_dev : (column + 1) * rows_dev]
            total = total + jnp.dot(part, ref[...], preferred_element_type=F32)
        out_ref[...] = total

    return call(
        kernel,
        [((last - first, hidden), F32)],
        [dense, *([] if start is None else [start]), *sources],
    )[0]


def layer(spot, own_sum, mate_sum, weight, bias, grad_out, pieces):
    rows_dev, hidden = mate_sum.shape
    piece = hidden // pieces
    half = (pieces // 2, piece + BIAS_ROWS, hidden)

    def kernel(spot_ref, own_ref, mate_ref, weight_ref, bias_ref, grad_out_ref, out_ref, ga_ref, keep_ref, give_ref):
        agg = (own_ref[:rows_dev] + mate_ref[...]).astype(BF16)
        pre = jnp.dot(agg, weight_ref[...], preferred_element_type=F32) + bias_ref[...]
        sig = jax.nn.sigmoid(pre)
        out_ref[...] = (pre * sig).astype(BF16)
        grad_pre = (grad_out_ref[...].astype(F32) * sig * (1.0 + pre * (1.0 - sig))).astype(BF16)
        ga_ref[...] = lax.dot_general(
            grad_pre, weight_ref[...], (((1,), (1,)), ((), ())), preferred_element_type=F32
        ).astype(BF16)
        bias_term = jnp.sum(grad_pre.astype(F32), axis=0, keepdims=True)
        bias_rows = jnp.broadcast_to(bias_term, (BIAS_ROWS, hidden))
        terms = lax.dot_general(agg, grad_pre, (((0,), (0,)), ((), ())), preferred_element_type=F32)
        low, high = terms[: hidden // 2], terms[hidden // 2 :]
        even = spot_ref[0] % 2 == 0
        for ref, value in ((keep_ref, jnp.where(even, low, high)), (give_ref, jnp.where(even, high, low))):
            for q in range(pieces // 2):
                ref[q, :piece] = value[q * piece : (q + 1) * piece].astype(ref.dtype)
                ref[q, piece:] = bias_rows.astype(ref.dtype)

    shape = (rows_dev, hidden)
    return call(
        kernel,
        [(shape, BF16), (shape, BF16), (half, F32), (half, BF16)],
        [spot, own_sum, mate_sum, weight, bias.reshape(1, hidden), grad_out],
        smem=1,
    )


def folded(spot, keep, got):
    count, rows, hidden = keep.shape

    def kernel(spot_ref, keep_ref, got_ref, own_ref, *out_refs):
        for other in range(count):
            q = (spot_ref[0] >> 1) ^ other
            value = keep_ref[q] + got_ref[q].astype(F32)
            if other == 0:
                own_ref[...] = value
            else:
                out_refs[other - 1][...] = value.astype(BF16)

    shape = (rows, hidden)
    return call(kernel, [(shape, F32)] + [(shape, BF16)] * (count - 1), [spot, keep, got], smem=1)


def summed_terms(spot, terms, masks=None, cost=10):
    masks = masks or [None] * len(terms)

    def kernel(spot_ref, *refs):
        total = None
        for ref, mask in zip(refs, masks):
            value = ref[...].astype(F32)
            if mask is not None:
                value = jnp.where((mask >> spot_ref[0]) % 2 == 1, value, 0.0)
            total = value if total is None else total + value
        refs[-1][...] = total.astype(BF16)

    return call(kernel, [(terms[0].shape, BF16)], [spot, *terms], smem=1, cost=cost)[0]


def joined_pieces(spot, pieces):
    rows, hidden = pieces[0].shape
    count = len(pieces)

    def kernel(spot_ref, *refs):
        for other, ref in enumerate(refs[:-1]):
            q = (spot_ref[0] >> 1) ^ other
            refs[-1][pl.ds(pl.multiple_of(q * rows, rows), rows)] = ref[...]

    return call(kernel, [((count * rows, hidden), BF16)], [spot, *pieces], smem=1, cost=10)[0]


def whole_weight(spot, mine, other):
    rows, hidden = mine.shape

    def kernel(spot_ref, mine_ref, other_ref, out_ref):
        core = spot_ref[0] % 2
        out_ref[pl.ds(pl.multiple_of(core * rows, rows), rows)] = mine_ref[...].astype(F32)
        out_ref[pl.ds(pl.multiple_of((1 - core) * rows, rows), rows)] = other_ref[...].astype(F32)

    return call(kernel, [((2 * rows, hidden), F32)], [spot, mine, other], smem=1)[0]


def finished(values, piece):
    hidden = values[0].shape[1]

    def kernel(*refs):
        parts = [ref[...].astype(F32) for ref in refs[:-2]]
        while len(parts) > 1:
            parts = [parts[k] + parts[k + 1] for k in range(0, len(parts), 2)]
        refs[-2][...] = parts[0][:piece].astype(BF16)
        refs[-1][...] = parts[0][piece : piece + 1]

    return call(kernel, [((piece, hidden), BF16), ((1, hidden), F32)], list(values), cost=10)


def scattered_sums(flipped, own, mate, columns, dtypes, spot=None, lookup=None, cost=10):
    rows_dev, hidden = own.shape
    extra = [] if lookup is None else [spot, jnp.asarray(lookup, jnp.int32).reshape(-1)]

    def kernel(*refs):
        refs = list(refs)
        picks = [refs.pop(0) for _ in extra]
        flipped_ref, own_ref, mate_ref, *out_refs = refs
        for column, kinds in zip(columns, dtypes):
            if picks:
                column = picks[1][picks[0][0] * len(lookup[0]) + column]
                part = pl.ds(pl.multiple_of(column * rows_dev, rows_dev), rows_dev)
            else:
                part = pl.ds(column * rows_dev, rows_dev)
            total = jnp.dot(flipped_ref[part, :rows_dev], own_ref[...], preferred_element_type=F32)
            total += jnp.dot(flipped_ref[part, rows_dev:], mate_ref[...], preferred_element_type=F32)
            for kind in kinds:
                out_refs.pop(0)[...] = total.astype(kind)

    return call(
        kernel,
        [((rows_dev, hidden), kind) for kinds in dtypes for kind in kinds],
        [*extra, flipped, own, mate],
        cost=cost,
        smem=len(extra),
    )


def after(value, *others):
    return lax.optimization_barrier((value, *others))


class Direct:
    def __init__(self, count, reach, spot):
        self.count, self.reach, self.positions, self.spot = count, reach, 2 * reach + 1, spot

    def sent(self, value, chips, kept=lambda s: True):
        pairs = [(s, (s + 2 * chips) % self.count) for s in range(self.count) if kept(s)]
        return lax.ppermute(value, "blk", pairs)

    def gather(self, features):
        last = self.positions - 1
        self.sources = [
            features
            if m == self.reach
            else self.sent(features, self.reach - m, lambda s: m < last or s % 2 == 0)
            for m in range(self.positions)
        ]

    def sums(self, dense, rows_dev):
        last = self.positions - 1
        start = gathered_sums(dense, range(last), 0, self.sources[:last])
        return gathered_sums(dense, [last], rows_dev, self.sources[last:], start), start

    def scatter(self, flipped, own, mate):
        self.flipped, self.own, self.mate = flipped, own, mate

    def step(self, k, token):
        if k != 1:
            return []
        _, mate = after(token, self.mate)
        kinds = [[F32 if m == self.reach else BF16] for m in range(self.positions)]
        terms = scattered_sums(self.flipped, self.own, mate, range(self.positions), kinds)
        last = self.positions - 1
        self.arriving = [
            term if m == self.reach else self.sent(term, m - self.reach, lambda s: m < last or s % 2 == 0)
            for m, term in enumerate(terms)
        ]
        return terms[:1]

    def finish(self, token):
        return summed_terms(self.spot, self.arriving)


class Relayed(Direct):
    EVEN, MIDDLE, ENDS = 0b01010101, 0b00111100, 0b11000011
    LOOKUP = [
        [2, 4, 3, 0, 1], [2, 3, 4, 0, 1],
        [2, 4, 1, 0, 3], [2, 1, 4, 0, 3],
        [2, 0, 3, 4, 1], [2, 3, 0, 4, 1],
        [2, 0, 1, 4, 3], [2, 1, 0, 4, 3],
    ]

    def routed(self, value, steps):
        pairs = [(s, (s + steps[s % 8]) % self.count) for s in range(self.count) if s % 8 in steps]
        return lax.ppermute(value, "blk", pairs)

    def step(self, k, token):
        x = {spot: (spot ^ 2) - spot for spot in range(8)}
        y = {spot: (spot ^ 4) - spot for spot in range(8)}
        straight = {spot: (y if spot % 2 else x)[spot] for spot in range(8)}
        across = {spot: (x if spot % 2 else y)[spot] for spot in range(8)}
        take = lambda mate, *args, cost=10: scattered_sums(
            self.flipped, self.own, mate, *args, self.spot, self.LOOKUP, cost
        )
        if k == 0:
            _, mate = after(token, self.mate)
            self.to_last, self.to_plane, self.plane_rest, self.to_straight = take(
                mate, (4, 3, 2), [[BF16], [BF16, F32], [F32]]
            )
            self.from_last = self.routed(self.to_last, straight)
            self.from_plane = self.routed(self.to_plane, {1: -8, 3: 4})
            return [self.to_last]
        if k == 1:
            _, plane_rest = after(token, self.plane_rest)
            out = summed_terms(
                self.spot, [plane_rest, self.from_last, self.from_plane], [self.EVEN, self.MIDDLE, 0b10000000]
            )
            self.from_planes = self.routed(out, {0: -8, 2: -8, 4: 8, 6: 8, 5: -8, 3: 8, 7: -8})
            out, to_straight, mate = after(out, self.to_straight, self.mate)
            second = summed_terms(self.spot, [to_straight, self.from_plane], [None, 0b00000010])
            self.second = self.routed(second, straight)
            self.kept, self.to_across = take(mate, (0, 1), [[F32]] * 2, cost=10)
            return [second, self.kept]
        if k == 2:
            _, rest, _ = after(token, self.to_across, self.second)
            out = summed_terms(
                self.spot, [rest, self.from_planes, self.from_last], [None, self.EVEN | 0b00101000, self.ENDS]
            )
            self.first = self.routed(out, across)
            return [out]
        return []

    def finish(self, token):
        _, kept = after(token, self.kept)
        terms = [kept, self.second, self.first, self.from_planes]
        return summed_terms(self.spot, terms, [None, None, None, 0b10000000])


def local(features, tile_list, tile_count, tile_values, weight, bias, grad_out):
    count = lax.axis_size("blk")
    me = lax.axis_index("blk")
    window = tile_values.shape[1]
    reach = window // 4
    rows_dev, hidden = features.shape
    pieces = 8
    spot = (me % pieces).astype(jnp.int32).reshape(1)
    route = (Relayed if reach == 2 else Direct)(count, reach, spot)

    def swapped(value, distance):
        return lax.ppermute(value, "blk", [(s, s ^ distance) for s in range(count)])

    route.gather(features)
    mate_values, tile_list, tile_count = after(swapped(tile_values[0], 1), tile_list, tile_count)
    meta = jnp.concatenate([tile_list[0].reshape(window, -1), tile_count[0][:, None]], axis=1).reshape(-1)
    mate_meta = swapped(meta, 1)
    dense, flipped = dense_tiles(spot, meta, mate_meta, tile_values[0], mate_values, rows_dev, route.positions)
    mate_sum, own_sum = route.sums(dense, rows_dev)
    output, grad_agg, keep, give = layer(spot, own_sum, swapped(mate_sum, 1), weight, bias, grad_out, pieces)

    mate_grad, got = swapped(grad_agg, 1), swapped(give, 1)
    route.scatter(flipped, grad_agg, mate_grad)

    def exchanged(k, values, distances):
        others = [swapped(value, distance) for value, distance in zip(values, distances)]
        return after(others, *route.step(k, values[0]))[0]

    in_plane = [2 * d for d in range(1, pieces // 2)]
    own, *give = folded(spot, keep, got)
    total = summed_terms(spot, [own, *exchanged(0, give, in_plane)])
    step, k = pieces, 1
    while step < count:
        group = min(4, count // step)
        across = [step * d for d in range(1, group)]
        values = [total, *exchanged(k, [total] * (group - 1), across)]
        step, k = step * group, k + 1
        if step < count:
            total = summed_terms(spot, values)
    total, bias_sum = finished(values, hidden // pieces)
    half = joined_pieces(spot, [total, *exchanged(k, [total] * len(in_plane), in_plane)])
    grad_weight = whole_weight(spot, half, swapped(half, 1))
    return (output, route.finish(grad_weight), grad_weight, bias_sum.reshape(hidden))


def solution(mesh):
    placed = (
        P("blk", None),
        P("blk", None, None, None),
        P("blk", None),
        P("blk", None, None, None, None),
        P(),
        P(),
        P("blk", None),
    )
    return jax.shard_map(
        local,
        mesh=mesh,
        in_specs=placed,
        out_specs=(P("blk", None), P("blk", None), P(), P()),
        check_vma=False,
    )
```

```python
import jax
import jax.numpy as jnp
from jax import lax
from jax.experimental import pallas as pl
from jax.experimental.pallas import tpu as pltpu
from jax.sharding import PartitionSpec as P

BF16, F32 = jnp.bfloat16, jnp.float32
BIAS_ROWS = 16


def call(kernel, outs, ins, smem=0, cost=0):
    spec = lambda k: pl.BlockSpec(memory_space=pltpu.SMEM if k < smem else pltpu.VMEM)
    out_shape = [jax.ShapeDtypeStruct(s, d) for s, d in outs]
    moved = sum(a.size * a.dtype.itemsize for a in list(ins) + out_shape)
    return pl.pallas_call(
        kernel,
        out_shape=out_shape,
        in_specs=[spec(k) for k in range(len(ins))],
        out_specs=[pl.BlockSpec(memory_space=pltpu.VMEM)] * len(outs),
        compiler_params=pltpu.CompilerParams(vmem_limit_bytes=moved + moved // 4 + 4 * 1024 * 1024),
        cost_estimate=pl.CostEstimate(flops=int(cost * 1e9), bytes_accessed=0, transcendentals=0),
    )(*ins)


def dense_tiles(spot, own_meta, mate_meta, own_values, mate_values, rows_dev, positions):
    window, slots, tile, _ = own_values.shape
    tile_rows = rows_dev // tile

    def kernel(spot_ref, own_meta_ref, mate_meta_ref, own_ref, mate_ref, dense_ref, flipped_ref):
        dense_ref[...] = jnp.zeros_like(dense_ref)
        flipped_ref[...] = jnp.zeros_like(flipped_ref)

        def place(meta_ref, values_ref, first_j, shift, first_row):
            def slot(t, _):
                i, k = t // slots, t % slots
                j = 2 * i + first_j
                base = j * (2 * slots + 1)

                @pl.when(k < meta_ref[base + 2 * slots])
                def _():
                    row = pl.multiple_of((meta_ref[base + 2 * k] + first_row) * tile, tile)
                    col = pl.multiple_of(((i + shift) * tile_rows + meta_ref[base + 2 * k + 1]) * tile, tile)
                    values = values_ref[j, k]
                    dense_ref[pl.ds(row, tile), pl.ds(col, tile)] = values
                    flipped_ref[pl.ds(col, tile), pl.ds(row, tile)] = values.T

                return 0

            lax.fori_loop(0, (window // 2) * slots, slot, 0)

        place(own_meta_ref, own_ref, 0, 0, 0)
        place(mate_meta_ref, mate_ref, 1, 1 - spot_ref[0] % 2, tile_rows)

    wide = positions * rows_dev
    return call(
        kernel,
        [((2 * rows_dev, wide), BF16), ((wide, 2 * rows_dev), BF16)],
        [spot, own_meta, mate_meta, own_values, mate_values],
        smem=3,
    )


def gathered_sums(dense, columns, first, sources, start=None):
    rows_dev, hidden = sources[0].shape
    last = 2 * rows_dev

    def kernel(dense_ref, *refs):
        refs, out_ref = list(refs[:-1]), refs[-1]
        total = refs.pop(0)[first:last] if start is not None else jnp.zeros((last - first, hidden), F32)
        for column, ref in zip(columns, refs):
            part = dense_ref[first:last, column * rows_dev : (column + 1) * rows_dev]
            total = total + jnp.dot(part, ref[...], preferred_element_type=F32)
        out_ref[...] = total

    return call(
        kernel,
        [((last - first, hidden), F32)],
        [dense, *([] if start is None else [start]), *sources],
    )[0]


def layer(spot, own_sum, mate_sum, weight, bias, grad_out, pieces):
    rows_dev, hidden = mate_sum.shape
    piece = hidden // pieces
    half = (pieces // 2, piece + BIAS_ROWS, hidden)

    def kernel(spot_ref, own_ref, mate_ref, weight_ref, bias_ref, grad_out_ref, out_ref, ga_ref, keep_ref, give_ref):
        agg = (own_ref[:rows_dev] + mate_ref[...]).astype(BF16)
        pre = jnp.dot(agg, weight_ref[...], preferred_element_type=F32) + bias_ref[...]
        sig = jax.nn.sigmoid(pre)
        out_ref[...] = (pre * sig).astype(BF16)
        grad_pre = (grad_out_ref[...].astype(F32) * sig * (1.0 + pre * (1.0 - sig))).astype(BF16)
        ga_ref[...] = lax.dot_general(
            grad_pre, weight_ref[...], (((1,), (1,)), ((), ())), preferred_element_type=F32
        ).astype(BF16)
        bias_term = jnp.sum(grad_pre.astype(F32), axis=0, keepdims=True)
        bias_rows = jnp.broadcast_to(bias_term, (BIAS_ROWS, hidden))
        terms = lax.dot_general(agg, grad_pre, (((0,), (0,)), ((), ())), preferred_element_type=F32)
        low, high = terms[: hidden // 2], terms[hidden // 2 :]
        even = spot_ref[0] % 2 == 0
        for ref, value in ((keep_ref, jnp.where(even, low, high)), (give_ref, jnp.where(even, high, low))):
            for q in range(pieces // 2):
                ref[q, :piece] = value[q * piece : (q + 1) * piece].astype(ref.dtype)
                ref[q, piece:] = bias_rows.astype(ref.dtype)

    shape = (rows_dev, hidden)
    return call(
        kernel,
        [(shape, BF16), (shape, BF16), (half, F32), (half, BF16)],
        [spot, own_sum, mate_sum, weight, bias.reshape(1, hidden), grad_out],
        smem=1,
    )


def folded(spot, keep, got):
    count, rows, hidden = keep.shape

    def kernel(spot_ref, keep_ref, got_ref, own_ref, *out_refs):
        for other in range(count):
            q = (spot_ref[0] >> 1) ^ other
            value = keep_ref[q] + got_ref[q].astype(F32)
            if other == 0:
                own_ref[...] = value
            else:
                out_refs[other - 1][...] = value.astype(BF16)

    shape = (rows, hidden)
    return call(kernel, [(shape, F32)] + [(shape, BF16)] * (count - 1), [spot, keep, got], smem=1)


def summed_terms(spot, terms, masks=None, cost=10):
    masks = masks or [None] * len(terms)

    def kernel(spot_ref, *refs):
        total = None
        for ref, mask in zip(refs, masks):
            value = ref[...].astype(F32)
            if mask is not None:
                value = jnp.where((mask >> spot_ref[0]) % 2 == 1, value, 0.0)
            total = value if total is None else total + value
        refs[-1][...] = total.astype(BF16)

    return call(kernel, [(terms[0].shape, BF16)], [spot, *terms], smem=1, cost=cost)[0]


def joined_pieces(spot, pieces):
    rows, hidden = pieces[0].shape
    count = len(pieces)

    def kernel(spot_ref, *refs):
        for other, ref in enumerate(refs[:-1]):
            q = (spot_ref[0] >> 1) ^ other
            refs[-1][pl.ds(pl.multiple_of(q * rows, rows), rows)] = ref[...]

    return call(kernel, [((count * rows, hidden), BF16)], [spot, *pieces], smem=1, cost=10)[0]


def whole_weight(spot, mine, other):
    rows, hidden = mine.shape

    def kernel(spot_ref, mine_ref, other_ref, out_ref):
        core = spot_ref[0] % 2
        out_ref[pl.ds(pl.multiple_of(core * rows, rows), rows)] = mine_ref[...].astype(F32)
        out_ref[pl.ds(pl.multiple_of((1 - core) * rows, rows), rows)] = other_ref[...].astype(F32)

    return call(kernel, [((2 * rows, hidden), F32)], [spot, mine, other], smem=1)[0]


def finished(values, piece):
    hidden = values[0].shape[1]

    def kernel(*refs):
        parts = [ref[...].astype(F32) for ref in refs[:-2]]
        while len(parts) > 1:
            parts = [parts[k] + parts[k + 1] for k in range(0, len(parts), 2)]
        refs[-2][...] = parts[0][:piece].astype(BF16)
        refs[-1][...] = parts[0][piece : piece + 1]

    return call(kernel, [((piece, hidden), BF16), ((1, hidden), F32)], list(values), cost=10)


def scattered_sums(flipped, own, mate, columns, dtypes, spot=None, lookup=None, cost=10):
    rows_dev, hidden = own.shape
    extra = [] if lookup is None else [spot, jnp.asarray(lookup, jnp.int32).reshape(-1)]

    def kernel(*refs):
        refs = list(refs)
        picks = [refs.pop(0) for _ in extra]
        flipped_ref, own_ref, mate_ref, *out_refs = refs
        for column, kinds in zip(columns, dtypes):
            if picks:
                column = picks[1][picks[0][0] * len(lookup[0]) + column]
                part = pl.ds(pl.multiple_of(column * rows_dev, rows_dev), rows_dev)
            else:
                part = pl.ds(column * rows_dev, rows_dev)
            total = jnp.dot(flipped_ref[part, :rows_dev], own_ref[...], preferred_element_type=F32)
            total += jnp.dot(flipped_ref[part, rows_dev:], mate_ref[...], preferred_element_type=F32)
            for kind in kinds:
                out_refs.pop(0)[...] = total.astype(kind)

    return call(
        kernel,
        [((rows_dev, hidden), kind) for kinds in dtypes for kind in kinds],
        [*extra, flipped, own, mate],
        cost=cost,
        smem=len(extra),
    )


def after(value, *others):
    return lax.optimization_barrier((value, *others))


class Direct:
    def __init__(self, count, reach, spot):
        self.count, self.reach, self.positions, self.spot = count, reach, 2 * reach + 1, spot

    def sent(self, value, chips, kept=lambda s: True):
        pairs = [(s, (s + 2 * chips) % self.count) for s in range(self.count) if kept(s)]
        return lax.ppermute(value, "blk", pairs)

    def gather(self, features):
        last = self.positions - 1
        self.sources = [
            features
            if m == self.reach
            else self.sent(features, self.reach - m, lambda s: m < last or s % 2 == 0)
            for m in range(self.positions)
        ]

    def sums(self, dense, rows_dev):
        last = self.positions - 1
        start = gathered_sums(dense, range(last), 0, self.sources[:last])
        return gathered_sums(dense, [last], rows_dev, self.sources[last:], start), start

    def scatter(self, flipped, own, mate):
        self.flipped, self.own, self.mate = flipped, own, mate

    def step(self, k, token):
        if k != 1:
            return []
        _, mate = after(token, self.mate)
        kinds = [[F32 if m == self.reach else BF16] for m in range(self.positions)]
        terms = scattered_sums(self.flipped, self.own, mate, range(self.positions), kinds)
        last = self.positions - 1
        self.arriving = [
            term if m == self.reach else self.sent(term, m - self.reach, lambda s: m < last or s % 2 == 0)
            for m, term in enumerate(terms)
        ]
        return terms[:1]

    def finish(self, token):
        return summed_terms(self.spot, self.arriving)


class Relayed(Direct):
    EVEN, MIDDLE, ENDS = 0b01010101, 0b00111100, 0b11000011
    LOOKUP = [
        [2, 4, 3, 0, 1], [2, 3, 4, 0, 1],
        [2, 4, 1, 0, 3], [2, 1, 4, 0, 3],
        [2, 0, 3, 4, 1], [2, 3, 0, 4, 1],
        [2, 0, 1, 4, 3], [2, 1, 0, 4, 3],
    ]

    def routed(self, value, steps):
        pairs = [(s, (s + steps[s % 8]) % self.count) for s in range(self.count) if s % 8 in steps]
        return lax.ppermute(value, "blk", pairs)

    def step(self, k, token):
        x = {spot: (spot ^ 2) - spot for spot in range(8)}
        y = {spot: (spot ^ 4) - spot for spot in range(8)}
        straight = {spot: (y if spot % 2 else x)[spot] for spot in range(8)}
        across = {spot: (x if spot % 2 else y)[spot] for spot in range(8)}
        take = lambda mate, *args, cost=10: scattered_sums(
            self.flipped, self.own, mate, *args, self.spot, self.LOOKUP, cost
        )
        if k == 0:
            _, mate = after(token, self.mate)
            self.to_last, self.to_plane, self.plane_rest, self.to_straight = take(
                mate, (4, 3, 2), [[BF16], [BF16, F32], [F32]]
            )
            self.from_last = self.routed(self.to_last, straight)
            self.from_side = self.routed(self.to_plane, {3: 4})
            return [self.to_last]
        if k == 1:
            _, plane_rest, to_plane = after(token, self.plane_rest, self.to_plane)
            self.from_plane = self.routed(to_plane, {1: -8})
            out = summed_terms(
                self.spot, [plane_rest, self.from_last, self.from_side], [self.EVEN, self.MIDDLE, 0b10000000]
            )
            self.from_planes = self.routed(out, {0: -8, 2: -8, 4: 8, 6: 8, 5: -8, 3: 8, 7: -8})
            out, mate = after(out, self.mate)
            self.kept, self.to_across = take(mate, (0, 1), [[F32]] * 2, cost=10)
            return [self.kept]
        if k == 2:
            _, rest, to_straight = after(token, self.to_across, self.to_straight)
            second = summed_terms(self.spot, [to_straight, self.from_plane], [None, 0b00000010])
            self.second = self.routed(second, straight)
            out = summed_terms(
                self.spot, [rest, self.from_planes, self.from_last], [None, self.EVEN | 0b00101000, self.ENDS]
            )
            self.first = self.routed(out, across)
            return [second, out]
        return []

    def finish(self, token):
        _, kept = after(token, self.kept)
        terms = [kept, self.second, self.first, self.from_planes]
        return summed_terms(self.spot, terms, [None, None, None, 0b10000000])


def local(features, tile_list, tile_count, tile_values, weight, bias, grad_out):
    count = lax.axis_size("blk")
    me = lax.axis_index("blk")
    window = tile_values.shape[1]
    reach = window // 4
    rows_dev, hidden = features.shape
    pieces = 8
    spot = (me % pieces).astype(jnp.int32).reshape(1)
    route = (Relayed if reach == 2 else Direct)(count, reach, spot)

    def swapped(value, distance):
        return lax.ppermute(value, "blk", [(s, s ^ distance) for s in range(count)])

    route.gather(features)
    mate_values, tile_list, tile_count = after(swapped(tile_values[0], 1), tile_list, tile_count)
    meta = jnp.concatenate([tile_list[0].reshape(window, -1), tile_count[0][:, None]], axis=1).reshape(-1)
    mate_meta = swapped(meta, 1)
    dense, flipped = dense_tiles(spot, meta, mate_meta, tile_values[0], mate_values, rows_dev, route.positions)
    mate_sum, own_sum = route.sums(dense, rows_dev)
    output, grad_agg, keep, give = layer(spot, own_sum, swapped(mate_sum, 1), weight, bias, grad_out, pieces)

    mate_grad, got = swapped(grad_agg, 1), swapped(give, 1)
    route.scatter(flipped, grad_agg, mate_grad)

    def exchanged(k, values, distances):
        others = [swapped(value, distance) for value, distance in zip(values, distances)]
        return after(others, *route.step(k, values[0]))[0]

    in_plane = [2 * d for d in range(1, pieces // 2)]
    own, *give = folded(spot, keep, got)
    total = summed_terms(spot, [own, *exchanged(0, give, in_plane)])
    step, k = pieces, 1
    while step < count:
        group = min(4, count // step)
        across = [step * d for d in range(1, group)]
        values = [total, *exchanged(k, [total] * (group - 1), across)]
        step, k = step * group, k + 1
        if step < count:
            total = summed_terms(spot, values)
    total, bias_sum = finished(values, hidden // pieces)
    half = joined_pieces(spot, [total, *exchanged(k, [total] * len(in_plane), in_plane)])
    grad_weight = whole_weight(spot, half, swapped(half, 1))
    return (output, route.finish(grad_weight), grad_weight, bias_sum.reshape(hidden))


def solution(mesh):
    placed = (
        P("blk", None),
        P("blk", None, None, None),
        P("blk", None),
        P("blk", None, None, None, None),
        P(),
        P(),
        P("blk", None),
    )
    return jax.shard_map(
        local,
        mesh=mesh,
        in_specs=placed,
        out_specs=(P("blk", None), P("blk", None), P(), P()),
        check_vma=False,
    )
```

```python
import jax
import jax.numpy as jnp
from jax import lax
from jax.experimental import pallas as pl
from jax.experimental.pallas import tpu as pltpu
from jax.sharding import PartitionSpec as P

BF16, F32 = jnp.bfloat16, jnp.float32
BIAS_ROWS = 16


def call(kernel, outs, ins, smem=0, cost=0):
    spec = lambda k: pl.BlockSpec(memory_space=pltpu.SMEM if k < smem else pltpu.VMEM)
    out_shape = [jax.ShapeDtypeStruct(s, d) for s, d in outs]
    moved = sum(a.size * a.dtype.itemsize for a in list(ins) + out_shape)
    return pl.pallas_call(
        kernel,
        out_shape=out_shape,
        in_specs=[spec(k) for k in range(len(ins))],
        out_specs=[pl.BlockSpec(memory_space=pltpu.VMEM)] * len(outs),
        compiler_params=pltpu.CompilerParams(vmem_limit_bytes=moved + moved // 4 + 4 * 1024 * 1024),
        cost_estimate=pl.CostEstimate(flops=int(cost * 1e9), bytes_accessed=0, transcendentals=0),
    )(*ins)


def dense_tiles(spot, own_meta, mate_meta, own_values, mate_values, rows_dev, positions):
    window, slots, tile, _ = own_values.shape
    tile_rows = rows_dev // tile

    def kernel(spot_ref, own_meta_ref, mate_meta_ref, own_ref, mate_ref, dense_ref, flipped_ref):
        dense_ref[...] = jnp.zeros_like(dense_ref)
        flipped_ref[...] = jnp.zeros_like(flipped_ref)

        def place(meta_ref, values_ref, first_j, shift, first_row):
            def slot(t, _):
                i, k = t // slots, t % slots
                j = 2 * i + first_j
                base = j * (2 * slots + 1)

                @pl.when(k < meta_ref[base + 2 * slots])
                def _():
                    row = pl.multiple_of((meta_ref[base + 2 * k] + first_row) * tile, tile)
                    col = pl.multiple_of(((i + shift) * tile_rows + meta_ref[base + 2 * k + 1]) * tile, tile)
                    values = values_ref[j, k]
                    dense_ref[pl.ds(row, tile), pl.ds(col, tile)] = values
                    flipped_ref[pl.ds(col, tile), pl.ds(row, tile)] = values.T

                return 0

            lax.fori_loop(0, (window // 2) * slots, slot, 0)

        place(own_meta_ref, own_ref, 0, 0, 0)
        place(mate_meta_ref, mate_ref, 1, 1 - spot_ref[0] % 2, tile_rows)

    wide = positions * rows_dev
    return call(
        kernel,
        [((2 * rows_dev, wide), BF16), ((wide, 2 * rows_dev), BF16)],
        [spot, own_meta, mate_meta, own_values, mate_values],
        smem=3,
    )


def gathered_sums(dense, columns, first, sources, start=None):
    rows_dev, hidden = sources[0].shape
    last = 2 * rows_dev

    def kernel(dense_ref, *refs):
        refs, out_ref = list(refs[:-1]), refs[-1]
        total = refs.pop(0)[first:last] if start is not None else jnp.zeros((last - first, hidden), F32)
        for column, ref in zip(columns, refs):
            part = dense_ref[first:last, column * rows_dev : (column + 1) * rows_dev]
            total = total + jnp.dot(part, ref[...], preferred_element_type=F32)
        out_ref[...] = total

    return call(
        kernel,
        [((last - first, hidden), F32)],
        [dense, *([] if start is None else [start]), *sources],
    )[0]


def layer(spot, own_sum, mate_sum, weight, bias, grad_out, pieces):
    rows_dev, hidden = mate_sum.shape
    piece = hidden // pieces
    half = (pieces // 2, piece + BIAS_ROWS, hidden)

    def kernel(spot_ref, own_ref, mate_ref, weight_ref, bias_ref, grad_out_ref, out_ref, ga_ref, keep_ref, give_ref):
        agg = (own_ref[:rows_dev] + mate_ref[...]).astype(BF16)
        pre = jnp.dot(agg, weight_ref[...], preferred_element_type=F32) + bias_ref[...]
        sig = jax.nn.sigmoid(pre)
        out_ref[...] = (pre * sig).astype(BF16)
        grad_pre = (grad_out_ref[...].astype(F32) * sig * (1.0 + pre * (1.0 - sig))).astype(BF16)
        ga_ref[...] = lax.dot_general(
            grad_pre, weight_ref[...], (((1,), (1,)), ((), ())), preferred_element_type=F32
        ).astype(BF16)
        bias_term = jnp.sum(grad_pre.astype(F32), axis=0, keepdims=True)
        bias_rows = jnp.broadcast_to(bias_term, (BIAS_ROWS, hidden))
        terms = lax.dot_general(agg, grad_pre, (((0,), (0,)), ((), ())), preferred_element_type=F32)
        low, high = terms[: hidden // 2], terms[hidden // 2 :]
        even = spot_ref[0] % 2 == 0
        for ref, value in ((keep_ref, jnp.where(even, low, high)), (give_ref, jnp.where(even, high, low))):
            for q in range(pieces // 2):
                ref[q, :piece] = value[q * piece : (q + 1) * piece].astype(ref.dtype)
                ref[q, piece:] = bias_rows.astype(ref.dtype)

    shape = (rows_dev, hidden)
    return call(
        kernel,
        [(shape, BF16), (shape, BF16), (half, F32), (half, BF16)],
        [spot, own_sum, mate_sum, weight, bias.reshape(1, hidden), grad_out],
        smem=1,
    )


def folded(spot, keep, got):
    count, rows, hidden = keep.shape

    def kernel(spot_ref, keep_ref, got_ref, own_ref, *out_refs):
        for other in range(count):
            q = (spot_ref[0] >> 1) ^ other
            value = keep_ref[q] + got_ref[q].astype(F32)
            if other == 0:
                own_ref[...] = value
            else:
                out_refs[other - 1][...] = value.astype(BF16)

    shape = (rows, hidden)
    return call(kernel, [(shape, F32)] + [(shape, BF16)] * (count - 1), [spot, keep, got], smem=1)


def summed_terms(spot, terms, masks=None, cost=10):
    masks = masks or [None] * len(terms)

    def kernel(spot_ref, *refs):
        total = None
        for ref, mask in zip(refs, masks):
            value = ref[...].astype(F32)
            if mask is not None:
                value = jnp.where((mask >> spot_ref[0]) % 2 == 1, value, 0.0)
            total = value if total is None else total + value
        refs[-1][...] = total.astype(BF16)

    return call(kernel, [(terms[0].shape, BF16)], [spot, *terms], smem=1, cost=cost)[0]


def joined_pieces(spot, pieces):
    rows, hidden = pieces[0].shape
    count = len(pieces)

    def kernel(spot_ref, *refs):
        for other, ref in enumerate(refs[:-1]):
            q = (spot_ref[0] >> 1) ^ other
            refs[-1][pl.ds(pl.multiple_of(q * rows, rows), rows)] = ref[...]

    return call(kernel, [((count * rows, hidden), BF16)], [spot, *pieces], smem=1, cost=10)[0]


def whole_weight(spot, mine, other):
    rows, hidden = mine.shape

    def kernel(spot_ref, mine_ref, other_ref, out_ref):
        core = spot_ref[0] % 2
        out_ref[pl.ds(pl.multiple_of(core * rows, rows), rows)] = mine_ref[...].astype(F32)
        out_ref[pl.ds(pl.multiple_of((1 - core) * rows, rows), rows)] = other_ref[...].astype(F32)

    return call(kernel, [((2 * rows, hidden), F32)], [spot, mine, other], smem=1)[0]


def finished(values, piece):
    hidden = values[0].shape[1]

    def kernel(*refs):
        parts = [ref[...].astype(F32) for ref in refs[:-2]]
        while len(parts) > 1:
            parts = [parts[k] + parts[k + 1] for k in range(0, len(parts), 2)]
        refs[-2][...] = parts[0][:piece].astype(BF16)
        refs[-1][...] = parts[0][piece : piece + 1]

    return call(kernel, [((piece, hidden), BF16), ((1, hidden), F32)], list(values), cost=4)


def scattered_sums(flipped, own, mate, columns, dtypes, spot=None, lookup=None, cost=10):
    rows_dev, hidden = own.shape
    extra = [] if lookup is None else [spot, jnp.asarray(lookup, jnp.int32).reshape(-1)]

    def kernel(*refs):
        refs = list(refs)
        picks = [refs.pop(0) for _ in extra]
        flipped_ref, own_ref, mate_ref, *out_refs = refs
        for column, kinds in zip(columns, dtypes):
            if picks:
                column = picks[1][picks[0][0] * len(lookup[0]) + column]
                part = pl.ds(pl.multiple_of(column * rows_dev, rows_dev), rows_dev)
            else:
                part = pl.ds(column * rows_dev, rows_dev)
            total = jnp.dot(flipped_ref[part, :rows_dev], own_ref[...], preferred_element_type=F32)
            total += jnp.dot(flipped_ref[part, rows_dev:], mate_ref[...], preferred_element_type=F32)
            for kind in kinds:
                out_refs.pop(0)[...] = total.astype(kind)

    return call(
        kernel,
        [((rows_dev, hidden), kind) for kinds in dtypes for kind in kinds],
        [*extra, flipped, own, mate],
        cost=cost,
        smem=len(extra),
    )


def after(value, *others):
    return lax.optimization_barrier((value, *others))


class Direct:
    def __init__(self, count, reach, spot):
        self.count, self.reach, self.positions, self.spot = count, reach, 2 * reach + 1, spot

    def sent(self, value, chips, kept=lambda s: True):
        pairs = [(s, (s + 2 * chips) % self.count) for s in range(self.count) if kept(s)]
        return lax.ppermute(value, "blk", pairs)

    def gather(self, features):
        last = self.positions - 1
        self.sources = [
            features
            if m == self.reach
            else self.sent(features, self.reach - m, lambda s: m < last or s % 2 == 0)
            for m in range(self.positions)
        ]

    def sums(self, dense, rows_dev):
        last = self.positions - 1
        start = gathered_sums(dense, range(last), 0, self.sources[:last])
        return gathered_sums(dense, [last], rows_dev, self.sources[last:], start), start

    def scatter(self, flipped, own, mate):
        self.flipped, self.own, self.mate = flipped, own, mate

    def step(self, k, token):
        if k != 1:
            return []
        _, mate = after(token, self.mate)
        kinds = [[F32 if m == self.reach else BF16] for m in range(self.positions)]
        terms = scattered_sums(self.flipped, self.own, mate, range(self.positions), kinds)
        last = self.positions - 1
        self.arriving = [
            term if m == self.reach else self.sent(term, m - self.reach, lambda s: m < last or s % 2 == 0)
            for m, term in enumerate(terms)
        ]
        return terms[:1]

    def finish(self, token):
        return summed_terms(self.spot, self.arriving)


class Relayed(Direct):
    EVEN, MIDDLE, ENDS = 0b01010101, 0b00111100, 0b11000011
    LOOKUP = [
        [2, 4, 3, 0, 1], [2, 3, 4, 0, 1],
        [2, 4, 1, 0, 3], [2, 1, 4, 0, 3],
        [2, 0, 3, 4, 1], [2, 3, 0, 4, 1],
        [2, 0, 1, 4, 3], [2, 1, 0, 4, 3],
    ]

    def routed(self, value, steps):
        pairs = [(s, (s + steps[s % 8]) % self.count) for s in range(self.count) if s % 8 in steps]
        return lax.ppermute(value, "blk", pairs)

    def step(self, k, token):
        x = {spot: (spot ^ 2) - spot for spot in range(8)}
        y = {spot: (spot ^ 4) - spot for spot in range(8)}
        straight = {spot: (y if spot % 2 else x)[spot] for spot in range(8)}
        across = {spot: (x if spot % 2 else y)[spot] for spot in range(8)}
        take = lambda mate, *args, cost=10: scattered_sums(
            self.flipped, self.own, mate, *args, self.spot, self.LOOKUP, cost
        )
        if k == 0:
            _, mate = after(token, self.mate)
            self.to_last, self.to_plane, self.plane_rest, self.to_straight = take(
                mate, (4, 3, 2), [[BF16], [BF16, F32], [BF16]]
            )
            self.from_last = self.routed(self.to_last, straight)
            self.from_side = self.routed(self.to_plane, {3: 4})
            return [self.to_last]
        if k == 1:
            _, plane_rest = after(token, self.plane_rest)
            out = summed_terms(
                self.spot, [plane_rest, self.from_last, self.from_side], [self.EVEN, self.MIDDLE, 0b10000000]
            )
            self.from_planes = self.routed(out, {0: -8, 2: -8, 4: 8, 6: 8, 5: -8, 3: 8, 7: -8})
            out, mate, to_straight = after(out, self.mate, self.to_straight)
            self.second = self.routed(to_straight, {spot: straight[spot] for spot in (0, 2, 4, 5, 6, 7)})
            self.kept, self.to_across = take(mate, (0, 1), [[F32]] * 2, cost=10)
            return [self.kept]
        if k == 2:
            _, rest, to_plane, _ = after(token, self.to_across, self.to_plane, self.second)
            from_plane = self.routed(to_plane, {1: -8})
            self.passed = self.routed(from_plane, {1: 4})
            out = summed_terms(
                self.spot, [rest, self.from_planes, self.from_last], [None, self.EVEN | 0b00101000, self.ENDS]
            )
            self.first = self.routed(out, across)
            return [out, from_plane]
        return []

    def finish(self, token):
        _, kept = after(token, self.kept)
        terms = [kept, self.second, self.first, self.from_planes, self.passed]
        return summed_terms(self.spot, terms, [None, None, None, 0b10000000, 0b00100000])


def local(features, tile_list, tile_count, tile_values, weight, bias, grad_out):
    count = lax.axis_size("blk")
    me = lax.axis_index("blk")
    window = tile_values.shape[1]
    reach = window // 4
    rows_dev, hidden = features.shape
    pieces = 8
    spot = (me % pieces).astype(jnp.int32).reshape(1)
    route = (Relayed if reach == 2 else Direct)(count, reach, spot)

    def swapped(value, distance):
        return lax.ppermute(value, "blk", [(s, s ^ distance) for s in range(count)])

    route.gather(features)
    mate_values, tile_list, tile_count = after(swapped(tile_values[0], 1), tile_list, tile_count)
    meta = jnp.concatenate([tile_list[0].reshape(window, -1), tile_count[0][:, None]], axis=1).reshape(-1)
    mate_meta = swapped(meta, 1)
    dense, flipped = dense_tiles(spot, meta, mate_meta, tile_values[0], mate_values, rows_dev, route.positions)
    mate_sum, own_sum = route.sums(dense, rows_dev)
    output, grad_agg, keep, give = layer(spot, own_sum, swapped(mate_sum, 1), weight, bias, grad_out, pieces)

    mate_grad, got = swapped(grad_agg, 1), swapped(give, 1)
    route.scatter(flipped, grad_agg, mate_grad)

    def exchanged(k, values, distances):
        others = [swapped(value, distance) for value, distance in zip(values, distances)]
        return after(others, *route.step(k, values[0]))[0]

    in_plane = [2 * d for d in range(1, pieces // 2)]
    own, *give = folded(spot, keep, got)
    total = summed_terms(spot, [own, *exchanged(0, give, in_plane)])
    step, k = pieces, 1
    while step < count:
        group = min(4, count // step)
        across = [step * d for d in range(1, group)]
        values = [total, *exchanged(k, [total] * (group - 1), across)]
        step, k = step * group, k + 1
        if step < count:
            total = summed_terms(spot, values)
    total, bias_sum = finished(values, hidden // pieces)
    half = joined_pieces(spot, [total, *exchanged(k, [total] * len(in_plane), in_plane)])
    grad_weight = whole_weight(spot, half, swapped(half, 1))
    return (output, route.finish(grad_weight), grad_weight, bias_sum.reshape(hidden))


def solution(mesh):
    placed = (
        P("blk", None),
        P("blk", None, None, None),
        P("blk", None),
        P("blk", None, None, None, None),
        P(),
        P(),
        P("blk", None),
    )
    return jax.shard_map(
        local,
        mesh=mesh,
        in_specs=placed,
        out_specs=(P("blk", None), P("blk", None), P(), P()),
        check_vma=False,
    )
```

```python
import jax
import jax.numpy as jnp
from jax import lax
from jax.experimental import pallas as pl
from jax.experimental.pallas import tpu as pltpu
from jax.sharding import PartitionSpec as P

BF16, F32 = jnp.bfloat16, jnp.float32
BIAS_ROWS = 16


def call(kernel, outs, ins, smem=0, cost=0):
    spec = lambda k: pl.BlockSpec(memory_space=pltpu.SMEM if k < smem else pltpu.VMEM)
    out_shape = [jax.ShapeDtypeStruct(s, d) for s, d in outs]
    moved = sum(a.size * a.dtype.itemsize for a in list(ins) + out_shape)
    return pl.pallas_call(
        kernel,
        out_shape=out_shape,
        in_specs=[spec(k) for k in range(len(ins))],
        out_specs=[pl.BlockSpec(memory_space=pltpu.VMEM)] * len(outs),
        compiler_params=pltpu.CompilerParams(vmem_limit_bytes=moved + moved // 4 + 4 * 1024 * 1024),
        cost_estimate=pl.CostEstimate(flops=int(cost * 1e9), bytes_accessed=0, transcendentals=0),
    )(*ins)


def dense_tiles(spot, own_meta, mate_meta, own_values, mate_values, rows_dev, positions):
    window, slots, tile, _ = own_values.shape
    tile_rows = rows_dev // tile

    def kernel(spot_ref, own_meta_ref, mate_meta_ref, own_ref, mate_ref, dense_ref, flipped_ref):
        dense_ref[...] = jnp.zeros_like(dense_ref)
        flipped_ref[...] = jnp.zeros_like(flipped_ref)

        def place(meta_ref, values_ref, first_j, shift, first_row):
            def slot(t, _):
                i, k = t // slots, t % slots
                j = 2 * i + first_j
                base = j * (2 * slots + 1)

                @pl.when(k < meta_ref[base + 2 * slots])
                def _():
                    row = pl.multiple_of((meta_ref[base + 2 * k] + first_row) * tile, tile)
                    col = pl.multiple_of(((i + shift) * tile_rows + meta_ref[base + 2 * k + 1]) * tile, tile)
                    values = values_ref[j, k]
                    dense_ref[pl.ds(row, tile), pl.ds(col, tile)] = values
                    flipped_ref[pl.ds(col, tile), pl.ds(row, tile)] = values.T

                return 0

            lax.fori_loop(0, (window // 2) * slots, slot, 0)

        place(own_meta_ref, own_ref, 0, 0, 0)
        place(mate_meta_ref, mate_ref, 1, 1 - spot_ref[0] % 2, tile_rows)

    wide = positions * rows_dev
    return call(
        kernel,
        [((2 * rows_dev, wide), BF16), ((wide, 2 * rows_dev), BF16)],
        [spot, own_meta, mate_meta, own_values, mate_values],
        smem=3,
    )


def gathered_sums(dense, columns, first, sources, start=None):
    rows_dev, hidden = sources[0].shape
    last = 2 * rows_dev

    def kernel(dense_ref, *refs):
        refs, out_ref = list(refs[:-1]), refs[-1]
        total = refs.pop(0)[first:last] if start is not None else jnp.zeros((last - first, hidden), F32)
        for column, ref in zip(columns, refs):
            part = dense_ref[first:last, column * rows_dev : (column + 1) * rows_dev]
            total = total + jnp.dot(part, ref[...], preferred_element_type=F32)
        out_ref[...] = total

    return call(
        kernel,
        [((last - first, hidden), F32)],
        [dense, *([] if start is None else [start]), *sources],
    )[0]


def layer(spot, own_sum, mate_sum, weight, bias, grad_out, pieces):
    rows_dev, hidden = mate_sum.shape
    piece = hidden // pieces
    half = (pieces // 2, piece + BIAS_ROWS, hidden)

    def kernel(spot_ref, own_ref, mate_ref, weight_ref, bias_ref, grad_out_ref, out_ref, ga_ref, keep_ref, give_ref):
        agg = (own_ref[:rows_dev] + mate_ref[...]).astype(BF16)
        pre = jnp.dot(agg, weight_ref[...], preferred_element_type=F32) + bias_ref[...]
        sig = jax.nn.sigmoid(pre)
        out_ref[...] = (pre * sig).astype(BF16)
        grad_pre = (grad_out_ref[...].astype(F32) * sig * (1.0 + pre * (1.0 - sig))).astype(BF16)
        ga_ref[...] = lax.dot_general(
            grad_pre, weight_ref[...], (((1,), (1,)), ((), ())), preferred_element_type=F32
        ).astype(BF16)
        bias_term = jnp.sum(grad_pre.astype(F32), axis=0, keepdims=True)
        bias_rows = jnp.broadcast_to(bias_term, (BIAS_ROWS, hidden))
        terms = lax.dot_general(agg, grad_pre, (((0,), (0,)), ((), ())), preferred_element_type=F32)
        low, high = terms[: hidden // 2], terms[hidden // 2 :]
        even = spot_ref[0] % 2 == 0
        for ref, value in ((keep_ref, jnp.where(even, low, high)), (give_ref, jnp.where(even, high, low))):
            for q in range(pieces // 2):
                ref[q, :piece] = value[q * piece : (q + 1) * piece].astype(ref.dtype)
                ref[q, piece:] = bias_rows.astype(ref.dtype)

    shape = (rows_dev, hidden)
    return call(
        kernel,
        [(shape, BF16), (shape, BF16), (half, F32), (half, BF16)],
        [spot, own_sum, mate_sum, weight, bias.reshape(1, hidden), grad_out],
        smem=1,
    )


def folded(spot, keep, got):
    count, rows, hidden = keep.shape

    def kernel(spot_ref, keep_ref, got_ref, own_ref, *out_refs):
        for other in range(count):
            q = (spot_ref[0] >> 1) ^ other
            value = keep_ref[q] + got_ref[q].astype(F32)
            if other == 0:
                own_ref[...] = value
            else:
                out_refs[other - 1][...] = value.astype(BF16)

    shape = (rows, hidden)
    return call(kernel, [(shape, F32)] + [(shape, BF16)] * (count - 1), [spot, keep, got], smem=1)


def summed_terms(spot, terms, masks=None, cost=10):
    masks = masks or [None] * len(terms)

    def kernel(spot_ref, *refs):
        total = None
        for ref, mask in zip(refs, masks):
            value = ref[...].astype(F32)
            if mask is not None:
                value = jnp.where((mask >> spot_ref[0]) % 2 == 1, value, 0.0)
            total = value if total is None else total + value
        refs[-1][...] = total.astype(BF16)

    return call(kernel, [(terms[0].shape, BF16)], [spot, *terms], smem=1, cost=cost)[0]


def joined_pieces(spot, pieces):
    rows, hidden = pieces[0].shape
    count = len(pieces)

    def kernel(spot_ref, *refs):
        for other, ref in enumerate(refs[:-1]):
            q = (spot_ref[0] >> 1) ^ other
            refs[-1][pl.ds(pl.multiple_of(q * rows, rows), rows)] = ref[...]

    return call(kernel, [((count * rows, hidden), BF16)], [spot, *pieces], smem=1, cost=10)[0]


def whole_weight(spot, mine, other):
    rows, hidden = mine.shape

    def kernel(spot_ref, mine_ref, other_ref, out_ref):
        core = spot_ref[0] % 2
        out_ref[pl.ds(pl.multiple_of(core * rows, rows), rows)] = mine_ref[...].astype(F32)
        out_ref[pl.ds(pl.multiple_of((1 - core) * rows, rows), rows)] = other_ref[...].astype(F32)

    return call(kernel, [((2 * rows, hidden), F32)], [spot, mine, other], smem=1)[0]


def finished(values, piece):
    hidden = values[0].shape[1]

    def kernel(*refs):
        parts = [ref[...].astype(F32) for ref in refs[:-2]]
        while len(parts) > 1:
            parts = [parts[k] + parts[k + 1] for k in range(0, len(parts), 2)]
        refs[-2][...] = parts[0][:piece].astype(BF16)
        refs[-1][...] = parts[0][piece : piece + 1]

    return call(kernel, [((piece, hidden), BF16), ((1, hidden), F32)], list(values), cost=4)


def scattered_sums(flipped, own, mate, columns, dtypes, spot=None, lookup=None, cost=10):
    rows_dev, hidden = own.shape
    extra = [] if lookup is None else [spot, jnp.asarray(lookup, jnp.int32).reshape(-1)]

    def kernel(*refs):
        refs = list(refs)
        picks = [refs.pop(0) for _ in extra]
        flipped_ref, own_ref, mate_ref, *out_refs = refs
        for column, kinds in zip(columns, dtypes):
            if picks:
                column = picks[1][picks[0][0] * len(lookup[0]) + column]
                part = pl.ds(pl.multiple_of(column * rows_dev, rows_dev), rows_dev)
            else:
                part = pl.ds(column * rows_dev, rows_dev)
            total = jnp.dot(flipped_ref[part, :rows_dev], own_ref[...], preferred_element_type=F32)
            total += jnp.dot(flipped_ref[part, rows_dev:], mate_ref[...], preferred_element_type=F32)
            for kind in kinds:
                out_refs.pop(0)[...] = total.astype(kind)

    return call(
        kernel,
        [((rows_dev, hidden), kind) for kinds in dtypes for kind in kinds],
        [*extra, flipped, own, mate],
        cost=cost,
        smem=len(extra),
    )


def after(value, *others):
    return lax.optimization_barrier((value, *others))


class Direct:
    def __init__(self, count, reach, spot):
        self.count, self.reach, self.positions, self.spot = count, reach, 2 * reach + 1, spot

    def sent(self, value, chips, kept=lambda s: True):
        pairs = [(s, (s + 2 * chips) % self.count) for s in range(self.count) if kept(s)]
        return lax.ppermute(value, "blk", pairs)

    def gather(self, features):
        last = self.positions - 1
        self.sources = [
            features
            if m == self.reach
            else self.sent(features, self.reach - m, lambda s: m < last or s % 2 == 0)
            for m in range(self.positions)
        ]

    def sums(self, dense, rows_dev):
        last = self.positions - 1
        start = gathered_sums(dense, range(last), 0, self.sources[:last])
        return gathered_sums(dense, [last], rows_dev, self.sources[last:], start), start

    def scatter(self, flipped, own, mate):
        self.flipped, self.own, self.mate = flipped, own, mate

    def step(self, k, token):
        if k != 1:
            return []
        _, mate = after(token, self.mate)
        kinds = [[F32 if m == self.reach else BF16] for m in range(self.positions)]
        terms = scattered_sums(self.flipped, self.own, mate, range(self.positions), kinds)
        last = self.positions - 1
        self.arriving = [
            term if m == self.reach else self.sent(term, m - self.reach, lambda s: m < last or s % 2 == 0)
            for m, term in enumerate(terms)
        ]
        return terms[:1]

    def finish(self, token):
        return summed_terms(self.spot, self.arriving)


class Relayed(Direct):
    EVEN, MIDDLE, ENDS = 0b01010101, 0b00111100, 0b11000011
    LOOKUP = [
        [2, 4, 3, 0, 1], [2, 3, 0, 4, 1],
        [2, 4, 1, 0, 3], [2, 1, 0, 4, 3],
        [2, 0, 3, 4, 1], [2, 3, 0, 4, 1],
        [2, 0, 1, 4, 3], [2, 1, 0, 4, 3],
    ]

    def routed(self, value, steps):
        pairs = [(s, (s + steps[s % 8]) % self.count) for s in range(self.count) if s % 8 in steps]
        return lax.ppermute(value, "blk", pairs)

    def step(self, k, token):
        x = {spot: (spot ^ 2) - spot for spot in range(8)}
        y = {spot: (spot ^ 4) - spot for spot in range(8)}
        straight = {spot: (y if spot % 2 else x)[spot] for spot in range(8)}
        across = {spot: (x if spot % 2 else y)[spot] for spot in range(8)}
        take = lambda mate, *args, cost=10: scattered_sums(
            self.flipped, self.own, mate, *args, self.spot, self.LOOKUP, cost
        )
        if k == 0:
            _, mate = after(token, self.mate)
            to_last, self.to_planes, self.to_second = take(mate, (4, 3, 2), [[BF16], [F32], [BF16]])
            self.from_last = self.routed(to_last, straight)
            return [to_last]
        if k == 1:
            _, rest = after(token, self.to_planes)
            out = summed_terms(self.spot, [rest, self.from_last], [self.EVEN, self.MIDDLE])
            self.from_planes = self.routed(out, {0: -8, 2: -8, 4: 8, 6: 8, 5: -8, 3: 8})
            out, mate, to_second = after(out, self.mate, self.to_second)
            self.second = self.routed(to_second, {**straight, 1: -4, 3: -4})
            self.kept, self.to_across = take(mate, (0, 1), [[F32]] * 2, cost=10)
            return [self.kept]
        if k == 2:
            _, rest, _ = after(token, self.to_across, self.second)
            out = summed_terms(
                self.spot, [rest, self.from_planes, self.from_last], [None, self.EVEN | 0b00101000, self.ENDS]
            )
            self.first = self.routed(out, across)
            return [out]
        return []

    def finish(self, token):
        _, kept = after(token, self.kept)
        return summed_terms(self.spot, [kept, self.second, self.first])


def local(features, tile_list, tile_count, tile_values, weight, bias, grad_out):
    count = lax.axis_size("blk")
    me = lax.axis_index("blk")
    window = tile_values.shape[1]
    reach = window // 4
    rows_dev, hidden = features.shape
    pieces = 8
    spot = (me % pieces).astype(jnp.int32).reshape(1)
    route = (Relayed if reach == 2 else Direct)(count, reach, spot)

    def swapped(value, distance):
        return lax.ppermute(value, "blk", [(s, s ^ distance) for s in range(count)])

    route.gather(features)
    mate_values, tile_list, tile_count = after(swapped(tile_values[0], 1), tile_list, tile_count)
    meta = jnp.concatenate([tile_list[0].reshape(window, -1), tile_count[0][:, None]], axis=1).reshape(-1)
    mate_meta = swapped(meta, 1)
    dense, flipped = dense_tiles(spot, meta, mate_meta, tile_values[0], mate_values, rows_dev, route.positions)
    mate_sum, own_sum = route.sums(dense, rows_dev)
    output, grad_agg, keep, give = layer(spot, own_sum, swapped(mate_sum, 1), weight, bias, grad_out, pieces)

    mate_grad, got = swapped(grad_agg, 1), swapped(give, 1)
    route.scatter(flipped, grad_agg, mate_grad)

    def exchanged(k, values, distances):
        others = [swapped(value, distance) for value, distance in zip(values, distances)]
        return after(others, *route.step(k, values[0]))[0]

    in_plane = [2 * d for d in range(1, pieces // 2)]
    own, *give = folded(spot, keep, got)
    total = summed_terms(spot, [own, *exchanged(0, give, in_plane)])
    step, k = pieces, 1
    while step < count:
        group = min(4, count // step)
        across = [step * d for d in range(1, group)]
        values = [total, *exchanged(k, [total] * (group - 1), across)]
        step, k = step * group, k + 1
        if step < count:
            total = summed_terms(spot, values)
    total, bias_sum = finished(values, hidden // pieces)
    half = joined_pieces(spot, [total, *exchanged(k, [total] * len(in_plane), in_plane)])
    grad_weight = whole_weight(spot, half, swapped(half, 1))
    return (output, route.finish(grad_weight), grad_weight, bias_sum.reshape(hidden))


def solution(mesh):
    placed = (
        P("blk", None),
        P("blk", None, None, None),
        P("blk", None),
        P("blk", None, None, None, None),
        P(),
        P(),
        P("blk", None),
    )
    return jax.shard_map(
        local,
        mesh=mesh,
        in_specs=placed,
        out_specs=(P("blk", None), P("blk", None), P(), P()),
        check_vma=False,
    )
```

```python
import jax
import jax.numpy as jnp
from jax import lax
from jax.experimental import pallas as pl
from jax.experimental.pallas import tpu as pltpu
from jax.sharding import PartitionSpec as P

BF16, F32 = jnp.bfloat16, jnp.float32
BIAS_ROWS = 16


def call(kernel, outs, ins, smem=0, cost=0):
    spec = lambda k: pl.BlockSpec(memory_space=pltpu.SMEM if k < smem else pltpu.VMEM)
    out_shape = [jax.ShapeDtypeStruct(s, d) for s, d in outs]
    moved = sum(a.size * a.dtype.itemsize for a in list(ins) + out_shape)
    return pl.pallas_call(
        kernel,
        out_shape=out_shape,
        in_specs=[spec(k) for k in range(len(ins))],
        out_specs=[pl.BlockSpec(memory_space=pltpu.VMEM)] * len(outs),
        compiler_params=pltpu.CompilerParams(vmem_limit_bytes=moved + moved // 4 + 4 * 1024 * 1024),
        cost_estimate=pl.CostEstimate(flops=int(cost * 1e9), bytes_accessed=0, transcendentals=0),
    )(*ins)


def dense_tiles(spot, own_meta, mate_meta, own_values, mate_values, rows_dev, positions):
    window, slots, tile, _ = own_values.shape
    tile_rows = rows_dev // tile

    def kernel(spot_ref, own_meta_ref, mate_meta_ref, own_ref, mate_ref, dense_ref, flipped_ref):
        dense_ref[...] = jnp.zeros_like(dense_ref)
        flipped_ref[...] = jnp.zeros_like(flipped_ref)

        def place(meta_ref, values_ref, first_j, shift, first_row):
            def slot(t, _):
                i, k = t // slots, t % slots
                j = 2 * i + first_j
                base = j * (2 * slots + 1)

                @pl.when(k < meta_ref[base + 2 * slots])
                def _():
                    row = pl.multiple_of((meta_ref[base + 2 * k] + first_row) * tile, tile)
                    col = pl.multiple_of(((i + shift) * tile_rows + meta_ref[base + 2 * k + 1]) * tile, tile)
                    values = values_ref[j, k]
                    dense_ref[pl.ds(row, tile), pl.ds(col, tile)] = values
                    flipped_ref[pl.ds(col, tile), pl.ds(row, tile)] = values.T

                return 0

            lax.fori_loop(0, (window // 2) * slots, slot, 0)

        place(own_meta_ref, own_ref, 0, 0, 0)
        place(mate_meta_ref, mate_ref, 1, 1 - spot_ref[0] % 2, tile_rows)

    wide = positions * rows_dev
    return call(
        kernel,
        [((2 * rows_dev, wide), BF16), ((wide, 2 * rows_dev), BF16)],
        [spot, own_meta, mate_meta, own_values, mate_values],
        smem=3,
    )


def gathered_sums(dense, columns, first, sources, start=None):
    rows_dev, hidden = sources[0].shape
    last = 2 * rows_dev

    def kernel(dense_ref, *refs):
        refs, out_ref = list(refs[:-1]), refs[-1]
        total = refs.pop(0)[first:last] if start is not None else jnp.zeros((last - first, hidden), F32)
        for column, ref in zip(columns, refs):
            part = dense_ref[first:last, column * rows_dev : (column + 1) * rows_dev]
            total = total + jnp.dot(part, ref[...], preferred_element_type=F32)
        out_ref[...] = total

    return call(
        kernel,
        [((last - first, hidden), F32)],
        [dense, *([] if start is None else [start]), *sources],
    )[0]


def layer(spot, own_sum, mate_sum, weight, bias, grad_out, pieces):
    rows_dev, hidden = mate_sum.shape
    piece = hidden // pieces
    half = (pieces // 2, piece + BIAS_ROWS, hidden)

    def kernel(spot_ref, own_ref, mate_ref, weight_ref, bias_ref, grad_out_ref, out_ref, ga_ref, keep_ref, give_ref):
        agg = (own_ref[:rows_dev] + mate_ref[...]).astype(BF16)
        pre = jnp.dot(agg, weight_ref[...], preferred_element_type=F32) + bias_ref[...]
        sig = jax.nn.sigmoid(pre)
        out_ref[...] = (pre * sig).astype(BF16)
        grad_pre = (grad_out_ref[...].astype(F32) * sig * (1.0 + pre * (1.0 - sig))).astype(BF16)
        ga_ref[...] = lax.dot_general(
            grad_pre, weight_ref[...], (((1,), (1,)), ((), ())), preferred_element_type=F32
        ).astype(BF16)
        bias_term = jnp.sum(grad_pre.astype(F32), axis=0, keepdims=True)
        bias_rows = jnp.broadcast_to(bias_term, (BIAS_ROWS, hidden))
        terms = lax.dot_general(agg, grad_pre, (((0,), (0,)), ((), ())), preferred_element_type=F32)
        low, high = terms[: hidden // 2], terms[hidden // 2 :]
        even = spot_ref[0] % 2 == 0
        for ref, value in ((keep_ref, jnp.where(even, low, high)), (give_ref, jnp.where(even, high, low))):
            for q in range(pieces // 2):
                ref[q, :piece] = value[q * piece : (q + 1) * piece].astype(ref.dtype)
                ref[q, piece:] = bias_rows.astype(ref.dtype)

    shape = (rows_dev, hidden)
    return call(
        kernel,
        [(shape, BF16), (shape, BF16), (half, F32), (half, BF16)],
        [spot, own_sum, mate_sum, weight, bias.reshape(1, hidden), grad_out],
        smem=1,
    )


def folded(spot, keep, got):
    count, rows, hidden = keep.shape

    def kernel(spot_ref, keep_ref, got_ref, own_ref, *out_refs):
        for other in range(count):
            q = (spot_ref[0] >> 1) ^ other
            value = keep_ref[q] + got_ref[q].astype(F32)
            if other == 0:
                own_ref[...] = value
            else:
                out_refs[other - 1][...] = value.astype(BF16)

    shape = (rows, hidden)
    return call(kernel, [(shape, F32)] + [(shape, BF16)] * (count - 1), [spot, keep, got], smem=1)


def summed_terms(spot, terms, masks=None, cost=10):
    masks = masks or [None] * len(terms)

    def kernel(spot_ref, *refs):
        total = None
        for ref, mask in zip(refs, masks):
            value = ref[...].astype(F32)
            if mask is not None:
                value = jnp.where((mask >> spot_ref[0]) % 2 == 1, value, 0.0)
            total = value if total is None else total + value
        refs[-1][...] = total.astype(BF16)

    return call(kernel, [(terms[0].shape, BF16)], [spot, *terms], smem=1, cost=cost)[0]


def joined_pieces(spot, pieces):
    rows, hidden = pieces[0].shape
    count = len(pieces)

    def kernel(spot_ref, *refs):
        for other, ref in enumerate(refs[:-1]):
            q = (spot_ref[0] >> 1) ^ other
            refs[-1][pl.ds(pl.multiple_of(q * rows, rows), rows)] = ref[...]

    return call(kernel, [((count * rows, hidden), BF16)], [spot, *pieces], smem=1, cost=10)[0]


def whole_weight(spot, mine, other):
    rows, hidden = mine.shape

    def kernel(spot_ref, mine_ref, other_ref, out_ref):
        core = spot_ref[0] % 2
        out_ref[pl.ds(pl.multiple_of(core * rows, rows), rows)] = mine_ref[...].astype(F32)
        out_ref[pl.ds(pl.multiple_of((1 - core) * rows, rows), rows)] = other_ref[...].astype(F32)

    return call(kernel, [((2 * rows, hidden), F32)], [spot, mine, other], smem=1)[0]


def finished(values, piece):
    hidden = values[0].shape[1]

    def kernel(*refs):
        parts = [ref[...].astype(F32) for ref in refs[:-2]]
        while len(parts) > 1:
            parts = [parts[k] + parts[k + 1] for k in range(0, len(parts), 2)]
        refs[-2][...] = parts[0][:piece].astype(BF16)
        refs[-1][...] = parts[0][piece : piece + 1]

    return call(kernel, [((piece, hidden), BF16), ((1, hidden), F32)], list(values), cost=4)


def scattered_sums(flipped, own, mate, columns, dtypes, spot=None, lookup=None, cost=10):
    rows_dev, hidden = own.shape
    extra = [] if lookup is None else [spot, jnp.asarray(lookup, jnp.int32).reshape(-1)]

    def kernel(*refs):
        refs = list(refs)
        picks = [refs.pop(0) for _ in extra]
        flipped_ref, own_ref, mate_ref, *out_refs = refs
        for column, kinds in zip(columns, dtypes):
            if picks:
                column = picks[1][picks[0][0] * len(lookup[0]) + column]
                part = pl.ds(pl.multiple_of(column * rows_dev, rows_dev), rows_dev)
            else:
                part = pl.ds(column * rows_dev, rows_dev)
            total = jnp.dot(flipped_ref[part, :rows_dev], own_ref[...], preferred_element_type=F32)
            total += jnp.dot(flipped_ref[part, rows_dev:], mate_ref[...], preferred_element_type=F32)
            for kind in kinds:
                out_refs.pop(0)[...] = total.astype(kind)

    return call(
        kernel,
        [((rows_dev, hidden), kind) for kinds in dtypes for kind in kinds],
        [*extra, flipped, own, mate],
        cost=cost,
        smem=len(extra),
    )


def after(value, *others):
    return lax.optimization_barrier((value, *others))


class Direct:
    def __init__(self, count, reach, spot):
        self.count, self.reach, self.positions, self.spot = count, reach, 2 * reach + 1, spot

    def sent(self, value, chips, kept=lambda s: True):
        pairs = [(s, (s + 2 * chips) % self.count) for s in range(self.count) if kept(s)]
        return lax.ppermute(value, "blk", pairs)

    def gather(self, features):
        last = self.positions - 1
        self.sources = [
            features
            if m == self.reach
            else self.sent(features, self.reach - m, lambda s: m < last or s % 2 == 0)
            for m in range(self.positions)
        ]

    def sums(self, dense, rows_dev):
        last = self.positions - 1
        start = gathered_sums(dense, range(last), 0, self.sources[:last])
        return gathered_sums(dense, [last], rows_dev, self.sources[last:], start), start

    def scatter(self, flipped, own, mate):
        self.flipped, self.own, self.mate = flipped, own, mate

    def step(self, k, token):
        if k != 1:
            return []
        _, mate = after(token, self.mate)
        kinds = [[F32 if m == self.reach else BF16] for m in range(self.positions)]
        terms = scattered_sums(self.flipped, self.own, mate, range(self.positions), kinds)
        last = self.positions - 1
        self.arriving = [
            term if m == self.reach else self.sent(term, m - self.reach, lambda s: m < last or s % 2 == 0)
            for m, term in enumerate(terms)
        ]
        return terms[:1]

    def finish(self, half, grad_weight):
        return summed_terms(self.spot, self.arriving)


class Relayed(Direct):
    EVEN, MIDDLE, ENDS = 0b01010101, 0b00111100, 0b11000011
    LOOKUP = [
        [2, 4, 3, 0, 1], [2, 3, 0, 4, 1],
        [2, 4, 1, 0, 3], [2, 1, 0, 4, 3],
        [2, 0, 3, 4, 1], [2, 3, 0, 4, 1],
        [2, 0, 1, 4, 3], [2, 1, 0, 4, 3],
    ]

    def routed(self, value, steps):
        pairs = [(s, (s + steps[s % 8]) % self.count) for s in range(self.count) if s % 8 in steps]
        return lax.ppermute(value, "blk", pairs)

    def step(self, k, token):
        x = {spot: (spot ^ 2) - spot for spot in range(8)}
        y = {spot: (spot ^ 4) - spot for spot in range(8)}
        straight = {spot: (y if spot % 2 else x)[spot] for spot in range(8)}
        across = {spot: (x if spot % 2 else y)[spot] for spot in range(8)}
        take = lambda mate, *args, cost=10: scattered_sums(
            self.flipped, self.own, mate, *args, self.spot, self.LOOKUP, cost
        )
        if k == 0:
            _, mate = after(token, self.mate)
            to_last, self.to_planes, self.to_second = take(mate, (4, 3, 2), [[BF16], [F32], [BF16]])
            self.from_last = self.routed(to_last, straight)
            return [to_last]
        if k == 1:
            _, rest = after(token, self.to_planes)
            out = summed_terms(self.spot, [rest, self.from_last], [self.EVEN, self.MIDDLE])
            self.from_planes = self.routed(out, {0: -8, 2: -8, 4: 8, 6: 8, 5: -8, 3: 8})
            out, mate, to_second = after(out, self.mate, self.to_second)
            self.second = self.routed(to_second, {**straight, 1: -4, 3: -4})
            self.to_across = take(mate, (1,), [[F32]], cost=10)[0]
            return [self.to_across]
        if k == 2:
            _, rest, _ = after(token, self.to_across, self.second)
            out = summed_terms(
                self.spot, [rest, self.from_planes, self.from_last], [None, self.EVEN | 0b00101000, self.ENDS]
            )
            self.first = self.routed(out, across)
            return [out]
        return []

    def finish(self, half, grad_weight):
        _, mate = after(half, self.mate)
        kept = scattered_sums(self.flipped, self.own, mate, (0,), [[F32]], self.spot, self.LOOKUP)[0]
        _, kept = after(grad_weight, kept)
        return summed_terms(self.spot, [kept, self.second, self.first])


def local(features, tile_list, tile_count, tile_values, weight, bias, grad_out):
    count = lax.axis_size("blk")
    me = lax.axis_index("blk")
    window = tile_values.shape[1]
    reach = window // 4
    rows_dev, hidden = features.shape
    pieces = 8
    spot = (me % pieces).astype(jnp.int32).reshape(1)
    route = (Relayed if reach == 2 else Direct)(count, reach, spot)

    def swapped(value, distance):
        return lax.ppermute(value, "blk", [(s, s ^ distance) for s in range(count)])

    route.gather(features)
    mate_values, tile_list, tile_count = after(swapped(tile_values[0], 1), tile_list, tile_count)
    meta = jnp.concatenate([tile_list[0].reshape(window, -1), tile_count[0][:, None]], axis=1).reshape(-1)
    mate_meta = swapped(meta, 1)
    dense, flipped = dense_tiles(spot, meta, mate_meta, tile_values[0], mate_values, rows_dev, route.positions)
    mate_sum, own_sum = route.sums(dense, rows_dev)
    output, grad_agg, keep, give = layer(spot, own_sum, swapped(mate_sum, 1), weight, bias, grad_out, pieces)

    mate_grad, got = swapped(grad_agg, 1), swapped(give, 1)
    route.scatter(flipped, grad_agg, mate_grad)

    def exchanged(k, values, distances):
        others = [swapped(value, distance) for value, distance in zip(values, distances)]
        return after(others, *route.step(k, values[0]))[0]

    in_plane = [2 * d for d in range(1, pieces // 2)]
    own, *give = folded(spot, keep, got)
    total = summed_terms(spot, [own, *exchanged(0, give, in_plane)])
    step, k = pieces, 1
    while step < count:
        group = min(4, count // step)
        across = [step * d for d in range(1, group)]
        values = [total, *exchanged(k, [total] * (group - 1), across)]
        step, k = step * group, k + 1
        if step < count:
            total = summed_terms(spot, values)
    total, bias_sum = finished(values, hidden // pieces)
    half = joined_pieces(spot, [total, *exchanged(k, [total] * len(in_plane), in_plane)])
    grad_weight = whole_weight(spot, half, swapped(half, 1))
    return (output, route.finish(half, grad_weight), grad_weight, bias_sum.reshape(hidden))


def solution(mesh):
    placed = (
        P("blk", None),
        P("blk", None, None, None),
        P("blk", None),
        P("blk", None, None, None, None),
        P(),
        P(),
        P("blk", None),
    )
    return jax.shard_map(
        local,
        mesh=mesh,
        in_specs=placed,
        out_specs=(P("blk", None), P("blk", None), P(), P()),
        check_vma=False,
    )
```
